32 devices in a mesh: win: 2 (over y), gz: 4 (over z), gy: 2 (over x), gx: 2 (over core).
Axes of the slice: x: 2, y: 2, z: 4, core: 2. Of those that a mesh axis runs over, the one named last changes fastest.
Arguments:
- noisy: float32 [32, 16, 256], P(('win', 'gz'), 'gy', 'gx'), parts along dimension 0, may hold values from -6 to 6
- first_weight: float32 [32, 1, 27], replicated, may hold values from -1.25 to 1.25
- first_bias: float32 [16], replicated, may hold values from -8 to -3
- second_weight: float32 [32, 16, 27], replicated, may hold values from -0.3125 to 0.3125
- second_bias: float32 [16], replicated, may hold values from -8 to -3
- head_weight: float32 [16], replicated, may hold values from -18 to 18
- seg_weight_in: float32 [16, 1, 27], replicated, may hold values from -1.25 to 1.25
- seg_bias_in: float32 [16], replicated, may hold values from -3 to 3
- seg_weight_out: float32 [16, 16, 27], replicated, may hold values from -0.3125 to 0.3125
- seg_bias_out: float32 [16], replicated, may hold values from -3 to 3
Outputs:
- denoised: float32 [32, 16, 256], P(('win', 'gz'), 'gy', 'gx'), parts along dimension 0
- segmented: float32 [16, 32, 16, 256], P(None, ('win', 'gz'), 'gy', 'gx'), parts along dimension 1
The draws below stay inside these ranges and needn't reach their ends.
There are 2 independent parts, one for each index of `win`. The reference program is written for one: setup_inputs(seed, part) draws one part's arguments, and reference() takes and returns one part's arrays. A program takes and returns all parts, laid end to end along the dimension named above; an argument that names none is the same for every part. Nothing has to cross between parts.
All inputs are finite; a program needn't handle non-finite values.
Results may differ from the reference program's by a relative error of at most 0.00029.
Values sent between devices are 32-bit elements; how exact they have to be, the bound alone decides.
No kernel may reach another device: no remote copies, remote signals or barrier semaphores. Data moves between devices by JAX's collectives and lax.ppermute only.
A program may use at most 64 MiB of HBM per device.

```python
import jax
import jax.numpy as jnp
from jax import lax

C = 16
TAPS = 27
NZ = 16
NY = 16
NX = 256


def level_of(key, shape, pieces, low, high):
    level = 1.0
    for dim, shards_of in pieces:
        steps = jax.random.uniform(jax.random.fold_in(jax.random.fold_in(key, 6), dim), (shards_of,), jnp.float32, low / len(pieces), high / len(pieces))
        level = level * jnp.repeat(jnp.exp(steps), shape[dim] // shards_of).reshape((-1,) + (1,) * (len(shape) - 1 - dim))
    return level


def noise(stream_key, extent, width, limit, cuts=(), kind=jnp.bfloat16):
    drawn = jax.random.normal(stream_key, extent, jnp.float32) * width
    if len(cuts) > 0:
        drawn = level_of(stream_key, extent, cuts, -0.22, 0.18) * drawn
    return jnp.clip(drawn, min=-limit, max=limit).astype(kind)


def setup_inputs(seed: int = 0, part: int = 0) -> dict:
    key_of = jax.random.split(jax.random.key(seed), 11)
    part_splits = jax.random.split(jax.random.fold_in(key_of[10], part), 11)
    noisy = noise(part_splits[0], (NZ, NY, NX), 1.0, 6.0, ((0, 4), (1, 2), (2, 2)), jnp.float32)
    first_weight = noise(key_of[1], (2 * C, 1, TAPS), TAPS ** -0.5, 1.25, (), jnp.float32)
    first_bias = jnp.clip(jax.random.uniform(key_of[2], (C,), jnp.float32, -8.0, -3.0), -8.0, -3.0)
    second_weight = noise(key_of[3], (2 * C, C, TAPS), (C * TAPS) ** -0.5, 0.3125, (), jnp.float32)
    second_bias = jnp.clip(jax.random.uniform(key_of[4], (C,), jnp.float32, -8.0, -3.0), -8.0, -3.0)
    head_weight = noise(key_of[5], (C,), 3.0, 18.0, (), jnp.float32)
    seg_weight_in = noise(key_of[6], (C, 1, TAPS), TAPS ** -0.5, 1.25, (), jnp.float32)
    seg_bias_in = noise(key_of[7], (C,), 0.5, 3.0, (), jnp.float32)
    seg_weight_out = noise(key_of[8], (C, C, TAPS), (C * TAPS) ** -0.5, 0.3125, (), jnp.float32)
    seg_bias_out = noise(key_of[9], (C,), 0.5, 3.0, (), jnp.float32)
    return dict(noisy=noisy, first_weight=first_weight, first_bias=first_bias, second_weight=second_weight, second_bias=second_bias, head_weight=head_weight, seg_weight_in=seg_weight_in, seg_bias_in=seg_bias_in, seg_weight_out=seg_weight_out, seg_bias_out=seg_bias_out)


def convolve(field, weight):
    kernel = weight.reshape(weight.shape[0], weight.shape[1], 3, 3, 3)
    result = lax.conv_general_dilated(field[None], kernel, (1, 1, 1), ((1, 1), (1, 1), (1, 1)), dimension_numbers=("NCDHW", "OIDHW", "NCDHW"), precision=lax.Precision.HIGHEST)
    return result[0]


def recurrent(field, weight, bias, backward):
    channels = bias.shape[0]
    pre = convolve(field, weight)
    cand = jnp.tanh(pre[:channels])
    keep = jax.nn.sigmoid(-(pre[channels:] + bias[:, None, None, None]))
    inject = (1.0 - keep) * cand

    def advance(state, inputs):
        state = inputs[0] * state + inputs[1]
        return state, state

    start = jnp.zeros((channels, field.shape[2], field.shape[3]), jnp.float32)
    _, states = lax.scan(advance, start, (jnp.moveaxis(keep, 1, 0), jnp.moveaxis(inject, 1, 0)), reverse=backward)
    return jnp.moveaxis(states, 0, 1)


def reference(noisy, first_weight, first_bias, second_weight, second_bias, head_weight, seg_weight_in, seg_bias_in, seg_weight_out, seg_bias_out):
    first_hidden = recurrent(noisy[None], first_weight, first_bias, False)
    second_hidden = recurrent(first_hidden, second_weight, second_bias, True)
    denoised = noisy + jnp.einsum("c,czyx->zyx", head_weight, second_hidden, precision=lax.Precision.HIGHEST)
    features = jnp.maximum(convolve(denoised[None], seg_weight_in) + seg_bias_in[:, None, None, None], 0.0)
    segmented = convolve(features, seg_weight_out) + seg_bias_out[:, None, None, None]
    return denoised, segmented
```

```python
import functools

import jax
import jax.numpy as jnp
import numpy as np
from jax import lax
from jax.experimental import pallas as pl
from jax.experimental.pallas import tpu as pltpu
from jax.sharding import PartitionSpec as P


def shifted(value, axis, steps):
    count = lax.axis_size(axis)
    first, last = (max(0, -steps), min(count, count - steps))
    return lax.ppermute(value, axis, [(source, source + steps) for source in range(first, last)])


def with_halo(block, sides, width):
    for axis, dim in sides:
        count = lax.axis_size(axis)
        forward = [(i, i + 1) for i in range(count - 1)]
        backward = [(target, source) for source, target in forward]
        low = lax.ppermute(
            lax.slice_in_dim(block, block.shape[dim] - width, None, axis=dim), axis, forward
        )
        high = lax.ppermute(lax.slice_in_dim(block, 0, width, axis=dim), axis, backward)
        block = jnp.concatenate([low, block, high], axis=dim)
    return block


def convolve(padded, weight):
    depth = padded.shape[1] - 2
    height = padded.shape[2] - 2
    width = padded.shape[3] - 2
    total = jnp.zeros((weight.shape[0], depth, height, width), jnp.float32)
    for tap in range(27):
        step_z = tap // 9
        step_y = tap // 3 % 3
        step_x = tap % 3
        piece = padded[
            :, step_z : step_z + depth, step_y : step_y + height, step_x : step_x + width
        ]
        total = total + jnp.einsum(
            "oc,czyx->ozyx", weight[:, :, tap], piece, precision=lax.Precision.HIGHEST
        )
    return total


def affine(earlier, later):
    return (earlier[0] * later[0], later[0] * earlier[1] + later[1])


def recurrent(padded, weight, bias, backward):
    channels = bias.shape[0]
    pre = convolve(padded, weight)
    cand = jnp.tanh(pre[:channels])
    keep = jax.nn.sigmoid(-(pre[channels:] + bias[:, None, None, None]))
    inject = (1.0 - keep) * cand
    if backward:
        keep = jnp.flip(keep, 1)
        inject = jnp.flip(inject, 1)
    cum_keep, cum_inject = lax.associative_scan(affine, (keep, inject), axis=1)
    total_keep = cum_keep[:, -1]
    total_inject = cum_inject[:, -1]
    offset = -1 if backward else 1

    def relay(turn, carry):
        return shifted(total_keep * carry + total_inject, "gz", offset)

    carry = lax.fori_loop(0, lax.axis_size("gz") - 1, relay, jnp.zeros_like(total_inject))
    hidden = cum_keep * carry[:, None] + cum_inject
    if backward:
        hidden = jnp.flip(hidden, 1)
    return hidden


def inside_mask(length, where, count):
    places = jnp.arange(length + 2)
    outside = (places == 0) & (where == 0) | (places == length + 1) & (where == count - 1)
    return jnp.where(outside, 0.0, 1.0).astype(jnp.float32)


def body(
    noisy,
    first_weight,
    first_bias,
    second_weight,
    second_bias,
    head_weight,
    seg_weight_in,
    seg_bias_in,
    seg_weight_out,
    seg_bias_out,
):
    noisy_pad = with_halo(noisy[None], (("gz", 1), ("gy", 2), ("gx", 3)), 1)
    first_hidden = recurrent(noisy_pad, first_weight, first_bias, False)
    hidden_pad = with_halo(first_hidden, (("gz", 1), ("gy", 2), ("gx", 3)), 1)
    second_hidden = recurrent(hidden_pad, second_weight, second_bias, True)
    denoised = noisy + jnp.einsum(
        "c,czyx->zyx", head_weight, second_hidden, precision=lax.Precision.HIGHEST
    )
    deep_pad = with_halo(denoised[None], (("gz", 1), ("gy", 2), ("gx", 3)), 2)
    grown = jnp.maximum(convolve(deep_pad, seg_weight_in) + seg_bias_in[:, None, None, None], 0.0)
    mask_z = inside_mask(denoised.shape[0], lax.axis_index("gz"), lax.axis_size("gz"))
    mask_y = inside_mask(denoised.shape[1], lax.axis_index("gy"), lax.axis_size("gy"))
    mask_x = inside_mask(denoised.shape[2], lax.axis_index("gx"), lax.axis_size("gx"))
    feature_pad = (
        grown * (mask_z[:, None, None] * mask_y[None, :, None] * mask_x[None, None, :])[None]
    )
    segmented = convolve(feature_pad, seg_weight_out) + seg_bias_out[:, None, None, None]
    return (denoised, segmented)


HALO = 4
LANES = 128


def split(value):
    high = value.astype(jnp.bfloat16)
    return high, (value - high.astype(jnp.float32)).astype(jnp.bfloat16)


def halves(value):
    high = lax.reduce_precision(value, 8, 7)
    return high.astype(jnp.bfloat16), (value - high).astype(jnp.bfloat16)


def swapped(value, axis):
    return lax.ppermute(value, axis, [(0, 1), (1, 0)])


def gathered(noisy):
    count = lax.axis_size("gz")
    place = lax.axis_index("gz")
    slabs = [
        lax.ppermute(noisy, "gz", [(i, (i + s) % count) for i in range(count)])
        for s in range(count - 1, 0, -1)
    ] + [noisy]
    turns = jnp.concatenate(slabs + slabs[:-1], axis=0)
    depth = noisy.shape[0]
    block = lax.dynamic_slice_in_dim(turns, (count - 1 - place) * depth, count * depth, 0)
    for axis, dim in (("gy", 1), ("gx", 2)):
        first = lax.axis_index(axis) == 0
        size = block.shape[dim]
        low = lax.slice_in_dim(block, 0, HALO, axis=dim)
        high = lax.slice_in_dim(block, size - HALO, size, axis=dim)
        other = swapped(jnp.where(first, high, low), axis)
        block = jnp.where(
            first,
            jnp.concatenate([block, other], dim),
            jnp.concatenate([other, block], dim),
        )
    return block


def kernel(
    geometry,
    place_ref,
    noisy_ref,
    mask_ref,
    w1_ref,
    bias1_ref,
    w2_ref,
    bias2_ref,
    head_ref,
    w3_ref,
    bias3_ref,
    w4_ref,
    bias4_ref,
    den_ref,
    seg_ref,
    stage,
    thin,
    pre,
    rows,
    wide_hi,
    wide_lo,
):
    deep, depth, channels, pitch, span, margin = geometry
    mask = mask_ref[...]
    shifts = [(b - 1) * pitch + (c - 1) for b in range(3) for c in range(3)]
    f32 = jnp.float32

    def shifted(slot, shift):
        return stage[slot, :, pl.ds(margin + shift, span)]

    def thin_columns(field):
        high, low = split(field)
        stage[0, :, pl.ds(margin, span)] = high
        stage[1, :, pl.ds(margin, span)] = low
        for t, s in enumerate(shifts):
            h = shifted(0, s)
            thin[pl.ds(t * deep, deep), :] = h
            thin[pl.ds((9 + t) * deep, deep), :] = h
            thin[pl.ds((18 + t) * deep, deep), :] = shifted(1, s)

    def wide_columns(z, field):
        high, low = split(field)
        stage[0, :, pl.ds(margin, span)] = high
        stage[1, :, pl.ds(margin, span)] = low
        for t, s in enumerate(shifts):
            at = pl.ds(pl.multiple_of((z * 9 + t) * channels, channels), channels)
            wide_hi[at, :] = shifted(0, s)
            wide_lo[at, :] = shifted(1, s)

    def banded(w_ref, start, taps):
        at = pl.ds(pl.multiple_of(start, channels), taps)
        rows_of = w_ref.shape[0] // 2
        wh = w_ref[:rows_of]
        wl = w_ref[rows_of:]
        h = wide_hi[at, :]
        out = jnp.dot(wh, h, preferred_element_type=f32)
        out = out + jnp.dot(wh, wide_lo[at, :], preferred_element_type=f32)
        return out + jnp.dot(wl, h, preferred_element_type=f32)

    def gate(at, bias, hidden):
        cand = jnp.tanh(pre[pl.ds(pl.multiple_of(at, channels), channels), :])
        up = pre[pl.ds(pl.multiple_of(at + channels, channels), channels), :] + bias
        fresh = 1.0 / (1.0 + jnp.exp(-up))
        return hidden + fresh * (cand - hidden)

    stage[...] = jnp.zeros_like(stage)
    noisy = noisy_ref[...]
    thin_columns(noisy)
    pre[...] = jnp.dot(w1_ref[...], thin[...], preferred_element_type=f32)
    edge = 9 * channels
    zeros = jnp.zeros((edge, span), jnp.bfloat16)
    for wide in (wide_hi, wide_lo):
        wide[pl.ds(0, edge), :] = zeros
        wide[pl.ds((deep + 1) * edge, edge), :] = zeros

    def first(z, hidden):
        hidden = gate(z * 2 * channels, bias1_ref[...], hidden)
        wide_columns(z + 1, hidden * mask)
        return hidden

    blank = jnp.zeros((channels, span), f32)
    lax.fori_loop(0, deep, first, blank)

    taps = (depth + 2) * edge
    block_rows = depth * 2 * channels

    def second(turn, hidden):
        b = deep // depth - 1 - turn
        pre[pl.ds(0, block_rows), :] = banded(w2_ref, b * depth * edge, taps)
        for zo in range(depth - 1, -1, -1):
            hidden = gate(zo * 2 * channels, bias2_ref[...], hidden)
            rows[pl.ds(b * depth + zo, 1), :] = jnp.sum(
                hidden * head_ref[...], axis=0, keepdims=True
            )
        return hidden

    lax.fori_loop(0, deep // depth, second, blank)

    rows[...] = (noisy + rows[...]) * mask
    mine = rows[pl.ds(0, depth), :]
    for b in range(1, deep // depth):
        mine = jnp.where(place_ref[0] == b, rows[pl.ds(b * depth, depth), :], mine)
    den_ref[...] = mine
    thin_columns(rows[...])
    grown = jnp.dot(w3_ref[...], thin[...], preferred_element_type=f32)
    grown = jnp.maximum(grown + bias3_ref[...], 0.0) * mask
    for z in range(depth + 2):
        wide_columns(z, grown[z * channels : (z + 1) * channels])
    seg_ref[...] = banded(w4_ref, 0, taps) + bias4_ref[...]


def thin_select(deep):
    out = np.zeros((deep + 2, 27, 9, deep), np.float32)
    for z in range(deep):
        for a in range(3):
            if 0 <= z + a - 1 < deep:
                for t in range(9):
                    out[z + 1, a * 9 + t, t, z + a - 1] = 1.0
    return out.reshape(deep + 2, 27, 9 * deep)


def band(weight, depth):
    out, inn = weight.shape[0], weight.shape[1]
    flat = jnp.transpose(weight, (0, 2, 1)).reshape(out, 27 * inn)
    step = 9 * inn
    return jnp.stack(
        [jnp.pad(flat, ((0, 0), (step * z, step * (depth - 1 - z)))) for z in range(depth)]
    )


def twice(matrix):
    return jnp.concatenate(halves(matrix), 0)


def local_body(
    noisy,
    first_weight,
    first_bias,
    second_weight,
    second_bias,
    head_weight,
    seg_weight_in,
    seg_bias_in,
    seg_weight_out,
    seg_bias_out,
):
    depth, height, width = noisy.shape
    count = lax.axis_size("gz")
    place = lax.axis_index("gz")
    deep = count * depth
    channels = first_bias.shape[0]
    high, pitch = height + HALO, width + HALO + 1
    span = -(-high * pitch // LANES) * LANES
    margin = -(-(pitch + 1) // LANES) * LANES

    window = gathered(noisy)
    flat = jnp.pad(window, ((0, 0), (0, 0), (0, 1))).reshape(deep, high * pitch)
    flat = jnp.pad(flat, ((0, 0), (0, span - high * pitch)))
    inside = np.zeros((high, pitch), np.float32)
    inside[:, : pitch - 1] = 1.0
    mask = jnp.asarray(np.pad(inside.reshape(1, -1), ((0, 0), (0, span - high * pitch))))

    select = jnp.asarray(thin_select(deep))
    exact = lax.Precision.HIGHEST

    def thin_matrix(weight, picked):
        full = jnp.einsum("ok,zkj->zoj", weight[:, 0], picked, precision=exact)
        h, l = halves(full.reshape(-1, full.shape[-1]))
        return jnp.concatenate([h, l, h], 1)

    w1 = thin_matrix(first_weight, select[1:-1])
    w3 = thin_matrix(
        seg_weight_in, lax.dynamic_slice_in_dim(select, place * depth, depth + 2, 0)
    )
    w2 = twice(band(second_weight, depth).reshape(depth * 2 * channels, -1))
    w4 = twice(
        jnp.transpose(band(seg_weight_out, depth), (1, 0, 2)).reshape(depth * channels, -1)
    )
    layers = place * depth - 1 + jnp.arange(depth + 2)
    real = ((layers >= 0) & (layers < deep)).astype(jnp.float32)
    bias3 = (real[:, None] * seg_bias_in[None, :]).reshape(-1, 1)
    bias4 = jnp.repeat(seg_bias_out, depth).reshape(-1, 1)

    vmem = pl.BlockSpec(memory_space=pltpu.VMEM)
    bf16 = jnp.bfloat16
    den, seg = pl.pallas_call(
        functools.partial(kernel, (deep, depth, channels, pitch, span, margin)),
        out_shape=(
            jax.ShapeDtypeStruct((depth, span), jnp.float32),
            jax.ShapeDtypeStruct((depth * channels, span), jnp.float32),
        ),
        in_specs=[pl.BlockSpec(memory_space=pltpu.SMEM)] + [vmem] * 11,
        out_specs=(vmem, vmem),
        scratch_shapes=[
            pltpu.VMEM((2, channels, span + 2 * margin), bf16),
            pltpu.VMEM((27 * deep, span), bf16),
            pltpu.VMEM((deep * 2 * channels, span), jnp.float32),
            pltpu.VMEM((deep, span), jnp.float32),
            pltpu.VMEM(((deep + 2) * 9 * channels, span), bf16),
            pltpu.VMEM(((deep + 2) * 9 * channels, span), bf16),
        ],
        compiler_params=pltpu.CompilerParams(vmem_limit_bytes=56 * 1024 * 1024),
    )(
        place.reshape(1),
        flat,
        mask,
        w1,
        first_bias.reshape(-1, 1),
        w2,
        second_bias.reshape(-1, 1),
        head_weight.reshape(-1, 1),
        w3,
        bias3,
        w4,
        bias4,
    )
    top = lax.axis_index("gy") * HALO
    left = lax.axis_index("gx") * HALO

    def own(field):
        field = field[:, : high * pitch].reshape(-1, high, pitch)
        return lax.dynamic_slice(field, (0, top, left), (field.shape[0], height, width))

    return own(den), own(seg).reshape(channels, depth, height, width)


def solution(mesh):
    in_specs = (P(("win", "gz"), "gy", "gx"), P(), P(), P(), P(), P(), P(), P(), P(), P())
    out_specs = (P(("win", "gz"), "gy", "gx"), P(None, ("win", "gz"), "gy", "gx"))
    shallow = mesh.shape["gz"] <= 4 and mesh.shape["gy"] == 2 and mesh.shape["gx"] == 2
    chosen = local_body if shallow else body
    return jax.shard_map(chosen, mesh=mesh, in_specs=in_specs, out_specs=out_specs, check_vma=False)
```

```python
import functools

import jax
import jax.numpy as jnp
import numpy as np
from jax import lax
from jax.experimental import pallas as pl
from jax.experimental.pallas import tpu as pltpu
from jax.sharding import PartitionSpec as P


def shifted(value, axis, steps):
    count = lax.axis_size(axis)
    first, last = (max(0, -steps), min(count, count - steps))
    return lax.ppermute(value, axis, [(source, source + steps) for source in range(first, last)])


def with_halo(block, sides, width):
    for axis, dim in sides:
        count = lax.axis_size(axis)
        forward = [(i, i + 1) for i in range(count - 1)]
        backward = [(target, source) for source, target in forward]
        low = lax.ppermute(
            lax.slice_in_dim(block, block.shape[dim] - width, None, axis=dim), axis, forward
        )
        high = lax.ppermute(lax.slice_in_dim(block, 0, width, axis=dim), axis, backward)
        block = jnp.concatenate([low, block, high], axis=dim)
    return block


def convolve(padded, weight):
    depth = padded.shape[1] - 2
    height = padded.shape[2] - 2
    width = padded.shape[3] - 2
    total = jnp.zeros((weight.shape[0], depth, height, width), jnp.float32)
    for tap in range(27):
        step_z = tap // 9
        step_y = tap // 3 % 3
        step_x = tap % 3
        piece = padded[
            :, step_z : step_z + depth, step_y : step_y + height, step_x : step_x + width
        ]
        total = total + jnp.einsum(
            "oc,czyx->ozyx", weight[:, :, tap], piece, precision=lax.Precision.HIGHEST
        )
    return total


def affine(earlier, later):
    return (earlier[0] * later[0], later[0] * earlier[1] + later[1])


def recurrent(padded, weight, bias, backward):
    channels = bias.shape[0]
    pre = convolve(padded, weight)
    cand = jnp.tanh(pre[:channels])
    keep = jax.nn.sigmoid(-(pre[channels:] + bias[:, None, None, None]))
    inject = (1.0 - keep) * cand
    if backward:
        keep = jnp.flip(keep, 1)
        inject = jnp.flip(inject, 1)
    cum_keep, cum_inject = lax.associative_scan(affine, (keep, inject), axis=1)
    total_keep = cum_keep[:, -1]
    total_inject = cum_inject[:, -1]
    offset = -1 if backward else 1

    def relay(turn, carry):
        return shifted(total_keep * carry + total_inject, "gz", offset)

    carry = lax.fori_loop(0, lax.axis_size("gz") - 1, relay, jnp.zeros_like(total_inject))
    hidden = cum_keep * carry[:, None] + cum_inject
    if backward:
        hidden = jnp.flip(hidden, 1)
    return hidden


def inside_mask(length, where, count):
    places = jnp.arange(length + 2)
    outside = (places == 0) & (where == 0) | (places == length + 1) & (where == count - 1)
    return jnp.where(outside, 0.0, 1.0).astype(jnp.float32)


def body(
    noisy,
    first_weight,
    first_bias,
    second_weight,
    second_bias,
    head_weight,
    seg_weight_in,
    seg_bias_in,
    seg_weight_out,
    seg_bias_out,
):
    noisy_pad = with_halo(noisy[None], (("gz", 1), ("gy", 2), ("gx", 3)), 1)
    first_hidden = recurrent(noisy_pad, first_weight, first_bias, False)
    hidden_pad = with_halo(first_hidden, (("gz", 1), ("gy", 2), ("gx", 3)), 1)
    second_hidden = recurrent(hidden_pad, second_weight, second_bias, True)
    denoised = noisy + jnp.einsum(
        "c,czyx->zyx", head_weight, second_hidden, precision=lax.Precision.HIGHEST
    )
    deep_pad = with_halo(denoised[None], (("gz", 1), ("gy", 2), ("gx", 3)), 2)
    grown = jnp.maximum(convolve(deep_pad, seg_weight_in) + seg_bias_in[:, None, None, None], 0.0)
    mask_z = inside_mask(denoised.shape[0], lax.axis_index("gz"), lax.axis_size("gz"))
    mask_y = inside_mask(denoised.shape[1], lax.axis_index("gy"), lax.axis_size("gy"))
    mask_x = inside_mask(denoised.shape[2], lax.axis_index("gx"), lax.axis_size("gx"))
    feature_pad = (
        grown * (mask_z[:, None, None] * mask_y[None, :, None] * mask_x[None, None, :])[None]
    )
    segmented = convolve(feature_pad, seg_weight_out) + seg_bias_out[:, None, None, None]
    return (denoised, segmented)


HALO = 4
LANES = 128


def split(value):
    high = value.astype(jnp.bfloat16)
    return high, (value - high.astype(jnp.float32)).astype(jnp.bfloat16)


def swapped(value, axis):
    return lax.ppermute(value, axis, [(0, 1), (1, 0)])


def gathered(noisy):
    count = lax.axis_size("gz")
    place = lax.axis_index("gz")
    slabs = [
        lax.ppermute(noisy, "gz", [(i, (i + s) % count) for i in range(count)])
        for s in range(count - 1, 0, -1)
    ] + [noisy]
    turns = jnp.concatenate(slabs + slabs[:-1], axis=0)
    depth = noisy.shape[0]
    block = lax.dynamic_slice_in_dim(turns, (count - 1 - place) * depth, count * depth, 0)
    for axis, dim in (("gy", 1), ("gx", 2)):
        first = lax.axis_index(axis) == 0
        size = block.shape[dim]
        low = lax.slice_in_dim(block, 0, HALO, axis=dim)
        high = lax.slice_in_dim(block, size - HALO, size, axis=dim)
        other = swapped(jnp.where(first, high, low), axis)
        block = jnp.where(
            first,
            jnp.concatenate([block, other], dim),
            jnp.concatenate([other, block], dim),
        )
    return block


def prepare(
    geometry,
    w1_ref,
    b1_ref,
    w2_ref,
    b2_ref,
    head_ref,
    w3_ref,
    b3_ref,
    w4_ref,
    b4_ref,
    thin_lane_ref,
    thin_sub_ref,
    spread_ref,
    keep_ref,
    gather_ref,
    w1_out,
    w2_out,
    w3_out,
    w4_out,
    columns_out,
    band,
):
    deep, depth, channels = geometry
    f32, bf16 = jnp.float32, jnp.bfloat16
    place = lax.axis_index("gz") * depth

    def dot(left, right):
        return jnp.dot(left, right, preferred_element_type=f32)

    tap_lane, z_lane, part_lane = (thin_lane_ref[i : i + 1, :] for i in range(3))
    tap_sub, a_sub = (thin_sub_ref[:, i : i + 1] for i in range(2))
    same = tap_lane == tap_sub
    crossed = part_lane == 1
    reach = z_lane - a_sub + 1

    def thin_rows(halves, z):
        hit = same & (reach == z)
        high = jnp.where(hit & ~crossed, 1.0, 0.0).astype(bf16)
        low = jnp.where(hit & crossed, 1.0, 0.0).astype(bf16)
        return (dot(halves[0], high) + dot(halves[1], low)).astype(bf16)

    first = split(w1_ref[:, 0, :])
    out = 2 * channels
    for z in range(deep):
        w1_out[z * out : (z + 1) * out, :] = thin_rows(first, z)
    grow = split(w3_ref[:, 0, :])
    for i in range(depth + 2):
        z = place + i - 1
        inside = (z >= 0) & (z < deep)
        w3_out[i * channels : (i + 1) * channels, :] = thin_rows(
            grow, jnp.where(inside, z, -deep)
        )

    spread = spread_ref[...]
    step = 9 * channels
    for w_ref, w_out in ((w2_ref, w2_out), (w4_ref, w4_out)):
        out = w_ref.shape[0] // channels
        keep = jnp.concatenate([keep_ref[...]] * out, 0)
        gather = gather_ref[:out, : out * channels]
        for part, half in enumerate(split(w_ref[...])):
            flat = dot(gather, (dot(half, spread) * keep).astype(bf16))
            band[...] = jnp.zeros_like(band)
            for z in range(depth):
                band[z * out : (z + 1) * out, pl.ds(z * step, 3 * step)] = flat
            rows = depth * out
            w_out[part * rows : (part + 1) * rows, :] = band[:rows, :].astype(bf16)

    at_row = lax.broadcasted_iota(jnp.int32, (channels, channels), 0)
    at_lane = lax.broadcasted_iota(jnp.int32, (channels, channels), 1)
    for i, ref in enumerate((b1_ref, b2_ref, head_ref, b3_ref, b4_ref)):
        columns_out[:, i : i + 1] = jnp.sum(
            jnp.where(at_row == at_lane, ref[...], 0.0), axis=1, keepdims=True
        )


def kernel(
    geometry,
    noisy_ref,
    mask_ref,
    w1_ref,
    w2_ref,
    w3_ref,
    w4_ref,
    columns_ref,
    den_ref,
    seg_ref,
    stage,
    thin,
    pre,
    rows,
    wide_hi,
    wide_lo,
):
    deep, depth, channels, pitch, span, margin = geometry
    mask = mask_ref[...]
    place = lax.axis_index("gz")
    bias1, bias2, head, bias3, bias4 = (columns_ref[:, i : i + 1] for i in range(5))
    shifts = [(b - 1) * pitch + (c - 1) for b in range(3) for c in range(3)]
    f32 = jnp.float32

    def shifted(slot, shift):
        return stage[slot, :, pl.ds(margin + shift, span)]

    def thin_columns(field):
        high, low = split(field)
        stage[0, :, pl.ds(margin, span)] = high
        stage[1, :, pl.ds(margin, span)] = low
        for t, s in enumerate(shifts):
            h = shifted(0, s)
            thin[pl.ds(t * deep, deep), :] = h
            thin[pl.ds((9 + t) * deep, deep), :] = h
            thin[pl.ds((18 + t) * deep, deep), :] = shifted(1, s)

    def wide_columns(z, field):
        high, low = split(field)
        stage[0, :, pl.ds(margin, span)] = high
        stage[1, :, pl.ds(margin, span)] = low
        for t, s in enumerate(shifts):
            at = pl.ds(pl.multiple_of((z * 9 + t) * channels, channels), channels)
            wide_hi[at, :] = shifted(0, s)
            wide_lo[at, :] = shifted(1, s)

    def banded(w_ref, start, taps):
        at = pl.ds(pl.multiple_of(start, channels), taps)
        rows_of = w_ref.shape[0] // 2
        wh = w_ref[:rows_of]
        wl = w_ref[rows_of:]
        h = wide_hi[at, :]
        out = jnp.dot(wh, h, preferred_element_type=f32)
        out = out + jnp.dot(wh, wide_lo[at, :], preferred_element_type=f32)
        return out + jnp.dot(wl, h, preferred_element_type=f32)

    def gate(at, bias, hidden):
        cand = jnp.tanh(pre[pl.ds(pl.multiple_of(at, channels), channels), :])
        up = pre[pl.ds(pl.multiple_of(at + channels, channels), channels), :] + bias
        fresh = 1.0 / (1.0 + jnp.exp(-up))
        return hidden + fresh * (cand - hidden)

    stage[...] = jnp.zeros_like(stage)
    noisy = noisy_ref[...]
    thin_columns(noisy)
    pre[...] = jnp.dot(w1_ref[...], thin[...], preferred_element_type=f32)
    edge = 9 * channels
    zeros = jnp.zeros((edge, span), jnp.bfloat16)
    for wide in (wide_hi, wide_lo):
        wide[pl.ds(0, edge), :] = zeros
        wide[pl.ds((deep + 1) * edge, edge), :] = zeros

    def first(z, hidden):
        hidden = gate(z * 2 * channels, bias1, hidden)
        wide_columns(z + 1, hidden * mask)
        return hidden

    blank = jnp.zeros((channels, span), f32)
    lax.fori_loop(0, deep, first, blank)

    taps = (depth + 2) * edge
    block_rows = depth * 2 * channels

    def second(turn, hidden):
        b = deep // depth - 1 - turn
        pre[pl.ds(0, block_rows), :] = banded(w2_ref, b * depth * edge, taps)
        for zo in range(depth - 1, -1, -1):
            hidden = gate(zo * 2 * channels, bias2, hidden)
            rows[pl.ds(b * depth + zo, 1), :] = jnp.sum(
                hidden * head, axis=0, keepdims=True
            )
        return hidden

    lax.fori_loop(0, deep // depth, second, blank)

    rows[...] = (noisy + rows[...]) * mask
    finished = rows[...]
    thin_columns(finished)
    grown = jnp.dot(w3_ref[...], thin[...], preferred_element_type=f32)
    for i in range(depth + 2):
        z = place * depth + i - 1
        real = jnp.where((z >= 0) & (z < deep), 1.0, 0.0)
        layer = grown[i * channels : (i + 1) * channels]
        wide_columns(i, jnp.maximum(layer + bias3, 0.0) * (mask * real))
    pre[pl.ds(0, depth * channels), :] = banded(w4_ref, 0, taps)

    height, width = den_ref.shape[1:]
    for y in range(2):
        for x in range(2):

            @pl.when((lax.axis_index("gy") == y) & (lax.axis_index("gx") == x))
            def _():
                for r in range(height):
                    lanes = pl.ds((y * HALO + r) * pitch + x * HALO, width)
                    mine = rows[pl.ds(0, depth), lanes]
                    for b in range(1, deep // depth):
                        mine = jnp.where(place == b, rows[pl.ds(b * depth, depth), lanes], mine)
                    den_ref[:, r, :] = mine
                    for z in range(depth):
                        seg_ref[:, z, r, :] = (
                            pre[pl.ds(z * channels, channels), lanes] + bias4
                        )


def local_body(
    noisy,
    first_weight,
    first_bias,
    second_weight,
    second_bias,
    head_weight,
    seg_weight_in,
    seg_bias_in,
    seg_weight_out,
    seg_bias_out,
):
    depth, height, width = noisy.shape
    count = lax.axis_size("gz")
    place = lax.axis_index("gz")
    deep = count * depth
    channels = first_bias.shape[0]
    high, pitch = height + HALO, width + HALO + 1
    span = -(-high * pitch // LANES) * LANES
    margin = -(-(pitch + 1) // LANES) * LANES

    window = gathered(noisy)
    flat = jnp.pad(window, ((0, 0), (0, 0), (0, 1))).reshape(deep, high * pitch)
    flat = jnp.pad(flat, ((0, 0), (0, span - high * pitch)))
    inside = np.zeros((high, pitch), np.float32)
    inside[:, : pitch - 1] = 1.0
    mask = jnp.asarray(np.pad(inside.reshape(1, -1), ((0, 0), (0, span - high * pitch))))

    f32, bf16, int32 = jnp.float32, jnp.bfloat16, jnp.int32
    lane = np.arange(27 * deep)
    thin_lane = np.stack(
        [lane // deep % 9, lane % deep, lane // (9 * deep)] + [lane * 0] * 5
    ).astype(np.int32)
    thin_sub = np.stack([np.arange(27) % 9, np.arange(27) // 9], 1).astype(np.int32)
    lane = np.arange(27 * channels)
    spread = (np.arange(27)[:, None] == lane[None] // channels).astype(bf16)
    keep = (np.arange(channels)[:, None] == lane[None] % channels).astype(np.float32)
    lane = np.arange(2 * channels * channels)
    gather = (np.arange(2 * channels)[:, None] == lane[None] // channels).astype(bf16)

    taps = (depth + 2) * 9 * channels
    in_vmem = pl.BlockSpec(memory_space=pltpu.VMEM)
    w1, w2, w3, w4, columns = pl.pallas_call(
        functools.partial(prepare, (deep, depth, channels)),
        out_shape=(
            pltpu.VMEM((deep * 2 * channels, 27 * deep), bf16),
            pltpu.VMEM((2 * depth * 2 * channels, taps), bf16),
            pltpu.VMEM(((depth + 2) * channels, 27 * deep), bf16),
            pltpu.VMEM((2 * depth * channels, taps), bf16),
            pltpu.VMEM((channels, LANES), f32),
        ),
        in_specs=[in_vmem] * 14,
        out_specs=(in_vmem,) * 5,
        scratch_shapes=[pltpu.VMEM((depth * 2 * channels, taps), f32)],
        compiler_params=pltpu.CompilerParams(vmem_limit_bytes=16 * 1024 * 1024),
    )(
        first_weight,
        first_bias.reshape(1, -1),
        second_weight.reshape(-1, 27),
        second_bias.reshape(1, -1),
        head_weight.reshape(1, -1),
        seg_weight_in,
        seg_bias_in.reshape(1, -1),
        seg_weight_out.reshape(-1, 27),
        seg_bias_out.reshape(1, -1),
        jnp.asarray(thin_lane),
        jnp.asarray(thin_sub),
        jnp.asarray(spread),
        jnp.asarray(keep),
        jnp.asarray(gather),
    )
    operands = [
        pltpu.with_memory_space_constraint(v, pltpu.VMEM)
        for v in (flat, mask, w1, w2, w3, w4, columns)
    ]
    return pl.pallas_call(
        functools.partial(kernel, (deep, depth, channels, pitch, span, margin)),
        out_shape=(
            jax.ShapeDtypeStruct((depth, height, width), f32),
            jax.ShapeDtypeStruct((channels, depth, height, width), f32),
        ),
        in_specs=[in_vmem] * 7,
        out_specs=(in_vmem,) * 2,
        scratch_shapes=[
            pltpu.VMEM((2, channels, span + 2 * margin), bf16),
            pltpu.VMEM((27 * deep, span), bf16),
            pltpu.VMEM((deep * 2 * channels, span), f32),
            pltpu.VMEM((deep, span), f32),
            pltpu.VMEM(((deep + 2) * 9 * channels, span), bf16),
            pltpu.VMEM(((deep + 2) * 9 * channels, span), bf16),
        ],
        compiler_params=pltpu.CompilerParams(vmem_limit_bytes=36 * 1024 * 1024),
    )(*operands)


def solution(mesh):
    in_specs = (P(("win", "gz"), "gy", "gx"), P(), P(), P(), P(), P(), P(), P(), P(), P())
    out_specs = (P(("win", "gz"), "gy", "gx"), P(None, ("win", "gz"), "gy", "gx"))
    shallow = mesh.shape["gz"] <= 4 and mesh.shape["gy"] == 2 and mesh.shape["gx"] == 2
    chosen = local_body if shallow else body
    return jax.shard_map(chosen, mesh=mesh, in_specs=in_specs, out_specs=out_specs, check_vma=False)
```

```python
import functools

import jax
import jax.numpy as jnp
import numpy as np
from jax import lax
from jax.experimental import pallas as pl
from jax.experimental.pallas import tpu as pltpu
from jax.sharding import PartitionSpec as P


def shifted(value, axis, steps):
    count = lax.axis_size(axis)
    first, last = (max(0, -steps), min(count, count - steps))
    return lax.ppermute(value, axis, [(source, source + steps) for source in range(first, last)])


def with_halo(block, sides, width):
    for axis, dim in sides:
        count = lax.axis_size(axis)
        forward = [(i, i + 1) for i in range(count - 1)]
        backward = [(target, source) for source, target in forward]
        low = lax.ppermute(
            lax.slice_in_dim(block, block.shape[dim] - width, None, axis=dim), axis, forward
        )
        high = lax.ppermute(lax.slice_in_dim(block, 0, width, axis=dim), axis, backward)
        block = jnp.concatenate([low, block, high], axis=dim)
    return block


def convolve(padded, weight):
    depth = padded.shape[1] - 2
    height = padded.shape[2] - 2
    width = padded.shape[3] - 2
    total = jnp.zeros((weight.shape[0], depth, height, width), jnp.float32)
    for tap in range(27):
        step_z = tap // 9
        step_y = tap // 3 % 3
        step_x = tap % 3
        piece = padded[
            :, step_z : step_z + depth, step_y : step_y + height, step_x : step_x + width
        ]
        total = total + jnp.einsum(
            "oc,czyx->ozyx", weight[:, :, tap], piece, precision=lax.Precision.HIGHEST
        )
    return total


def affine(earlier, later):
    return (earlier[0] * later[0], later[0] * earlier[1] + later[1])


def recurrent(padded, weight, bias, backward):
    channels = bias.shape[0]
    pre = convolve(padded, weight)
    cand = jnp.tanh(pre[:channels])
    keep = jax.nn.sigmoid(-(pre[channels:] + bias[:, None, None, None]))
    inject = (1.0 - keep) * cand
    if backward:
        keep = jnp.flip(keep, 1)
        inject = jnp.flip(inject, 1)
    cum_keep, cum_inject = lax.associative_scan(affine, (keep, inject), axis=1)
    total_keep = cum_keep[:, -1]
    total_inject = cum_inject[:, -1]
    offset = -1 if backward else 1

    def relay(turn, carry):
        return shifted(total_keep * carry + total_inject, "gz", offset)

    carry = lax.fori_loop(0, lax.axis_size("gz") - 1, relay, jnp.zeros_like(total_inject))
    hidden = cum_keep * carry[:, None] + cum_inject
    if backward:
        hidden = jnp.flip(hidden, 1)
    return hidden


def inside_mask(length, where, count):
    places = jnp.arange(length + 2)
    outside = (places == 0) & (where == 0) | (places == length + 1) & (where == count - 1)
    return jnp.where(outside, 0.0, 1.0).astype(jnp.float32)


def body(
    noisy,
    first_weight,
    first_bias,
    second_weight,
    second_bias,
    head_weight,
    seg_weight_in,
    seg_bias_in,
    seg_weight_out,
    seg_bias_out,
):
    noisy_pad = with_halo(noisy[None], (("gz", 1), ("gy", 2), ("gx", 3)), 1)
    first_hidden = recurrent(noisy_pad, first_weight, first_bias, False)
    hidden_pad = with_halo(first_hidden, (("gz", 1), ("gy", 2), ("gx", 3)), 1)
    second_hidden = recurrent(hidden_pad, second_weight, second_bias, True)
    denoised = noisy + jnp.einsum(
        "c,czyx->zyx", head_weight, second_hidden, precision=lax.Precision.HIGHEST
    )
    deep_pad = with_halo(denoised[None], (("gz", 1), ("gy", 2), ("gx", 3)), 2)
    grown = jnp.maximum(convolve(deep_pad, seg_weight_in) + seg_bias_in[:, None, None, None], 0.0)
    mask_z = inside_mask(denoised.shape[0], lax.axis_index("gz"), lax.axis_size("gz"))
    mask_y = inside_mask(denoised.shape[1], lax.axis_index("gy"), lax.axis_size("gy"))
    mask_x = inside_mask(denoised.shape[2], lax.axis_index("gx"), lax.axis_size("gx"))
    feature_pad = (
        grown * (mask_z[:, None, None] * mask_y[None, :, None] * mask_x[None, None, :])[None]
    )
    segmented = convolve(feature_pad, seg_weight_out) + seg_bias_out[:, None, None, None]
    return (denoised, segmented)


HALO = 4
LANES = 128


def split(value):
    high = value.astype(jnp.bfloat16)
    return high, (value - high.astype(jnp.float32)).astype(jnp.bfloat16)


def swapped(value, axis):
    return lax.ppermute(value, axis, [(0, 1), (1, 0)])


def gathered(noisy):
    count = lax.axis_size("gz")
    place = lax.axis_index("gz")
    slabs = [
        lax.ppermute(noisy, "gz", [(i, (i + s) % count) for i in range(count)])
        for s in range(count - 1, 0, -1)
    ] + [noisy]
    turns = jnp.concatenate(slabs + slabs[:-1], axis=0)
    depth = noisy.shape[0]
    block = lax.dynamic_slice_in_dim(turns, (count - 1 - place) * depth, count * depth, 0)
    block = jnp.where(lax.axis_index("gy") == 0, block, jnp.flip(block, 1))
    near = lax.slice_in_dim(block, block.shape[1] - HALO, None, axis=1)
    block = jnp.concatenate([block, swapped(jnp.flip(near, 1), "gy")], 1)
    first = lax.axis_index("gx") == 0
    size = block.shape[2]
    low = lax.slice_in_dim(block, 0, HALO, axis=2)
    high = lax.slice_in_dim(block, size - HALO, size, axis=2)
    other = swapped(jnp.where(first, high, low), "gx")
    return jnp.where(
        first, jnp.concatenate([block, other], 2), jnp.concatenate([other, block], 2)
    )


def prepare(
    geometry,
    w1_ref,
    b1_ref,
    w2_ref,
    b2_ref,
    head_ref,
    w3_ref,
    b3_ref,
    w4_ref,
    b4_ref,
    thin_lane_ref,
    thin_sub_ref,
    wide_lane_ref,
    keep_ref,
    gather_ref,
    w1_out,
    w2_out,
    w3_out,
    w4_out,
    columns_out,
    band,
):
    deep, depth, channels = geometry
    f32, bf16 = jnp.float32, jnp.bfloat16
    place = lax.axis_index("gz") * depth
    turned = lax.axis_index("gy") == 1

    def dot(left, right):
        return jnp.dot(left, right, preferred_element_type=f32)

    tap_lane, z_lane, part_lane = (thin_lane_ref[i : i + 1, :] for i in range(3))
    a_sub, tap_ahead, tap_turned = (thin_sub_ref[:, i : i + 1] for i in range(3))
    same = tap_lane == jnp.where(turned, tap_turned, tap_ahead)
    crossed = part_lane == 1
    reach = z_lane - a_sub + 1

    def thin_rows(halves, z):
        hit = same & (reach == z)
        high = jnp.where(hit & ~crossed, 1.0, 0.0).astype(bf16)
        low = jnp.where(hit & crossed, 1.0, 0.0).astype(bf16)
        return (dot(halves[0], high) + dot(halves[1], low)).astype(bf16)

    first = split(w1_ref[:, 0, :])
    out = 2 * channels
    for z in range(deep):
        w1_out[z * out : (z + 1) * out, :] = thin_rows(first, z)
    grow = split(w3_ref[:, 0, :])
    for i in range(depth + 2):
        z = place + i - 1
        inside = (z >= 0) & (z < deep)
        w3_out[i * channels : (i + 1) * channels, :] = thin_rows(
            grow, jnp.where(inside, z, -deep)
        )

    taps = lax.broadcasted_iota(jnp.int32, (27, wide_lane_ref.shape[1]), 0)
    spread = taps == jnp.where(turned, wide_lane_ref[1:2, :], wide_lane_ref[0:1, :])
    spread = jnp.where(spread, 1.0, 0.0).astype(bf16)
    step = 3 * channels
    part = (depth + 2) * step
    band[...] = jnp.zeros_like(band)
    for w_ref, w_out in ((w2_ref, w2_out), (w4_ref, w4_out)):
        out = w_ref.shape[0] // channels
        keep = jnp.concatenate([keep_ref[...]] * out, 0)
        gather = gather_ref[:out, : out * channels]
        flats = [
            dot(gather, (dot(half, spread) * keep).astype(bf16)) for half in split(w_ref[...])
        ]
        for b in range(3):
            for i, half in enumerate((0, 0, 1)):
                piece = flats[half][:, b * 3 * step : (b + 1) * 3 * step]
                for z in range(depth):
                    row = (b * depth + z) * out
                    band[row : row + out, pl.ds(i * part + z * step, 3 * step)] = piece
        w_out[...] = band[: w_out.shape[0], :].astype(bf16)
        if w_ref is w2_ref:
            band[: w4_out.shape[0], :] = jnp.zeros((w4_out.shape[0], 3 * part), f32)

    at_row = lax.broadcasted_iota(jnp.int32, (channels, channels), 0)
    at_lane = lax.broadcasted_iota(jnp.int32, (channels, channels), 1)
    for i, ref in enumerate((b1_ref, b2_ref, head_ref, b3_ref, b4_ref)):
        columns_out[:, i : i + 1] = jnp.sum(
            jnp.where(at_row == at_lane, ref[...], 0.0), axis=1, keepdims=True
        )


def kernel(
    geometry,
    noisy_ref,
    mask_ref,
    w1_ref,
    w2_ref,
    w3_ref,
    w4_ref,
    columns_ref,
    den_ref,
    seg_ref,
    stage,
    thin,
    pre,
    rows,
    wide_hi,
    wide_lo,
    sums,
):
    deep, depth, channels, pitch, high, span, margin = geometry
    f32 = jnp.float32
    mask = mask_ref[...]
    place = lax.axis_index("gz")
    bias1, bias2, head, bias3, bias4 = (columns_ref[:, i : i + 1] for i in range(5))
    shifts = [(b - 1) * pitch + (c - 1) for b in range(3) for c in range(3)]
    first_span, second_span, third_span = (
        -(-(high - i) * pitch // LANES) * LANES for i in range(1, 4)
    )
    blocks = deep // depth

    def put(field):
        for slot, half in enumerate(split(field)):
            stage[slot, :, pl.ds(margin, field.shape[1])] = half

    def shifted(slot, shift, length):
        return stage[slot, :, pl.ds(margin + shift, length)]

    def thin_columns(field, length):
        put(field)
        for t, s in enumerate(shifts):
            h = shifted(0, s, length)
            thin[t * deep : (t + 1) * deep, :length] = h
            thin[(9 + t) * deep : (10 + t) * deep, :length] = h
            thin[(18 + t) * deep : (19 + t) * deep, :length] = shifted(1, s, length)

    def wide_columns(z, field):
        length = field.shape[1]
        put(field)
        for c in range(3):
            at = (z * 3 + c) * channels
            wide_hi[at : at + channels, :length] = shifted(0, c - 1, length)
            wide_lo[at : at + channels, :length] = shifted(1, c - 1, length)

    taps = (depth + 2) * 3 * channels

    def chunks(length):
        return [(i, min(2 * LANES, length - i)) for i in range(0, length, 2 * LANES)]

    def banded(w_ref, slot, start, chunk):
        at, length = chunk
        h = wide_hi[start : start + taps, at : at + length]
        l = wide_lo[start : start + taps, at : at + length]
        sums[slot, : w_ref.shape[0], pl.ds(margin + at, length)] = jnp.dot(
            w_ref[...], jnp.concatenate([h, l, h], 0), preferred_element_type=f32
        )

    def gate(cand, up, hidden):
        fresh = 1.0 / (1.0 + jnp.exp(-up))
        return hidden + fresh * (jnp.tanh(cand) - hidden)

    stage[...] = jnp.zeros_like(stage)
    aside = jnp.zeros(sums.shape[:2] + (margin,), f32)
    sums[:, :, :margin] = aside
    sums[:, :, sums.shape[2] - margin :] = aside
    edge = 3 * channels
    zeros = jnp.zeros((edge, wide_hi.shape[1]), jnp.bfloat16)
    for wide in (wide_hi, wide_lo):
        wide[:edge, :] = zeros
        wide[(deep + 1) * edge :, :] = zeros

    noisy = noisy_ref[...]
    thin_columns(noisy, first_span)
    pre[...] = jnp.dot(w1_ref[...], thin[:, :first_span], preferred_element_type=f32)

    hidden = jnp.zeros((channels, first_span), f32)
    for z in range(deep):
        at = z * 2 * channels
        hidden = gate(
            pre[at : at + channels, :],
            pre[at + channels : at + 2 * channels, :] + bias1,
            hidden,
        )
        wide_columns(z + 1, hidden * mask[:, :first_span])

    def layer(slot, at, length, lift=0):
        return sum(
            sums[
                slot,
                at + b * depth * lift : at + b * depth * lift + channels,
                pl.ds(margin + (b - 1) * pitch, length),
            ]
            for b in range(3)
        )

    hidden = jnp.zeros((channels, second_span), f32)
    todo = chunks(first_span)
    for chunk in todo:
        banded(w2_ref, (blocks - 1) % 2, (blocks - 1) * depth * edge, chunk)
    for b in range(blocks - 1, -1, -1):
        for zo in range(depth - 1, -1, -1):
            if b > 0:
                turn = depth - 1 - zo
                for chunk in todo[turn::depth]:
                    banded(w2_ref, (b - 1) % 2, (b - 1) * depth * edge, chunk)
            at = zo * 2 * channels
            hidden = gate(
                layer(b % 2, at, second_span, 2 * channels),
                layer(b % 2, at + channels, second_span, 2 * channels) + bias2,
                hidden,
            )
            z = b * depth + zo
            rows[z : z + 1, :second_span] = jnp.sum(hidden * head, axis=0, keepdims=True)

    finished = (noisy[:, :second_span] + rows[:, :second_span]) * mask[:, :second_span]
    rows[:, :second_span] = finished
    thin_columns(finished, third_span)
    grown = jnp.dot(w3_ref[...], thin[:, :third_span], preferred_element_type=f32)
    for i in range(depth + 2):
        z = place * depth + i - 1
        real = jnp.where((z >= 0) & (z < deep), 1.0, 0.0)
        features = jnp.maximum(grown[i * channels : (i + 1) * channels] + bias3, 0.0)
        wide_columns(i, features * (mask[:, :third_span] * real))
    for chunk in chunks(third_span):
        banded(w4_ref, 0, 0, chunk)

    height, width = den_ref.shape[1:]
    for y in range(2):
        for x in range(2):

            @pl.when((lax.axis_index("gy") == y) & (lax.axis_index("gx") == x))
            def _():
                for r in range(height):
                    row = height - 1 - r if y else r
                    at = r * pitch + x * HALO
                    mine = rows[:depth, pl.ds(at, width)]
                    for b in range(1, blocks):
                        other = rows[b * depth : (b + 1) * depth, pl.ds(at, width)]
                        mine = jnp.where(place == b, other, mine)
                    den_ref[:, row, :] = mine
                    for z in range(depth):
                        total = bias4
                        for b in range(3):
                            k = (b * depth + z) * channels
                            lanes = pl.ds(margin + at + (b - 1) * pitch, width)
                            total = total + sums[0, k : k + channels, lanes]
                        seg_ref[:, z, row, :] = total


def local_body(
    noisy,
    first_weight,
    first_bias,
    second_weight,
    second_bias,
    head_weight,
    seg_weight_in,
    seg_bias_in,
    seg_weight_out,
    seg_bias_out,
):
    depth, height, width = noisy.shape
    count = lax.axis_size("gz")
    place = lax.axis_index("gz")
    deep = count * depth
    channels = first_bias.shape[0]
    high, pitch = height + HALO, width + HALO + 1
    span = -(-high * pitch // LANES) * LANES
    margin = -(-(pitch + 1) // LANES) * LANES
    narrow = -(-(high - 1) * pitch // LANES) * LANES

    window = gathered(noisy)
    flat = jnp.pad(window, ((0, 0), (0, 0), (0, 1))).reshape(deep, high * pitch)
    flat = jnp.pad(flat, ((0, 0), (0, span - high * pitch)))
    inside = np.zeros((high, pitch), np.float32)
    inside[:, : pitch - 1] = 1.0
    mask = jnp.asarray(np.pad(inside.reshape(1, -1), ((0, 0), (0, span - high * pitch))))

    f32, bf16, int32 = jnp.float32, jnp.bfloat16, jnp.int32
    lane = np.arange(27 * deep)
    thin_lane = np.stack(
        [lane // deep % 9, lane % deep, lane // (9 * deep)] + [lane * 0] * 5
    ).astype(np.int32)
    tap = np.arange(27)
    thin_sub = np.stack(
        [tap // 9, tap % 9, (2 - tap // 3 % 3) * 3 + tap % 3], 1
    ).astype(np.int32)
    lane = np.arange(27 * channels)
    b, a, c = lane // channels // 9, lane // channels // 3 % 3, lane // channels % 3
    wide_lane = np.stack(
        [a * 9 + b * 3 + c, a * 9 + (2 - b) * 3 + c] + [lane * 0] * 6
    ).astype(np.int32)
    keep = (np.arange(channels)[:, None] == lane[None] % channels).astype(np.float32)
    lane = np.arange(2 * channels * channels)
    gather = (np.arange(2 * channels)[:, None] == lane[None] // channels).astype(bf16)

    taps = 3 * (depth + 2) * 3 * channels
    in_vmem = pl.BlockSpec(memory_space=pltpu.VMEM)
    w1, w2, w3, w4, columns = pl.pallas_call(
        functools.partial(prepare, (deep, depth, channels)),
        out_shape=(
            pltpu.VMEM((deep * 2 * channels, 27 * deep), bf16),
            pltpu.VMEM((3 * depth * 2 * channels, taps), bf16),
            pltpu.VMEM(((depth + 2) * channels, 27 * deep), bf16),
            pltpu.VMEM((3 * depth * channels, taps), bf16),
            pltpu.VMEM((channels, LANES), f32),
        ),
        in_specs=[in_vmem] * 14,
        out_specs=(in_vmem,) * 5,
        scratch_shapes=[pltpu.VMEM((3 * depth * 2 * channels, taps), f32)],
        compiler_params=pltpu.CompilerParams(vmem_limit_bytes=16 * 1024 * 1024),
    )(
        first_weight,
        first_bias.reshape(1, -1),
        second_weight.reshape(-1, 27),
        second_bias.reshape(1, -1),
        head_weight.reshape(1, -1),
        seg_weight_in,
        seg_bias_in.reshape(1, -1),
        seg_weight_out.reshape(-1, 27),
        seg_bias_out.reshape(1, -1),
        jnp.asarray(thin_lane),
        jnp.asarray(thin_sub),
        jnp.asarray(wide_lane),
        jnp.asarray(keep),
        jnp.asarray(gather),
    )
    operands = [
        pltpu.with_memory_space_constraint(v, pltpu.VMEM)
        for v in (flat, mask, w1, w2, w3, w4, columns)
    ]
    return pl.pallas_call(
        functools.partial(kernel, (deep, depth, channels, pitch, high, span, margin)),
        out_shape=(
            jax.ShapeDtypeStruct((depth, height, width), f32),
            jax.ShapeDtypeStruct((channels, depth, height, width), f32),
        ),
        in_specs=[in_vmem] * 7,
        out_specs=(in_vmem,) * 2,
        scratch_shapes=[
            pltpu.VMEM((2, channels, span + 2 * margin), bf16),
            pltpu.VMEM((27 * deep, span), bf16),
            pltpu.VMEM((deep * 2 * channels, narrow), f32),
            pltpu.VMEM((deep, span), f32),
            pltpu.VMEM(((deep + 2) * 3 * channels, narrow), bf16),
            pltpu.VMEM(((deep + 2) * 3 * channels, narrow), bf16),
            pltpu.VMEM((2, 3 * depth * 2 * channels, narrow + 2 * margin), f32),
        ],
        compiler_params=pltpu.CompilerParams(vmem_limit_bytes=36 * 1024 * 1024),
    )(*operands)


def solution(mesh):
    in_specs = (P(("win", "gz"), "gy", "gx"), P(), P(), P(), P(), P(), P(), P(), P(), P())
    out_specs = (P(("win", "gz"), "gy", "gx"), P(None, ("win", "gz"), "gy", "gx"))
    shallow = mesh.shape["gz"] <= 4 and mesh.shape["gy"] == 2 and mesh.shape["gx"] == 2
    chosen = local_body if shallow else body
    return jax.shard_map(chosen, mesh=mesh, in_specs=in_specs, out_specs=out_specs, check_vma=False)
```

```python
import functools

import jax
import jax.numpy as jnp
import numpy as np
from jax import lax
from jax.experimental import pallas as pl
from jax.experimental.pallas import tpu as pltpu
from jax.sharding import PartitionSpec as P


def shifted(value, axis, steps):
    count = lax.axis_size(axis)
    first, last = (max(0, -steps), min(count, count - steps))
    return lax.ppermute(value, axis, [(source, source + steps) for source in range(first, last)])


def with_halo(block, sides, width):
    for axis, dim in sides:
        count = lax.axis_size(axis)
        forward = [(i, i + 1) for i in range(count - 1)]
        backward = [(target, source) for source, target in forward]
        low = lax.ppermute(
            lax.slice_in_dim(block, block.shape[dim] - width, None, axis=dim), axis, forward
        )
        high = lax.ppermute(lax.slice_in_dim(block, 0, width, axis=dim), axis, backward)
        block = jnp.concatenate([low, block, high], axis=dim)
    return block


def convolve(padded, weight):
    depth = padded.shape[1] - 2
    height = padded.shape[2] - 2
    width = padded.shape[3] - 2
    total = jnp.zeros((weight.shape[0], depth, height, width), jnp.float32)
    for tap in range(27):
        step_z = tap // 9
        step_y = tap // 3 % 3
        step_x = tap % 3
        piece = padded[
            :, step_z : step_z + depth, step_y : step_y + height, step_x : step_x + width
        ]
        total = total + jnp.einsum(
            "oc,czyx->ozyx", weight[:, :, tap], piece, precision=lax.Precision.HIGHEST
        )
    return total


def affine(earlier, later):
    return (earlier[0] * later[0], later[0] * earlier[1] + later[1])


def recurrent(padded, weight, bias, backward):
    channels = bias.shape[0]
    pre = convolve(padded, weight)
    cand = jnp.tanh(pre[:channels])
    keep = jax.nn.sigmoid(-(pre[channels:] + bias[:, None, None, None]))
    inject = (1.0 - keep) * cand
    if backward:
        keep = jnp.flip(keep, 1)
        inject = jnp.flip(inject, 1)
    cum_keep, cum_inject = lax.associative_scan(affine, (keep, inject), axis=1)
    total_keep = cum_keep[:, -1]
    total_inject = cum_inject[:, -1]
    offset = -1 if backward else 1

    def relay(turn, carry):
        return shifted(total_keep * carry + total_inject, "gz", offset)

    carry = lax.fori_loop(0, lax.axis_size("gz") - 1, relay, jnp.zeros_like(total_inject))
    hidden = cum_keep * carry[:, None] + cum_inject
    if backward:
        hidden = jnp.flip(hidden, 1)
    return hidden


def inside_mask(length, where, count):
    places = jnp.arange(length + 2)
    outside = (places == 0) & (where == 0) | (places == length + 1) & (where == count - 1)
    return jnp.where(outside, 0.0, 1.0).astype(jnp.float32)


def body(
    noisy,
    first_weight,
    first_bias,
    second_weight,
    second_bias,
    head_weight,
    seg_weight_in,
    seg_bias_in,
    seg_weight_out,
    seg_bias_out,
):
    noisy_pad = with_halo(noisy[None], (("gz", 1), ("gy", 2), ("gx", 3)), 1)
    first_hidden = recurrent(noisy_pad, first_weight, first_bias, False)
    hidden_pad = with_halo(first_hidden, (("gz", 1), ("gy", 2), ("gx", 3)), 1)
    second_hidden = recurrent(hidden_pad, second_weight, second_bias, True)
    denoised = noisy + jnp.einsum(
        "c,czyx->zyx", head_weight, second_hidden, precision=lax.Precision.HIGHEST
    )
    deep_pad = with_halo(denoised[None], (("gz", 1), ("gy", 2), ("gx", 3)), 2)
    grown = jnp.maximum(convolve(deep_pad, seg_weight_in) + seg_bias_in[:, None, None, None], 0.0)
    mask_z = inside_mask(denoised.shape[0], lax.axis_index("gz"), lax.axis_size("gz"))
    mask_y = inside_mask(denoised.shape[1], lax.axis_index("gy"), lax.axis_size("gy"))
    mask_x = inside_mask(denoised.shape[2], lax.axis_index("gx"), lax.axis_size("gx"))
    feature_pad = (
        grown * (mask_z[:, None, None] * mask_y[None, :, None] * mask_x[None, None, :])[None]
    )
    segmented = convolve(feature_pad, seg_weight_out) + seg_bias_out[:, None, None, None]
    return (denoised, segmented)


HALO = 4
LANES = 128


def split(value):
    high = value.astype(jnp.bfloat16)
    return high, (value - high.astype(jnp.float32)).astype(jnp.bfloat16)


def swapped(value, axis):
    return lax.ppermute(value, axis, [(0, 1), (1, 0)])


def gathered(noisy, laid_out):
    count = lax.axis_size("gz")
    block = noisy
    step = 1
    while step < count:
        pairs = [(i, i ^ step) for i in range(count)]
        other = lax.ppermute(block, "gz", pairs)
        low = lax.axis_index("gz") // step % 2 == 0
        block = jnp.where(
            low, jnp.concatenate([block, other], 0), jnp.concatenate([other, block], 0)
        )
        if step == 1:
            block, laid_out = lax.optimization_barrier((block, laid_out))
        step *= 2
    block = jnp.where(lax.axis_index("gy") == 0, block, jnp.flip(block, 1))
    near = lax.slice_in_dim(block, block.shape[1] - HALO, None, axis=1)
    block = jnp.concatenate([block, swapped(jnp.flip(near, 1), "gy")], 1)
    first = lax.axis_index("gx") == 0
    size = block.shape[2]
    low = lax.slice_in_dim(block, 0, HALO, axis=2)
    high = lax.slice_in_dim(block, size - HALO, size, axis=2)
    other = swapped(jnp.where(first, high, low), "gx")
    blank = jnp.zeros(block.shape[:2] + (1,), block.dtype)
    window = jnp.where(
        first,
        jnp.concatenate([block, other, blank], 2),
        jnp.concatenate([other, block, blank], 2),
    )
    window = window.reshape(window.shape[0], -1)
    return jnp.pad(window, ((0, 0), (0, -window.shape[1] % LANES))), laid_out


def prepare(
    geometry,
    w1_ref,
    b1_ref,
    w2_ref,
    b2_ref,
    head_ref,
    w3_ref,
    b3_ref,
    w4_ref,
    b4_ref,
    thin_lane_ref,
    thin_sub_ref,
    wide_lane_ref,
    keep_ref,
    gather_ref,
    w1_out,
    w2_out,
    w3_out,
    w4_out,
    columns_out,
    band,
):
    deep, depth, channels = geometry
    f32, bf16 = jnp.float32, jnp.bfloat16
    place = lax.axis_index("gz") * depth
    turned = lax.axis_index("gy") == 1

    def dot(left, right):
        return jnp.dot(left, right, preferred_element_type=f32)

    tap_lane, z_lane, part_lane = (thin_lane_ref[i : i + 1, :] for i in range(3))
    a_sub, tap_ahead, tap_turned = (thin_sub_ref[:, i : i + 1] for i in range(3))
    same = tap_lane == jnp.where(turned, tap_turned, tap_ahead)
    crossed = part_lane == 1
    reach = z_lane - a_sub + 1

    def thin_rows(halves, z):
        hit = same & (reach == z)
        high = jnp.where(hit & ~crossed, 1.0, 0.0).astype(bf16)
        low = jnp.where(hit & crossed, 1.0, 0.0).astype(bf16)
        return (dot(halves[0], high) + dot(halves[1], low)).astype(bf16)

    first = split(w1_ref[:, 0, :].T)
    out = 2 * channels
    for z in range(deep):
        w1_out[z * out : (z + 1) * out, :] = thin_rows(first, z)
    grow = split(w3_ref[:, 0, :])
    for i in range(depth + 2):
        z = place + i - 1
        inside = (z >= 0) & (z < deep)
        w3_out[i * channels : (i + 1) * channels, :] = thin_rows(
            grow, jnp.where(inside, z, -deep)
        )

    step = 3 * channels
    part = (depth + 2) * step

    def lay(pieces, w_out):
        out = pieces[0][0].shape[0]
        for b in range(3):
            for i, half in enumerate((0, 0, 1)):
                for z in range(depth):
                    row = (b * depth + z) * out
                    band[row : row + out, pl.ds(i * part + z * step, 3 * step)] = pieces[b][half]
        w_out[...] = band[: w_out.shape[0], :].astype(bf16)

    band[...] = jnp.zeros_like(band)
    tall = w2_ref[...]
    pieces = []
    for b in range(3):
        ahead, back = (
            jnp.concatenate([tall[(a * 3 + k) * step : (a * 3 + k + 1) * step] for a in range(3)], 0)
            for k in (b, 2 - b)
        )
        pieces.append(tuple(h.astype(f32) for h in split(jnp.where(turned, back, ahead).T)))
    lay(pieces, w2_out)

    band[: w4_out.shape[0], :] = jnp.zeros((w4_out.shape[0], 3 * part), f32)
    taps = lax.broadcasted_iota(jnp.int32, (27, wide_lane_ref.shape[1]), 0)
    spread = taps == jnp.where(turned, wide_lane_ref[1:2, :], wide_lane_ref[0:1, :])
    spread = jnp.where(spread, 1.0, 0.0).astype(bf16)
    keep = jnp.concatenate([keep_ref[...]] * channels, 0)
    flats = [
        dot(gather_ref[...], (dot(half, spread) * keep).astype(bf16))
        for half in split(w4_ref[...])
    ]
    lay([[f[:, b * 3 * step : (b + 1) * 3 * step] for f in flats] for b in range(3)], w4_out)

    at_row = lax.broadcasted_iota(jnp.int32, (channels, channels), 0)
    at_lane = lax.broadcasted_iota(jnp.int32, (channels, channels), 1)
    for i, ref in enumerate((b1_ref, b2_ref, head_ref, b3_ref, b4_ref)):
        columns_out[:, i : i + 1] = jnp.sum(
            jnp.where(at_row == at_lane, ref[...], 0.0), axis=1, keepdims=True
        )


def kernel(
    geometry,
    noisy_ref,
    w1_ref,
    w2_ref,
    w3_ref,
    w4_ref,
    columns_ref,
    den_ref,
    seg_ref,
    stage,
    thin,
    pre,
    rows,
    wide_hi,
    wide_lo,
    sums,
):
    deep, depth, channels, pitch, high, span, margin = geometry
    f32 = jnp.float32
    lanes = lax.broadcasted_iota(jnp.int32, (1, span), 1)
    blank = lanes >= high * pitch
    for r in range(high):
        blank = blank | (lanes == (r + 1) * pitch - 1)
    mask = jnp.where(blank, 0.0, 1.0).astype(jnp.float32)
    place = lax.axis_index("gz")
    bias1, bias2, head, bias3, bias4 = (columns_ref[:, i : i + 1] for i in range(5))
    shifts = [(b - 1) * pitch + (c - 1) for b in range(3) for c in range(3)]
    first_span, second_span, third_span = (
        -(-(high - i) * pitch // LANES) * LANES for i in range(1, 4)
    )
    blocks = deep // depth

    def put(field):
        for slot, half in enumerate(split(field)):
            stage[slot, :, pl.ds(margin, field.shape[1])] = half

    def shifted(slot, shift, length):
        return stage[slot, :, pl.ds(margin + shift, length)]

    def thin_columns(field, length):
        put(field)
        for t, s in enumerate(shifts):
            h = shifted(0, s, length)
            thin[t * deep : (t + 1) * deep, :length] = h
            thin[(9 + t) * deep : (10 + t) * deep, :length] = h
            thin[(18 + t) * deep : (19 + t) * deep, :length] = shifted(1, s, length)

    def wide_columns(z, field):
        length = field.shape[1]
        put(field)
        for c in range(3):
            at = (z * 3 + c) * channels
            wide_hi[at : at + channels, :length] = shifted(0, c - 1, length)
            wide_lo[at : at + channels, :length] = shifted(1, c - 1, length)

    taps = (depth + 2) * 3 * channels

    def chunks(length):
        return [(i, min(2 * LANES, length - i)) for i in range(0, length, 2 * LANES)]

    def banded(w_ref, slot, start, chunk):
        at, length = chunk
        h = wide_hi[start : start + taps, at : at + length]
        l = wide_lo[start : start + taps, at : at + length]
        sums[slot, : w_ref.shape[0], pl.ds(margin + at, length)] = jnp.dot(
            w_ref[...], jnp.concatenate([h, l, h], 0), preferred_element_type=f32
        )

    def gate(cand, up, hidden):
        fresh = 1.0 / (1.0 + jnp.exp(-up))
        return hidden + fresh * (jnp.tanh(cand) - hidden)

    stage[...] = jnp.zeros_like(stage)
    aside = jnp.zeros(sums.shape[:2] + (margin,), f32)
    sums[:, :, :margin] = aside
    sums[:, :, sums.shape[2] - margin :] = aside
    edge = 3 * channels
    zeros = jnp.zeros((edge, wide_hi.shape[1]), jnp.bfloat16)
    for wide in (wide_hi, wide_lo):
        wide[:edge, :] = zeros
        wide[(deep + 1) * edge :, :] = zeros

    noisy = noisy_ref[...]
    thin_columns(noisy, first_span)
    pre[...] = jnp.dot(w1_ref[...], thin[:, :first_span], preferred_element_type=f32)

    hidden = jnp.zeros((channels, first_span), f32)
    for z in range(deep):
        at = z * 2 * channels
        hidden = gate(
            pre[at : at + channels, :],
            pre[at + channels : at + 2 * channels, :] + bias1,
            hidden,
        )
        wide_columns(z + 1, hidden * mask[:, :first_span])

    def layer(slot, at, length, lift=0):
        return sum(
            sums[
                slot,
                at + b * depth * lift : at + b * depth * lift + channels,
                pl.ds(margin + (b - 1) * pitch, length),
            ]
            for b in range(3)
        )

    hidden = jnp.zeros((channels, second_span), f32)
    todo = chunks(first_span)
    for chunk in todo:
        banded(w2_ref, (blocks - 1) % 2, (blocks - 1) * depth * edge, chunk)
    for b in range(blocks - 1, -1, -1):
        for zo in range(depth - 1, -1, -1):
            if b > 0:
                turn = depth - 1 - zo
                for chunk in todo[turn::depth]:
                    banded(w2_ref, (b - 1) % 2, (b - 1) * depth * edge, chunk)
            at = zo * 2 * channels
            hidden = gate(
                layer(b % 2, at, second_span, 2 * channels),
                layer(b % 2, at + channels, second_span, 2 * channels) + bias2,
                hidden,
            )
            z = b * depth + zo
            rows[z : z + 1, :second_span] = jnp.sum(hidden * head, axis=0, keepdims=True)

    finished = (noisy[:, :second_span] + rows[:, :second_span]) * mask[:, :second_span]
    rows[:, :second_span] = finished
    thin_columns(finished, third_span)
    grown = jnp.dot(w3_ref[...], thin[:, :third_span], preferred_element_type=f32)
    for i in range(depth + 2):
        z = place * depth + i - 1
        real = jnp.where((z >= 0) & (z < deep), 1.0, 0.0)
        features = jnp.maximum(grown[i * channels : (i + 1) * channels] + bias3, 0.0)
        wide_columns(i, features * (mask[:, :third_span] * real))
    for chunk in chunks(third_span):
        banded(w4_ref, 0, 0, chunk)

    height, width = den_ref.shape[1:]
    for y in range(2):
        for x in range(2):

            @pl.when((lax.axis_index("gy") == y) & (lax.axis_index("gx") == x))
            def _():
                for r in range(height):
                    row = height - 1 - r if y else r
                    at = r * pitch + x * HALO
                    mine = rows[:depth, pl.ds(at, width)]
                    for b in range(1, blocks):
                        other = rows[b * depth : (b + 1) * depth, pl.ds(at, width)]
                        mine = jnp.where(place == b, other, mine)
                    den_ref[:, row, :] = mine
                    for z in range(depth):
                        total = bias4
                        for b in range(3):
                            k = (b * depth + z) * channels
                            lanes = pl.ds(margin + at + (b - 1) * pitch, width)
                            total = total + sums[0, k : k + channels, lanes]
                        seg_ref[:, z, row, :] = total


def local_body(
    noisy,
    first_weight,
    first_bias,
    second_weight,
    second_bias,
    head_weight,
    seg_weight_in,
    seg_bias_in,
    seg_weight_out,
    seg_bias_out,
):
    depth, height, width = noisy.shape
    count = lax.axis_size("gz")
    place = lax.axis_index("gz")
    deep = count * depth
    channels = first_bias.shape[0]
    high, pitch = height + HALO, width + HALO + 1
    span = -(-high * pitch // LANES) * LANES
    margin = -(-(pitch + 1) // LANES) * LANES
    narrow = -(-(high - 1) * pitch // LANES) * LANES

    f32, bf16 = jnp.float32, jnp.bfloat16
    lane = np.arange(27 * deep)
    thin_lane = np.stack(
        [lane // deep % 9, lane % deep, lane // (9 * deep)] + [lane * 0] * 5
    ).astype(np.int32)
    tap = np.arange(27)
    thin_sub = np.stack(
        [tap // 9, tap % 9, (2 - tap // 3 % 3) * 3 + tap % 3], 1
    ).astype(np.int32)
    lane = np.arange(27 * channels)
    b, a, c = lane // channels // 9, lane // channels // 3 % 3, lane // channels % 3
    wide_lane = np.stack(
        [a * 9 + b * 3 + c, a * 9 + (2 - b) * 3 + c] + [lane * 0] * 6
    ).astype(np.int32)
    keep = (np.arange(channels)[:, None] == lane[None] % channels).astype(np.float32)
    lane = np.arange(channels * channels)
    gather = (np.arange(channels)[:, None] == lane[None] // channels).astype(bf16)

    taps = 3 * (depth + 2) * 3 * channels
    in_vmem = pl.BlockSpec(memory_space=pltpu.VMEM)
    prepared = pl.pallas_call(
        functools.partial(prepare, (deep, depth, channels)),
        out_shape=(
            pltpu.VMEM((deep * 2 * channels, 27 * deep), bf16),
            pltpu.VMEM((3 * depth * 2 * channels, taps), bf16),
            pltpu.VMEM(((depth + 2) * channels, 27 * deep), bf16),
            pltpu.VMEM((3 * depth * channels, taps), bf16),
            pltpu.VMEM((channels, LANES), f32),
        ),
        in_specs=[in_vmem] * 14,
        out_specs=(in_vmem,) * 5,
        scratch_shapes=[pltpu.VMEM((3 * depth * 2 * channels, taps), f32)],
        compiler_params=pltpu.CompilerParams(vmem_limit_bytes=16 * 1024 * 1024),
    )
    weights = (
        jnp.transpose(first_weight, (2, 1, 0)),
        first_bias.reshape(1, -1),
        jnp.transpose(second_weight, (2, 1, 0)).reshape(-1, 2 * channels),
        second_bias.reshape(1, -1),
        head_weight.reshape(1, -1),
        seg_weight_in,
        seg_bias_in.reshape(1, -1),
        seg_weight_out.reshape(-1, 27),
        seg_bias_out.reshape(1, -1),
    )
    tables = tuple(jnp.asarray(v) for v in (thin_lane, thin_sub, wide_lane, keep, gather))

    given = [pltpu.with_memory_space_constraint(v, pltpu.HBM) for v in weights + tables]
    flat, laid_out = gathered(noisy, prepared(*given))
    operands = [
        pltpu.with_memory_space_constraint(v, pltpu.VMEM)
        for v in (flat, *laid_out)
    ]
    return pl.pallas_call(
        functools.partial(kernel, (deep, depth, channels, pitch, high, span, margin)),
        out_shape=(
            jax.ShapeDtypeStruct((depth, height, width), f32),
            jax.ShapeDtypeStruct((channels, depth, height, width), f32),
        ),
        in_specs=[in_vmem] * 6,
        out_specs=(in_vmem,) * 2,
        scratch_shapes=[
            pltpu.VMEM((2, channels, span + 2 * margin), bf16),
            pltpu.VMEM((27 * deep, span), bf16),
            pltpu.VMEM((deep * 2 * channels, narrow), f32),
            pltpu.VMEM((deep, span), f32),
            pltpu.VMEM(((deep + 2) * 3 * channels, narrow), bf16),
            pltpu.VMEM(((deep + 2) * 3 * channels, narrow), bf16),
            pltpu.VMEM((2, 3 * depth * 2 * channels, narrow + 2 * margin), f32),
        ],
        compiler_params=pltpu.CompilerParams(vmem_limit_bytes=36 * 1024 * 1024),
    )(*operands)


def solution(mesh):
    in_specs = (P(("win", "gz"), "gy", "gx"), P(), P(), P(), P(), P(), P(), P(), P(), P())
    out_specs = (P(("win", "gz"), "gy", "gx"), P(None, ("win", "gz"), "gy", "gx"))
    shallow = mesh.shape["gz"] in (1, 2, 4) and mesh.shape["gy"] == 2 and mesh.shape["gx"] == 2
    chosen = local_body if shallow else body
    return jax.shard_map(chosen, mesh=mesh, in_specs=in_specs, out_specs=out_specs, check_vma=False)
```

```python
import functools

import jax
import jax.numpy as jnp
import numpy as np
from jax import lax
from jax.experimental import pallas as pl
from jax.experimental.pallas import tpu as pltpu
from jax.sharding import PartitionSpec as P


def shifted(value, axis, steps):
    count = lax.axis_size(axis)
    first, last = (max(0, -steps), min(count, count - steps))
    return lax.ppermute(value, axis, [(source, source + steps) for source in range(first, last)])


def with_halo(block, sides, width):
    for axis, dim in sides:
        count = lax.axis_size(axis)
        forward = [(i, i + 1) for i in range(count - 1)]
        backward = [(target, source) for source, target in forward]
        low = lax.ppermute(
            lax.slice_in_dim(block, block.shape[dim] - width, None, axis=dim), axis, forward
        )
        high = lax.ppermute(lax.slice_in_dim(block, 0, width, axis=dim), axis, backward)
        block = jnp.concatenate([low, block, high], axis=dim)
    return block


def convolve(padded, weight):
    depth = padded.shape[1] - 2
    height = padded.shape[2] - 2
    width = padded.shape[3] - 2
    total = jnp.zeros((weight.shape[0], depth, height, width), jnp.float32)
    for tap in range(27):
        step_z = tap // 9
        step_y = tap // 3 % 3
        step_x = tap % 3
        piece = padded[
            :, step_z : step_z + depth, step_y : step_y + height, step_x : step_x + width
        ]
        total = total + jnp.einsum(
            "oc,czyx->ozyx", weight[:, :, tap], piece, precision=lax.Precision.HIGHEST
        )
    return total


def affine(earlier, later):
    return (earlier[0] * later[0], later[0] * earlier[1] + later[1])


def recurrent(padded, weight, bias, backward):
    channels = bias.shape[0]
    pre = convolve(padded, weight)
    cand = jnp.tanh(pre[:channels])
    keep = jax.nn.sigmoid(-(pre[channels:] + bias[:, None, None, None]))
    inject = (1.0 - keep) * cand
    if backward:
        keep = jnp.flip(keep, 1)
        inject = jnp.flip(inject, 1)
    cum_keep, cum_inject = lax.associative_scan(affine, (keep, inject), axis=1)
    total_keep = cum_keep[:, -1]
    total_inject = cum_inject[:, -1]
    offset = -1 if backward else 1

    def relay(turn, carry):
        return shifted(total_keep * carry + total_inject, "gz", offset)

    carry = lax.fori_loop(0, lax.axis_size("gz") - 1, relay, jnp.zeros_like(total_inject))
    hidden = cum_keep * carry[:, None] + cum_inject
    if backward:
        hidden = jnp.flip(hidden, 1)
    return hidden


def inside_mask(length, where, count):
    places = jnp.arange(length + 2)
    outside = (places == 0) & (where == 0) | (places == length + 1) & (where == count - 1)
    return jnp.where(outside, 0.0, 1.0).astype(jnp.float32)


def body(
    noisy,
    first_weight,
    first_bias,
    second_weight,
    second_bias,
    head_weight,
    seg_weight_in,
    seg_bias_in,
    seg_weight_out,
    seg_bias_out,
):
    noisy_pad = with_halo(noisy[None], (("gz", 1), ("gy", 2), ("gx", 3)), 1)
    first_hidden = recurrent(noisy_pad, first_weight, first_bias, False)
    hidden_pad = with_halo(first_hidden, (("gz", 1), ("gy", 2), ("gx", 3)), 1)
    second_hidden = recurrent(hidden_pad, second_weight, second_bias, True)
    denoised = noisy + jnp.einsum(
        "c,czyx->zyx", head_weight, second_hidden, precision=lax.Precision.HIGHEST
    )
    deep_pad = with_halo(denoised[None], (("gz", 1), ("gy", 2), ("gx", 3)), 2)
    grown = jnp.maximum(convolve(deep_pad, seg_weight_in) + seg_bias_in[:, None, None, None], 0.0)
    mask_z = inside_mask(denoised.shape[0], lax.axis_index("gz"), lax.axis_size("gz"))
    mask_y = inside_mask(denoised.shape[1], lax.axis_index("gy"), lax.axis_size("gy"))
    mask_x = inside_mask(denoised.shape[2], lax.axis_index("gx"), lax.axis_size("gx"))
    feature_pad = (
        grown * (mask_z[:, None, None] * mask_y[None, :, None] * mask_x[None, None, :])[None]
    )
    segmented = convolve(feature_pad, seg_weight_out) + seg_bias_out[:, None, None, None]
    return (denoised, segmented)


HALO = 4
LANES, SUBLANES = 128, 8


def split(value):
    high = value.astype(jnp.bfloat16)
    return high, (value - high.astype(jnp.float32)).astype(jnp.bfloat16)


def swapped(value, axis):
    return lax.ppermute(value, axis, [(0, 1), (1, 0)])


def gathered(noisy, laid_out):
    count = lax.axis_size("gz")
    block = noisy
    step = 1
    while step < count:
        pairs = [(i, i ^ step) for i in range(count)]
        other = lax.ppermute(block, "gz", pairs)
        low = lax.axis_index("gz") // step % 2 == 0
        block = jnp.where(
            low, jnp.concatenate([block, other], 0), jnp.concatenate([other, block], 0)
        )
        if step == 1:
            block, laid_out = lax.optimization_barrier((block, laid_out))
        step *= 2
    block = jnp.where(lax.axis_index("gy") == 0, block, jnp.flip(block, 1))
    near = lax.slice_in_dim(block, block.shape[1] - HALO, None, axis=1)
    block = jnp.concatenate([block, swapped(jnp.flip(near, 1), "gy")], 1)
    first = lax.axis_index("gx") == 0
    size = block.shape[2]
    low = lax.slice_in_dim(block, 0, HALO, axis=2)
    high = lax.slice_in_dim(block, size - HALO, size, axis=2)
    other = swapped(jnp.where(first, high, low), "gx")
    blank = jnp.zeros(block.shape[:2] + (1,), block.dtype)
    window = jnp.where(
        first,
        jnp.concatenate([block, other, blank], 2),
        jnp.concatenate([other, block, blank], 2),
    )
    window = window.reshape(window.shape[0], -1)
    return jnp.pad(window, ((0, 0), (0, -window.shape[1] % LANES))), laid_out


def prepare(
    geometry,
    w1_ref,
    b1_ref,
    w2_ref,
    b2_ref,
    head_ref,
    w3_ref,
    b3_ref,
    w4_ref,
    b4_ref,
    thin_lane_ref,
    thin_sub_ref,
    wide_lane_ref,
    keep_ref,
    gather_ref,
    w1_out,
    w2_out,
    w3_out,
    w4_out,
    columns_out,
    band,
):
    deep, depth, channels = geometry
    f32, bf16 = jnp.float32, jnp.bfloat16
    place = lax.axis_index("gz") * depth
    turned = lax.axis_index("gy") == 1

    def dot(left, right):
        return jnp.dot(left, right, preferred_element_type=f32)

    tap_lane, z_lane, part_lane = (thin_lane_ref[i : i + 1, :] for i in range(3))
    a_sub, tap_ahead, tap_turned = (thin_sub_ref[:, i : i + 1] for i in range(3))
    same = tap_lane == jnp.where(turned, tap_turned, tap_ahead)
    crossed = part_lane == 1
    reach = z_lane - a_sub + 1

    def thin_rows(halves, z):
        hit = same & (reach == z)
        high = jnp.where(hit & ~crossed, 1.0, 0.0).astype(bf16)
        low = jnp.where(hit & crossed, 1.0, 0.0).astype(bf16)
        return (dot(halves[0], high) + dot(halves[1], low)).astype(bf16)

    first = split(w1_ref[:, 0, :].T)
    out = 2 * channels
    for z in range(deep):
        w1_out[z * out : (z + 1) * out, :] = thin_rows(first, z)
    grow = split(w3_ref[:, 0, :])
    for i in range(depth + 2):
        z = place + i - 1
        inside = (z >= 0) & (z < deep)
        w3_out[i * channels : (i + 1) * channels, :] = thin_rows(
            grow, jnp.where(inside, z, -deep)
        )

    step = 3 * channels
    part = (depth + 2) * step

    def lay(pieces, w_out):
        out = pieces[0][0].shape[0]
        for b in range(3):
            for i, half in enumerate((0, 0, 1)):
                for z in range(depth):
                    row = (b * depth + z) * out
                    band[row : row + out, pl.ds(i * part + z * step, 3 * step)] = pieces[b][half]
        w_out[...] = band[: w_out.shape[0], :].astype(bf16)

    band[...] = jnp.zeros_like(band)
    tall = w2_ref[...]
    pieces = []
    for b in range(3):
        ahead, back = (
            jnp.concatenate([tall[(a * 3 + k) * step : (a * 3 + k + 1) * step] for a in range(3)], 0)
            for k in (b, 2 - b)
        )
        pieces.append(tuple(h.astype(f32) for h in split(jnp.where(turned, back, ahead).T)))
    lay(pieces, w2_out)

    band[: w4_out.shape[0], :] = jnp.zeros((w4_out.shape[0], 3 * part), f32)
    taps = lax.broadcasted_iota(jnp.int32, (27, wide_lane_ref.shape[1]), 0)
    spread = taps == jnp.where(turned, wide_lane_ref[1:2, :], wide_lane_ref[0:1, :])
    spread = jnp.where(spread, 1.0, 0.0).astype(bf16)
    keep = jnp.concatenate([keep_ref[...]] * channels, 0)
    flats = [
        dot(gather_ref[...], (dot(half, spread) * keep).astype(bf16))
        for half in split(w4_ref[...])
    ]
    lay([[f[:, b * 3 * step : (b + 1) * 3 * step] for f in flats] for b in range(3)], w4_out)

    at_row = lax.broadcasted_iota(jnp.int32, (channels, channels), 0)
    at_lane = lax.broadcasted_iota(jnp.int32, (channels, channels), 1)
    for i, ref in enumerate((b1_ref, b2_ref, head_ref, b3_ref, b4_ref)):
        columns_out[:, i : i + 1] = jnp.sum(
            jnp.where(at_row == at_lane, ref[...], 0.0), axis=1, keepdims=True
        )


def kernel(
    geometry,
    noisy_ref,
    w1_ref,
    w2_ref,
    w3_ref,
    w4_ref,
    columns_ref,
    den_ref,
    seg_ref,
    stage,
    thin,
    pre,
    rows,
    wide_hi,
    wide_lo,
    sums,
    tiles,
):
    deep, depth, channels, pitch, high, span, margin = geometry
    f32 = jnp.float32
    lanes = lax.broadcasted_iota(jnp.int32, (1, span), 1)
    blank = lanes >= high * pitch
    for r in range(high):
        blank = blank | (lanes == (r + 1) * pitch - 1)
    mask = jnp.where(blank, 0.0, 1.0).astype(jnp.float32)
    place = lax.axis_index("gz")
    bias1, bias2, head, bias3, bias4 = (columns_ref[:, i : i + 1] for i in range(5))
    shifts = [(b - 1) * pitch + (c - 1) for b in range(3) for c in range(3)]
    first_span, second_span, third_span = (
        -(-(high - i) * pitch // LANES) * LANES for i in range(1, 4)
    )
    blocks = deep // depth
    height, width = den_ref.shape[1:]

    def put(field, slot):
        for part, half in enumerate(split(field)):
            stage[2 * slot + part, :, pl.ds(margin, field.shape[1])] = half

    def shifted(part, shift, length, slot=0):
        return stage[2 * slot + part, :, pl.ds(margin + shift, length)]

    def thin_columns(field, length):
        put(field, 0)
        for t, s in enumerate(shifts):
            h = shifted(0, s, length)
            thin[t * deep : (t + 1) * deep, :length] = h
            thin[(9 + t) * deep : (10 + t) * deep, :length] = h
            thin[(18 + t) * deep : (19 + t) * deep, :length] = shifted(1, s, length)

    def wide_columns(z, field):
        length, slot = field.shape[1], z % (depth + 2)
        put(field, slot)
        for c in range(3):
            at = (z * 3 + c) * channels
            wide_hi[at : at + channels, :length] = shifted(0, c - 1, length, slot)
            wide_lo[at : at + channels, :length] = shifted(1, c - 1, length, slot)

    def own_columns(z, offset):
        for c in range(3):
            at = (z * 3 + c) * channels
            for r in range(height + 1):
                lanes = slice(r * width, (r + 1) * width)
                shift = r * pitch + offset + c - 1
                wide_hi[at : at + channels, lanes] = shifted(0, shift, width, z)
                wide_lo[at : at + channels, lanes] = shifted(1, shift, width, z)

    taps = (depth + 2) * 3 * channels

    def chunks(length):
        return [(i, min(2 * LANES, length - i)) for i in range(0, length, 2 * LANES)]

    def banded(w_ref, slot, start, chunk):
        at, length = chunk
        h = wide_hi[start : start + taps, at : at + length]
        l = wide_lo[start : start + taps, at : at + length]
        sums[slot, : w_ref.shape[0], pl.ds(margin + at, length)] = jnp.dot(
            w_ref[...], jnp.concatenate([h, l, h], 0), preferred_element_type=f32
        )

    def gate(cand, up, hidden):
        fresh = 1.0 / (1.0 + jnp.exp(-up))
        return hidden + fresh * (jnp.tanh(cand) - hidden)

    stage[...] = jnp.zeros_like(stage)
    aside = jnp.zeros(sums.shape[:2] + (margin,), f32)
    sums[:, :, :margin] = aside
    sums[:, :, sums.shape[2] - margin :] = aside
    edge = 3 * channels
    zeros = jnp.zeros((edge, wide_hi.shape[1]), jnp.bfloat16)
    for wide in (wide_hi, wide_lo):
        wide[:edge, :] = zeros
        wide[(deep + 1) * edge :, :] = zeros

    noisy = noisy_ref[...]
    thin_columns(noisy, first_span)
    pre[...] = jnp.dot(w1_ref[...], thin[:, :first_span], preferred_element_type=f32)

    hidden = jnp.zeros((channels, first_span), f32)
    for z in range(deep):
        at = z * 2 * channels
        hidden = gate(
            pre[at : at + channels, :],
            pre[at + channels : at + 2 * channels, :] + bias1,
            hidden,
        )
        wide_columns(z + 1, hidden * mask[:, :first_span])

    def layer(slot, at, length, lift=0):
        return sum(
            sums[
                slot,
                at + b * depth * lift : at + b * depth * lift + channels,
                pl.ds(margin + (b - 1) * pitch, length),
            ]
            for b in range(3)
        )

    hidden = jnp.zeros((channels, second_span), f32)
    todo = chunks(first_span)
    for chunk in todo:
        banded(w2_ref, (blocks - 1) % 2, (blocks - 1) * depth * edge, chunk)
    for b in range(blocks - 1, -1, -1):
        for zo in range(depth - 1, -1, -1):
            if b > 0:
                turn = depth - 1 - zo
                for chunk in todo[turn::depth]:
                    banded(w2_ref, (b - 1) % 2, (b - 1) * depth * edge, chunk)
            at = zo * 2 * channels
            hidden = gate(
                layer(b % 2, at, second_span, 2 * channels),
                layer(b % 2, at + channels, second_span, 2 * channels) + bias2,
                hidden,
            )
            z = b * depth + zo
            rows[z : z + 1, :second_span] = jnp.sum(hidden * head, axis=0, keepdims=True)

    finished = (noisy[:, :second_span] + rows[:, :second_span]) * mask[:, :second_span]
    rows[:, :second_span] = finished
    thin_columns(finished, third_span)
    grown = jnp.dot(w3_ref[...], thin[:, :third_span], preferred_element_type=f32)
    for i in range(depth + 2):
        z = place * depth + i - 1
        real = jnp.where((z >= 0) & (z < deep), 1.0, 0.0)
        features = jnp.maximum(grown[i * channels : (i + 1) * channels] + bias3, 0.0)
        put(features * (mask[:, :third_span] * real), i)

    turned = lax.axis_index("gy") == 1

    def at_row(r):
        return jnp.where(turned, height - 1 - r, r)

    for x in range(2):

        @pl.when(lax.axis_index("gx") == x)
        def _():
            for i in range(depth + 2):
                own_columns(i, x * HALO)
            for r in range(height):
                lanes = pl.ds(r * pitch + x * HALO, width)
                mine = rows[:depth, lanes]
                for b in range(1, deep // depth):
                    mine = jnp.where(place == b, rows[b * depth : (b + 1) * depth, lanes], mine)
                at = pl.multiple_of(at_row(r) * SUBLANES, SUBLANES)
                tiles[pl.ds(at, depth), :] = mine

    for z in range(depth):
        den_ref[z] = tiles[pl.ds(z, height, stride=SUBLANES), :]
    for chunk in chunks((height + 1) * width):
        banded(w4_ref, 0, 0, chunk)
    for z in range(depth):
        for r in range(height):
            total = bias4
            for b in range(3):
                if r + b > 0:
                    k = (b * depth + z) * channels
                    lanes = pl.ds(margin + (r + b - 1) * width, width)
                    total = total + sums[0, k : k + channels, lanes]
            at = pl.multiple_of((z * height + at_row(r)) * channels, channels)
            tiles[pl.ds(at, channels), :] = total
    for z in range(depth):
        for o in range(channels):
            seg_ref[o, z] = tiles[pl.ds(z * height * channels + o, height, stride=channels), :]


def local_body(
    noisy,
    first_weight,
    first_bias,
    second_weight,
    second_bias,
    head_weight,
    seg_weight_in,
    seg_bias_in,
    seg_weight_out,
    seg_bias_out,
):
    depth, height, width = noisy.shape
    count = lax.axis_size("gz")
    place = lax.axis_index("gz")
    deep = count * depth
    channels = first_bias.shape[0]
    high, pitch = height + HALO, width + HALO + 1
    span = -(-high * pitch // LANES) * LANES
    margin = -(-(pitch + 1) // LANES) * LANES
    narrow = -(-(high - 1) * pitch // LANES) * LANES

    f32, bf16 = jnp.float32, jnp.bfloat16
    lane = np.arange(27 * deep)
    thin_lane = np.stack(
        [lane // deep % 9, lane % deep, lane // (9 * deep)] + [lane * 0] * 5
    ).astype(np.int32)
    tap = np.arange(27)
    thin_sub = np.stack(
        [tap // 9, tap % 9, (2 - tap // 3 % 3) * 3 + tap % 3], 1
    ).astype(np.int32)
    lane = np.arange(27 * channels)
    b, a, c = lane // channels // 9, lane // channels // 3 % 3, lane // channels % 3
    wide_lane = np.stack(
        [a * 9 + b * 3 + c, a * 9 + (2 - b) * 3 + c] + [lane * 0] * 6
    ).astype(np.int32)
    keep = (np.arange(channels)[:, None] == lane[None] % channels).astype(np.float32)
    lane = np.arange(channels * channels)
    gather = (np.arange(channels)[:, None] == lane[None] // channels).astype(bf16)

    taps = 3 * (depth + 2) * 3 * channels
    in_vmem = pl.BlockSpec(memory_space=pltpu.VMEM)
    prepared = pl.pallas_call(
        functools.partial(prepare, (deep, depth, channels)),
        out_shape=(
            pltpu.VMEM((deep * 2 * channels, 27 * deep), bf16),
            pltpu.VMEM((3 * depth * 2 * channels, taps), bf16),
            pltpu.VMEM(((depth + 2) * channels, 27 * deep), bf16),
            pltpu.VMEM((3 * depth * channels, taps), bf16),
            pltpu.VMEM((channels, LANES), f32),
        ),
        in_specs=[in_vmem] * 14,
        out_specs=(in_vmem,) * 5,
        scratch_shapes=[pltpu.VMEM((3 * depth * 2 * channels, taps), f32)],
        compiler_params=pltpu.CompilerParams(vmem_limit_bytes=16 * 1024 * 1024),
    )
    weights = (
        jnp.transpose(first_weight, (2, 1, 0)),
        first_bias.reshape(1, -1),
        jnp.transpose(second_weight, (2, 1, 0)).reshape(-1, 2 * channels),
        second_bias.reshape(1, -1),
        head_weight.reshape(1, -1),
        seg_weight_in,
        seg_bias_in.reshape(1, -1),
        seg_weight_out.reshape(-1, 27),
        seg_bias_out.reshape(1, -1),
    )
    tables = tuple(jnp.asarray(v) for v in (thin_lane, thin_sub, wide_lane, keep, gather))

    given = [pltpu.with_memory_space_constraint(v, pltpu.HBM) for v in weights + tables]
    flat, laid_out = gathered(noisy, prepared(*given))
    operands = [
        pltpu.with_memory_space_constraint(v, pltpu.VMEM)
        for v in (flat, *laid_out)
    ]
    return pl.pallas_call(
        functools.partial(kernel, (deep, depth, channels, pitch, high, span, margin)),
        out_shape=(
            jax.ShapeDtypeStruct((depth, height, width), f32),
            jax.ShapeDtypeStruct((channels, depth, height, width), f32),
        ),
        in_specs=[in_vmem] * 6,
        out_specs=(in_vmem,) * 2,
        scratch_shapes=[
            pltpu.VMEM((2 * (depth + 2), channels, span + 2 * margin), bf16),
            pltpu.VMEM((27 * deep, span), bf16),
            pltpu.VMEM((deep * 2 * channels, narrow), f32),
            pltpu.VMEM((deep, span), f32),
            pltpu.VMEM(((deep + 2) * 3 * channels, narrow), bf16),
            pltpu.VMEM(((deep + 2) * 3 * channels, narrow), bf16),
            pltpu.VMEM((2, 3 * depth * 2 * channels, narrow + 2 * margin), f32),
            pltpu.VMEM((depth * height * channels, width), f32),
        ],
        compiler_params=pltpu.CompilerParams(vmem_limit_bytes=36 * 1024 * 1024),
    )(*operands)


def solution(mesh):
    in_specs = (P(("win", "gz"), "gy", "gx"), P(), P(), P(), P(), P(), P(), P(), P(), P())
    out_specs = (P(("win", "gz"), "gy", "gx"), P(None, ("win", "gz"), "gy", "gx"))
    shallow = mesh.shape["gz"] in (1, 2, 4) and mesh.shape["gy"] == 2 and mesh.shape["gx"] == 2
    chosen = local_body if shallow else body
    return jax.shard_map(chosen, mesh=mesh, in_specs=in_specs, out_specs=out_specs, check_vma=False)
```

```python
import functools

import jax
import jax.numpy as jnp
import numpy as np
from jax import lax
from jax.experimental import pallas as pl
from jax.experimental.pallas import tpu as pltpu
from jax.sharding import PartitionSpec as P


def shifted(value, axis, steps):
    count = lax.axis_size(axis)
    first, last = (max(0, -steps), min(count, count - steps))
    return lax.ppermute(value, axis, [(source, source + steps) for source in range(first, last)])


def with_halo(block, sides, width):
    for axis, dim in sides:
        count = lax.axis_size(axis)
        forward = [(i, i + 1) for i in range(count - 1)]
        backward = [(target, source) for source, target in forward]
        low = lax.ppermute(
            lax.slice_in_dim(block, block.shape[dim] - width, None, axis=dim), axis, forward
        )
        high = lax.ppermute(lax.slice_in_dim(block, 0, width, axis=dim), axis, backward)
        block = jnp.concatenate([low, block, high], axis=dim)
    return block


def convolve(padded, weight):
    depth = padded.shape[1] - 2
    height = padded.shape[2] - 2
    width = padded.shape[3] - 2
    total = jnp.zeros((weight.shape[0], depth, height, width), jnp.float32)
    for tap in range(27):
        step_z = tap // 9
        step_y = tap // 3 % 3
        step_x = tap % 3
        piece = padded[
            :, step_z : step_z + depth, step_y : step_y + height, step_x : step_x + width
        ]
        total = total + jnp.einsum(
            "oc,czyx->ozyx", weight[:, :, tap], piece, precision=lax.Precision.HIGHEST
        )
    return total


def affine(earlier, later):
    return (earlier[0] * later[0], later[0] * earlier[1] + later[1])


def recurrent(padded, weight, bias, backward):
    channels = bias.shape[0]
    pre = convolve(padded, weight)
    cand = jnp.tanh(pre[:channels])
    keep = jax.nn.sigmoid(-(pre[channels:] + bias[:, None, None, None]))
    inject = (1.0 - keep) * cand
    if backward:
        keep = jnp.flip(keep, 1)
        inject = jnp.flip(inject, 1)
    cum_keep, cum_inject = lax.associative_scan(affine, (keep, inject), axis=1)
    total_keep = cum_keep[:, -1]
    total_inject = cum_inject[:, -1]
    offset = -1 if backward else 1

    def relay(turn, carry):
        return shifted(total_keep * carry + total_inject, "gz", offset)

    carry = lax.fori_loop(0, lax.axis_size("gz") - 1, relay, jnp.zeros_like(total_inject))
    hidden = cum_keep * carry[:, None] + cum_inject
    if backward:
        hidden = jnp.flip(hidden, 1)
    return hidden


def inside_mask(length, where, count):
    places = jnp.arange(length + 2)
    outside = (places == 0) & (where == 0) | (places == length + 1) & (where == count - 1)
    return jnp.where(outside, 0.0, 1.0).astype(jnp.float32)


def body(
    noisy,
    first_weight,
    first_bias,
    second_weight,
    second_bias,
    head_weight,
    seg_weight_in,
    seg_bias_in,
    seg_weight_out,
    seg_bias_out,
):
    noisy_pad = with_halo(noisy[None], (("gz", 1), ("gy", 2), ("gx", 3)), 1)
    first_hidden = recurrent(noisy_pad, first_weight, first_bias, False)
    hidden_pad = with_halo(first_hidden, (("gz", 1), ("gy", 2), ("gx", 3)), 1)
    second_hidden = recurrent(hidden_pad, second_weight, second_bias, True)
    denoised = noisy + jnp.einsum(
        "c,czyx->zyx", head_weight, second_hidden, precision=lax.Precision.HIGHEST
    )
    deep_pad = with_halo(denoised[None], (("gz", 1), ("gy", 2), ("gx", 3)), 2)
    grown = jnp.maximum(convolve(deep_pad, seg_weight_in) + seg_bias_in[:, None, None, None], 0.0)
    mask_z = inside_mask(denoised.shape[0], lax.axis_index("gz"), lax.axis_size("gz"))
    mask_y = inside_mask(denoised.shape[1], lax.axis_index("gy"), lax.axis_size("gy"))
    mask_x = inside_mask(denoised.shape[2], lax.axis_index("gx"), lax.axis_size("gx"))
    feature_pad = (
        grown * (mask_z[:, None, None] * mask_y[None, :, None] * mask_x[None, None, :])[None]
    )
    segmented = convolve(feature_pad, seg_weight_out) + seg_bias_out[:, None, None, None]
    return (denoised, segmented)


HALO = 4
AHEAD, PACE = 8, 4
LANES, SUBLANES = 128, 8


def split(value):
    high = value.astype(jnp.bfloat16)
    return high, (value - high.astype(jnp.float32)).astype(jnp.bfloat16)


def swapped(value, axis):
    return lax.ppermute(value, axis, [(0, 1), (1, 0)])


def gathered(noisy, laid_out):
    count = lax.axis_size("gz")
    block = noisy
    step = 1
    while step < count:
        pairs = [(i, i ^ step) for i in range(count)]
        other = lax.ppermute(block, "gz", pairs)
        low = lax.axis_index("gz") // step % 2 == 0
        block = jnp.where(
            low, jnp.concatenate([block, other], 0), jnp.concatenate([other, block], 0)
        )
        if step == 1:
            block, laid_out = lax.optimization_barrier((block, laid_out))
        step *= 2
    block = jnp.where(lax.axis_index("gy") == 0, block, jnp.flip(block, 1))
    near = lax.slice_in_dim(block, block.shape[1] - HALO, None, axis=1)
    block = jnp.concatenate([block, swapped(jnp.flip(near, 1), "gy")], 1)
    first = lax.axis_index("gx") == 0
    size = block.shape[2]
    low = lax.slice_in_dim(block, 0, HALO, axis=2)
    high = lax.slice_in_dim(block, size - HALO, size, axis=2)
    other = swapped(jnp.where(first, high, low), "gx")
    blank = jnp.zeros(block.shape[:2] + (1,), block.dtype)
    window = jnp.where(
        first,
        jnp.concatenate([block, other, blank], 2),
        jnp.concatenate([other, block, blank], 2),
    )
    window = window.reshape(window.shape[0], -1)
    return jnp.pad(window, ((0, 0), (0, -window.shape[1] % LANES))), laid_out


def prepare(
    geometry,
    w1_ref,
    b1_ref,
    w2_ref,
    b2_ref,
    head_ref,
    w3_ref,
    b3_ref,
    w4_ref,
    b4_ref,
    thin_lane_ref,
    thin_sub_ref,
    wide_lane_ref,
    keep_ref,
    gather_ref,
    w1_out,
    w2_out,
    w3_out,
    w4_out,
    columns_out,
    band,
):
    deep, depth, channels = geometry
    f32, bf16 = jnp.float32, jnp.bfloat16
    place = lax.axis_index("gz") * depth
    turned = lax.axis_index("gy") == 1

    def dot(left, right):
        return jnp.dot(left, right, preferred_element_type=f32)

    tap_lane, z_lane, part_lane = (thin_lane_ref[i : i + 1, :] for i in range(3))
    a_sub, tap_ahead, tap_turned = (thin_sub_ref[:, i : i + 1] for i in range(3))
    same = tap_lane == jnp.where(turned, tap_turned, tap_ahead)
    crossed = part_lane == 1
    reach = z_lane - a_sub + 1

    def thin_rows(halves, z):
        hit = same & (reach == z)
        high = jnp.where(hit & ~crossed, 1.0, 0.0).astype(bf16)
        low = jnp.where(hit & crossed, 1.0, 0.0).astype(bf16)
        return (dot(halves[0], high) + dot(halves[1], low)).astype(bf16)

    first = split(w1_ref[:, 0, :].T)
    out = 2 * channels
    for z in range(deep):
        w1_out[z * out : (z + 1) * out, :] = thin_rows(first, z)
    grow = split(w3_ref[:, 0, :])
    for i in range(depth + 2):
        z = place + i - 1
        inside = (z >= 0) & (z < deep)
        w3_out[i * channels : (i + 1) * channels, :] = thin_rows(
            grow, jnp.where(inside, z, -deep)
        )

    step = 3 * channels

    def lay(pieces, w_out):
        out = pieces[0][0].shape[0]
        for b in range(3):
            for i, half in enumerate((0, 0, 1)):
                band[b * out : (b + 1) * out, pl.ds(i * 3 * step, 3 * step)] = pieces[b][half]
        w_out[...] = band[: w_out.shape[0], :].astype(bf16)

    tall = w2_ref[...]
    pieces = []
    for b in range(3):
        ahead, back = (
            jnp.concatenate([tall[(a * 3 + k) * step : (a * 3 + k + 1) * step] for a in range(3)], 0)
            for k in (b, 2 - b)
        )
        pieces.append(tuple(h.astype(f32) for h in split(jnp.where(turned, back, ahead).T)))
    lay(pieces, w2_out)

    taps = lax.broadcasted_iota(jnp.int32, (27, wide_lane_ref.shape[1]), 0)
    spread = taps == jnp.where(turned, wide_lane_ref[1:2, :], wide_lane_ref[0:1, :])
    spread = jnp.where(spread, 1.0, 0.0).astype(bf16)
    keep = jnp.concatenate([keep_ref[...]] * channels, 0)
    flats = [
        dot(gather_ref[...], (dot(half, spread) * keep).astype(bf16))
        for half in split(w4_ref[...])
    ]
    lay([[f[:, b * 3 * step : (b + 1) * 3 * step] for f in flats] for b in range(3)], w4_out)

    at_row = lax.broadcasted_iota(jnp.int32, (channels, channels), 0)
    at_lane = lax.broadcasted_iota(jnp.int32, (channels, channels), 1)
    for i, ref in enumerate((b1_ref, b2_ref, head_ref, b3_ref, b4_ref)):
        columns_out[:, i : i + 1] = jnp.sum(
            jnp.where(at_row == at_lane, ref[...], 0.0), axis=1, keepdims=True
        )


def kernel(
    geometry,
    noisy_ref,
    w1_ref,
    w2_ref,
    w3_ref,
    w4_ref,
    columns_ref,
    den_ref,
    seg_ref,
    stage,
    thin,
    pre,
    rows,
    wide_hi,
    wide_lo,
    sums,
    tiles,
):
    deep, depth, channels, pitch, high, span, margin = geometry
    f32 = jnp.float32
    lanes = lax.broadcasted_iota(jnp.int32, (1, span), 1)
    blank = lanes >= high * pitch
    for r in range(high):
        blank = blank | (lanes == (r + 1) * pitch - 1)
    mask = jnp.where(blank, 0.0, 1.0).astype(jnp.float32)
    place = lax.axis_index("gz")
    bias1, bias2, head, bias3, bias4 = (columns_ref[:, i : i + 1] for i in range(5))
    shifts = [(b - 1) * pitch + (c - 1) for b in range(3) for c in range(3)]
    first_span, second_span, third_span = (
        -(-(high - i) * pitch // LANES) * LANES for i in range(1, 4)
    )
    height, width = den_ref.shape[1:]

    edge = 3 * channels

    def put(field, slot):
        for part, half in enumerate(split(field)):
            stage[2 * slot + part, :, pl.ds(margin, field.shape[1])] = half

    def shifted(part, shift, length, slot=0):
        return stage[2 * slot + part, :, pl.ds(margin + shift, length)]

    def thin_columns(field, length):
        put(field, 0)
        for t, s in enumerate(shifts):
            h = shifted(0, s, length)
            thin[t * deep : (t + 1) * deep, :length] = h
            thin[(9 + t) * deep : (10 + t) * deep, :length] = h
            thin[(18 + t) * deep : (19 + t) * deep, :length] = shifted(1, s, length)

    def wide_columns(z, field):
        length, slot = field.shape[1], z % (depth + 2)
        put(field, slot)
        for c in range(3):
            at = (z * 3 + c) * channels
            wide_hi[at : at + channels, :length] = shifted(0, c - 1, length, slot)
            wide_lo[at : at + channels, :length] = shifted(1, c - 1, length, slot)

    def own_columns(z, offset):
        for c in range(3):
            at = (z * 3 + c) * channels
            for r in range(height + 1):
                lanes = slice(r * width, (r + 1) * width)
                shift = r * pitch + offset + c - 1
                wide_hi[at : at + channels, lanes] = shifted(0, shift, width, z)
                wide_lo[at : at + channels, lanes] = shifted(1, shift, width, z)

    def chunks(length):
        return [(i, min(2 * LANES, length - i)) for i in range(0, length, 2 * LANES)]

    def convolve(w_ref, z, chunk):
        at, length = chunk
        taps = slice(z * edge, (z + 3) * edge)
        h = wide_hi[taps, at : at + length]
        l = wide_lo[taps, at : at + length]
        sums[z, : w_ref.shape[0], pl.ds(margin + at, length)] = jnp.dot(
            w_ref[...], jnp.concatenate([h, l, h], 0), preferred_element_type=f32
        )

    def gate(cand, up, hidden):
        fresh = 1.0 / (1.0 + jnp.exp(-up))
        return hidden + fresh * (jnp.tanh(cand) - hidden)

    stage[...] = jnp.zeros_like(stage)
    before = jnp.zeros((deep, 2 * channels, margin), f32)
    sums[:, : 2 * channels, :margin] = before
    sums[:, 4 * channels :, margin + first_span :] = before
    zeros = jnp.zeros((edge, wide_hi.shape[1]), jnp.bfloat16)
    for wide in (wide_hi, wide_lo):
        wide[:edge, :] = zeros
        wide[(deep + 1) * edge :, :] = zeros

    noisy = noisy_ref[...]
    thin_columns(noisy, first_span)
    todo = chunks(first_span)
    part = depth * 2 * channels

    def thin_block(b, chunk):
        at, length = chunk
        pre[b * part : (b + 1) * part, at : at + length] = jnp.dot(
            w1_ref[b * part : (b + 1) * part, :],
            thin[:, at : at + length],
            preferred_element_type=f32,
        )

    for chunk in todo:
        thin_block(0, chunk)
    waiting = []
    hidden = jnp.zeros((channels, first_span), f32)
    for z in range(deep):
        at = z * 2 * channels
        hidden = gate(
            pre[at : at + channels, :],
            pre[at + channels : at + 2 * channels, :] + bias1,
            hidden,
        )
        wide_columns(z + 1, hidden * mask[:, :first_span])
        if z // depth + 1 < deep // depth:
            for chunk in todo[z % depth :: depth]:
                thin_block(z // depth + 1, chunk)
        if 0 < z <= AHEAD:
            waiting += [(z - 1, chunk) for chunk in todo]
        for _ in range(min(PACE, len(waiting))):
            convolve(w2_ref, *waiting.pop(0))

    def layer(z, at):
        return sum(
            sums[
                z,
                at + b * 2 * channels : at + (b * 2 + 1) * channels,
                pl.ds(margin + (b - 1) * pitch, second_span),
            ]
            for b in range(3)
        )

    later = [(z, chunk) for z in range(deep - 1, AHEAD - 1, -1) for chunk in todo] + waiting
    for _ in range(min(2 * len(todo), len(later))):
        convolve(w2_ref, *later.pop(0))
    hidden = jnp.zeros((channels, second_span), f32)
    for z in range(deep - 1, -1, -1):
        for _ in range(min(len(todo), len(later))):
            convolve(w2_ref, *later.pop(0))
        hidden = gate(layer(z, 0), layer(z, channels) + bias2, hidden)
        rows[z : z + 1, :second_span] = jnp.sum(hidden * head, axis=0, keepdims=True)

    finished = (noisy[:, :second_span] + rows[:, :second_span]) * mask[:, :second_span]
    rows[:, :second_span] = finished
    thin_columns(finished, third_span)
    grown = jnp.dot(w3_ref[...], thin[:, :third_span], preferred_element_type=f32)
    for i in range(depth + 2):
        z = place * depth + i - 1
        real = jnp.where((z >= 0) & (z < deep), 1.0, 0.0)
        features = jnp.maximum(grown[i * channels : (i + 1) * channels] + bias3, 0.0)
        put(features * (mask[:, :third_span] * real), i)

    turned = lax.axis_index("gy") == 1

    def at_row(r):
        return jnp.where(turned, height - 1 - r, r)

    for x in range(2):

        @pl.when(lax.axis_index("gx") == x)
        def _():
            for i in range(depth + 2):
                own_columns(i, x * HALO)
            for r in range(height):
                lanes = pl.ds(r * pitch + x * HALO, width)
                mine = rows[:depth, lanes]
                for b in range(1, deep // depth):
                    mine = jnp.where(place == b, rows[b * depth : (b + 1) * depth, lanes], mine)
                at = pl.multiple_of(at_row(r) * SUBLANES, SUBLANES)
                tiles[pl.ds(at, depth), :] = mine

    for z in range(depth):
        den_ref[z] = tiles[pl.ds(z, height, stride=SUBLANES), :]
    for z in range(depth):
        for chunk in chunks((height + 1) * width):
            convolve(w4_ref, z, chunk)
    for z in range(depth):
        for r in range(height):
            total = bias4
            for b in range(3):
                if r + b > 0:
                    lanes = pl.ds(margin + (r + b - 1) * width, width)
                    total = total + sums[z, b * channels : (b + 1) * channels, lanes]
            at = pl.multiple_of((z * height + at_row(r)) * channels, channels)
            tiles[pl.ds(at, channels), :] = total
    for z in range(depth):
        for o in range(channels):
            seg_ref[o, z] = tiles[pl.ds(z * height * channels + o, height, stride=channels), :]


def local_body(
    noisy,
    first_weight,
    first_bias,
    second_weight,
    second_bias,
    head_weight,
    seg_weight_in,
    seg_bias_in,
    seg_weight_out,
    seg_bias_out,
):
    depth, height, width = noisy.shape
    count = lax.axis_size("gz")
    place = lax.axis_index("gz")
    deep = count * depth
    channels = first_bias.shape[0]
    high, pitch = height + HALO, width + HALO + 1
    span = -(-high * pitch // LANES) * LANES
    margin = -(-(pitch + 1) // LANES) * LANES
    narrow = -(-(high - 1) * pitch // LANES) * LANES

    f32, bf16 = jnp.float32, jnp.bfloat16
    lane = np.arange(27 * deep)
    thin_lane = np.stack(
        [lane // deep % 9, lane % deep, lane // (9 * deep)] + [lane * 0] * 5
    ).astype(np.int32)
    tap = np.arange(27)
    thin_sub = np.stack(
        [tap // 9, tap % 9, (2 - tap // 3 % 3) * 3 + tap % 3], 1
    ).astype(np.int32)
    lane = np.arange(27 * channels)
    b, a, c = lane // channels // 9, lane // channels // 3 % 3, lane // channels % 3
    wide_lane = np.stack(
        [a * 9 + b * 3 + c, a * 9 + (2 - b) * 3 + c] + [lane * 0] * 6
    ).astype(np.int32)
    keep = (np.arange(channels)[:, None] == lane[None] % channels).astype(np.float32)
    lane = np.arange(channels * channels)
    gather = (np.arange(channels)[:, None] == lane[None] // channels).astype(bf16)

    taps = 3 * 9 * channels
    in_vmem = pl.BlockSpec(memory_space=pltpu.VMEM)
    prepared = pl.pallas_call(
        functools.partial(prepare, (deep, depth, channels)),
        out_shape=(
            pltpu.VMEM((deep * 2 * channels, 27 * deep), bf16),
            pltpu.VMEM((3 * 2 * channels, taps), bf16),
            pltpu.VMEM(((depth + 2) * channels, 27 * deep), bf16),
            pltpu.VMEM((3 * channels, taps), bf16),
            pltpu.VMEM((channels, LANES), f32),
        ),
        in_specs=[in_vmem] * 14,
        out_specs=(in_vmem,) * 5,
        scratch_shapes=[pltpu.VMEM((3 * 2 * channels, taps), f32)],
        compiler_params=pltpu.CompilerParams(vmem_limit_bytes=16 * 1024 * 1024),
    )
    weights = (
        jnp.transpose(first_weight, (2, 1, 0)),
        first_bias.reshape(1, -1),
        jnp.transpose(second_weight, (2, 1, 0)).reshape(-1, 2 * channels),
        second_bias.reshape(1, -1),
        head_weight.reshape(1, -1),
        seg_weight_in,
        seg_bias_in.reshape(1, -1),
        seg_weight_out.reshape(-1, 27),
        seg_bias_out.reshape(1, -1),
    )
    tables = tuple(jnp.asarray(v) for v in (thin_lane, thin_sub, wide_lane, keep, gather))

    given = [pltpu.with_memory_space_constraint(v, pltpu.HBM) for v in weights + tables]
    flat, laid_out = gathered(noisy, prepared(*given))
    operands = [
        pltpu.with_memory_space_constraint(v, pltpu.VMEM)
        for v in (flat, *laid_out)
    ]
    return pl.pallas_call(
        functools.partial(kernel, (deep, depth, channels, pitch, high, span, margin)),
        out_shape=(
            jax.ShapeDtypeStruct((depth, height, width), f32),
            jax.ShapeDtypeStruct((channels, depth, height, width), f32),
        ),
        in_specs=[in_vmem] * 6,
        out_specs=(in_vmem,) * 2,
        scratch_shapes=[
            pltpu.VMEM((2 * (depth + 2), channels, span + 2 * margin), bf16),
            pltpu.VMEM((27 * deep, span), bf16),
            pltpu.VMEM((deep * 2 * channels, narrow), f32),
            pltpu.VMEM((deep, span), f32),
            pltpu.VMEM(((deep + 2) * 3 * channels, narrow), bf16),
            pltpu.VMEM(((deep + 2) * 3 * channels, narrow), bf16),
            pltpu.VMEM((deep, 3 * 2 * channels, narrow + 2 * margin), f32),
            pltpu.VMEM((depth * height * channels, width), f32),
        ],
        compiler_params=pltpu.CompilerParams(vmem_limit_bytes=36 * 1024 * 1024),
    )(*operands)


def solution(mesh):
    in_specs = (P(("win", "gz"), "gy", "gx"), P(), P(), P(), P(), P(), P(), P(), P(), P())
    out_specs = (P(("win", "gz"), "gy", "gx"), P(None, ("win", "gz"), "gy", "gx"))
    shallow = mesh.shape["gz"] in (1, 2, 4) and mesh.shape["gy"] == 2 and mesh.shape["gx"] == 2
    chosen = local_body if shallow else body
    return jax.shard_map(chosen, mesh=mesh, in_specs=in_specs, out_specs=out_specs, check_vma=False)
```

```python
import functools

import jax
import jax.numpy as jnp
import numpy as np
from jax import lax
from jax.experimental import pallas as pl
from jax.experimental.pallas import tpu as pltpu
from jax.sharding import PartitionSpec as P


def shifted(value, axis, steps):
    count = lax.axis_size(axis)
    first, last = (max(0, -steps), min(count, count - steps))
    return lax.ppermute(value, axis, [(source, source + steps) for source in range(first, last)])


def with_halo(block, sides, width):
    for axis, dim in sides:
        count = lax.axis_size(axis)
        forward = [(i, i + 1) for i in range(count - 1)]
        backward = [(target, source) for source, target in forward]
        low = lax.ppermute(
            lax.slice_in_dim(block, block.shape[dim] - width, None, axis=dim), axis, forward
        )
        high = lax.ppermute(lax.slice_in_dim(block, 0, width, axis=dim), axis, backward)
        block = jnp.concatenate([low, block, high], axis=dim)
    return block


def convolve(padded, weight):
    depth = padded.shape[1] - 2
    height = padded.shape[2] - 2
    width = padded.shape[3] - 2
    total = jnp.zeros((weight.shape[0], depth, height, width), jnp.float32)
    for tap in range(27):
        step_z = tap // 9
        step_y = tap // 3 % 3
        step_x = tap % 3
        piece = padded[
            :, step_z : step_z + depth, step_y : step_y + height, step_x : step_x + width
        ]
        total = total + jnp.einsum(
            "oc,czyx->ozyx", weight[:, :, tap], piece, precision=lax.Precision.HIGHEST
        )
    return total


def affine(earlier, later):
    return (earlier[0] * later[0], later[0] * earlier[1] + later[1])


def recurrent(padded, weight, bias, backward):
    channels = bias.shape[0]
    pre = convolve(padded, weight)
    cand = jnp.tanh(pre[:channels])
    keep = jax.nn.sigmoid(-(pre[channels:] + bias[:, None, None, None]))
    inject = (1.0 - keep) * cand
    if backward:
        keep = jnp.flip(keep, 1)
        inject = jnp.flip(inject, 1)
    cum_keep, cum_inject = lax.associative_scan(affine, (keep, inject), axis=1)
    total_keep = cum_keep[:, -1]
    total_inject = cum_inject[:, -1]
    offset = -1 if backward else 1

    def relay(turn, carry):
        return shifted(total_keep * carry + total_inject, "gz", offset)

    carry = lax.fori_loop(0, lax.axis_size("gz") - 1, relay, jnp.zeros_like(total_inject))
    hidden = cum_keep * carry[:, None] + cum_inject
    if backward:
        hidden = jnp.flip(hidden, 1)
    return hidden


def inside_mask(length, where, count):
    places = jnp.arange(length + 2)
    outside = (places == 0) & (where == 0) | (places == length + 1) & (where == count - 1)
    return jnp.where(outside, 0.0, 1.0).astype(jnp.float32)


def body(
    noisy,
    first_weight,
    first_bias,
    second_weight,
    second_bias,
    head_weight,
    seg_weight_in,
    seg_bias_in,
    seg_weight_out,
    seg_bias_out,
):
    noisy_pad = with_halo(noisy[None], (("gz", 1), ("gy", 2), ("gx", 3)), 1)
    first_hidden = recurrent(noisy_pad, first_weight, first_bias, False)
    hidden_pad = with_halo(first_hidden, (("gz", 1), ("gy", 2), ("gx", 3)), 1)
    second_hidden = recurrent(hidden_pad, second_weight, second_bias, True)
    denoised = noisy + jnp.einsum(
        "c,czyx->zyx", head_weight, second_hidden, precision=lax.Precision.HIGHEST
    )
    deep_pad = with_halo(denoised[None], (("gz", 1), ("gy", 2), ("gx", 3)), 2)
    grown = jnp.maximum(convolve(deep_pad, seg_weight_in) + seg_bias_in[:, None, None, None], 0.0)
    mask_z = inside_mask(denoised.shape[0], lax.axis_index("gz"), lax.axis_size("gz"))
    mask_y = inside_mask(denoised.shape[1], lax.axis_index("gy"), lax.axis_size("gy"))
    mask_x = inside_mask(denoised.shape[2], lax.axis_index("gx"), lax.axis_size("gx"))
    feature_pad = (
        grown * (mask_z[:, None, None] * mask_y[None, :, None] * mask_x[None, None, :])[None]
    )
    segmented = convolve(feature_pad, seg_weight_out) + seg_bias_out[:, None, None, None]
    return (denoised, segmented)


HALO = 4
AHEAD, PACE = 8, 4
LANES, SUBLANES = 128, 8


def split(value):
    high = value.astype(jnp.bfloat16)
    return high, (value - high.astype(jnp.float32)).astype(jnp.bfloat16)


def swapped(value, axis):
    return lax.ppermute(value, axis, [(0, 1), (1, 0)])


def gathered(noisy, laid_out):
    count = lax.axis_size("gz")
    block = noisy
    step = 1
    while step < count:
        pairs = [(i, i ^ step) for i in range(count)]
        other = lax.ppermute(block, "gz", pairs)
        low = lax.axis_index("gz") // step % 2 == 0
        block = jnp.where(
            low, jnp.concatenate([block, other], 0), jnp.concatenate([other, block], 0)
        )
        if step == 1:
            block, laid_out = lax.optimization_barrier((block, laid_out))
        step *= 2
    block = jnp.where(lax.axis_index("gy") == 0, block, jnp.flip(block, 1))
    near = lax.slice_in_dim(block, block.shape[1] - HALO, None, axis=1)
    block = jnp.concatenate([block, swapped(jnp.flip(near, 1), "gy")], 1)
    first = lax.axis_index("gx") == 0
    size = block.shape[2]
    low = lax.slice_in_dim(block, 0, HALO, axis=2)
    high = lax.slice_in_dim(block, size - HALO, size, axis=2)
    other = swapped(jnp.where(first, high, low), "gx")
    strip = jnp.where(
        first,
        jnp.concatenate([block[:, :, -2 * HALO :], other], 2),
        jnp.concatenate([other, block[:, :, : 2 * HALO]], 2),
    )
    return block, strip, laid_out


def prepare(
    geometry,
    w1_ref,
    b1_ref,
    w2_ref,
    b2_ref,
    head_ref,
    w3_ref,
    b3_ref,
    w4_ref,
    b4_ref,
    thin_lane_ref,
    thin_sub_ref,
    wide_lane_ref,
    keep_ref,
    gather_ref,
    w1_out,
    w2_out,
    w3_out,
    w4_out,
    columns_out,
    band,
):
    deep, depth, channels = geometry
    f32, bf16 = jnp.float32, jnp.bfloat16
    place = lax.axis_index("gz") * depth
    turned = lax.axis_index("gy") == 1

    def dot(left, right):
        return jnp.dot(left, right, preferred_element_type=f32)

    tap_lane, z_lane, part_lane = (thin_lane_ref[i : i + 1, :] for i in range(3))
    a_sub, tap_ahead, tap_turned = (thin_sub_ref[:, i : i + 1] for i in range(3))
    same = tap_lane == jnp.where(turned, tap_turned, tap_ahead)
    crossed = part_lane == 1
    reach = z_lane - a_sub + 1

    def thin_rows(halves, z):
        hit = same & (reach == z)
        high = jnp.where(hit & ~crossed, 1.0, 0.0).astype(bf16)
        low = jnp.where(hit & crossed, 1.0, 0.0).astype(bf16)
        return (dot(halves[0], high) + dot(halves[1], low)).astype(bf16)

    first = split(w1_ref[:, 0, :].T)
    out = 2 * channels
    for z in range(deep):
        w1_out[z * out : (z + 1) * out, :] = thin_rows(first, z)
    grow = split(w3_ref[:, 0, :])
    for i in range(depth + 2):
        z = place + i - 1
        inside = (z >= 0) & (z < deep)
        w3_out[i * channels : (i + 1) * channels, :] = thin_rows(
            grow, jnp.where(inside, z, -deep)
        )

    step = 3 * channels

    def lay(pieces, w_out):
        out = pieces[0][0].shape[0]
        for b in range(3):
            for i, half in enumerate((0, 0, 1)):
                band[b * out : (b + 1) * out, pl.ds(i * 3 * step, 3 * step)] = pieces[b][half]
        w_out[...] = band[: w_out.shape[0], :].astype(bf16)

    tall = w2_ref[...]
    pieces = []
    for b in range(3):
        ahead, back = (
            jnp.concatenate([tall[(a * 3 + k) * step : (a * 3 + k + 1) * step] for a in range(3)], 0)
            for k in (b, 2 - b)
        )
        pieces.append(tuple(h.astype(f32) for h in split(jnp.where(turned, back, ahead).T)))
    lay(pieces, w2_out)

    taps = lax.broadcasted_iota(jnp.int32, (27, wide_lane_ref.shape[1]), 0)
    spread = taps == jnp.where(turned, wide_lane_ref[1:2, :], wide_lane_ref[0:1, :])
    spread = jnp.where(spread, 1.0, 0.0).astype(bf16)
    keep = jnp.concatenate([keep_ref[...]] * channels, 0)
    flats = [
        dot(gather_ref[...], (dot(half, spread) * keep).astype(bf16))
        for half in split(w4_ref[...])
    ]
    lay([[f[:, b * 3 * step : (b + 1) * 3 * step] for f in flats] for b in range(3)], w4_out)

    at_row = lax.broadcasted_iota(jnp.int32, (channels, channels), 0)
    at_lane = lax.broadcasted_iota(jnp.int32, (channels, channels), 1)
    for i, ref in enumerate((b1_ref, b2_ref, head_ref, b3_ref, b4_ref)):
        columns_out[:, i : i + 1] = jnp.sum(
            jnp.where(at_row == at_lane, ref[...], 0.0), axis=1, keepdims=True
        )


def kernel(
    geometry,
    block_ref,
    strip_ref,
    w1_ref,
    w2_ref,
    w3_ref,
    w4_ref,
    columns_ref,
    den_ref,
    seg_ref,
    lines,
    thin,
    pre,
    partial,
    wide_hi,
    wide_lo,
    sums,
    tiles,
):
    deep, depth, channels, pitch, high = geometry
    f32, bf16 = jnp.float32, jnp.bfloat16
    height, width = den_ref.shape[1:]
    place = lax.axis_index("gz")
    turned = lax.axis_index("gy") == 1
    bias1, bias2, head, bias3, bias4 = (columns_ref[:, i : i + 1] for i in range(5))
    lane = lax.broadcasted_iota(jnp.int32, (1, LANES), 1)
    first_rows, second_rows, third_rows = high - 1, high - 2, high - 3
    edge = 3 * channels

    def split_strip(field):
        return field[:, :LANES], field[:, LANES:]

    def clean(field):
        strip, main = split_strip(field)
        return jnp.concatenate([jnp.where(lane < first_rows * pitch, strip, 0.0), main], 1)

    def beside(field, c):
        if c == 1:
            return field
        shift, end = (1, 0) if c == 0 else (LANES - 1, LANES - 1)
        out = [pltpu.roll(field[:, :LANES], shift, 1)]
        for at in range(LANES, field.shape[1], LANES):
            moved = pltpu.roll(field[:, at : at + LANES], shift, 1)
            out.append(jnp.where(lane == end, 0.0, moved))
        return jnp.concatenate(out, 1)

    def strip_row(strip, b):
        if b == 1:
            return strip
        moved = pltpu.roll(strip, pitch if b == 0 else LANES - pitch, 1)
        return jnp.where(lane < pitch, 0.0, moved) if b == 0 else moved

    def thin_columns(fields, rows):
        for c, field in enumerate(fields):
            strip, main = split_strip(field)
            for i, half in enumerate(split(main)):
                lines[3 * i + c, :, pl.ds(LANES, main.shape[1])] = half
            for b in range(3):
                t = 3 * b + c
                halves = split(strip_row(strip, b))
                for k, i in enumerate((0, 0, 1)):
                    at = slice((k * 9 + t) * deep, (k * 9 + t + 1) * deep)
                    thin[at, :LANES] = halves[i]
                    thin[at, LANES : (rows + 1) * LANES] = lines[
                        3 * i + c, :, b * LANES : (b + rows) * LANES
                    ]

    def wide_columns(z, field):
        length = field.shape[1]
        for c in range(3):
            at = (z * 3 + c) * channels
            h, l = split(beside(field, c))
            wide_hi[at : at + channels, :length] = h
            wide_lo[at : at + channels, :length] = l

    def chunks(length):
        return [(i, min(2 * LANES, length - i)) for i in range(0, length, 2 * LANES)]

    def convolve(w_ref, z, chunk):
        at, length = chunk
        taps = slice(z * edge, (z + 3) * edge)
        h = wide_hi[taps, at : at + length]
        l = wide_lo[taps, at : at + length]
        out = jnp.dot(w_ref[...], jnp.concatenate([h, l, h], 0), preferred_element_type=f32)
        n = w_ref.shape[0]
        if at == 0:
            sums[z, :n, :LANES] = out[:, :LANES]
            sums[z, :n, 2 * LANES : LANES + length] = out[:, LANES:]
        else:
            sums[z, :n, LANES + at : LANES + at + length] = out

    def layer(z, at, step, rows):
        strip = main = 0.0
        for b in range(3):
            k = slice(at + b * step, at + b * step + channels)
            strip = strip + strip_row(sums[z, k, :LANES], b)
            main = main + sums[z, k, (b + 1) * LANES : (b + 1 + rows) * LANES]
        return jnp.concatenate([strip, main], 1)

    def gate(cand, up, hidden):
        fresh = 1.0 / (1.0 + jnp.exp(-up))
        return hidden + fresh * (jnp.tanh(cand) - hidden)

    lines[:, :, :LANES] = jnp.zeros((6, deep, LANES), bf16)
    sums[:, :, LANES : 2 * LANES] = jnp.zeros((deep, sums.shape[1], LANES), f32)
    zeros = jnp.zeros((edge, wide_hi.shape[1]), bf16)
    for wide in (wide_hi, wide_lo):
        wide[:edge, :] = zeros
        wide[(deep + 1) * edge :, :] = zeros

    strips = [jnp.zeros((deep, LANES), f32)] * 3
    for r in range(high):
        columns = strip_ref[:, r, :]
        columns = jnp.concatenate(
            [columns, jnp.zeros((deep, LANES - columns.shape[1]), f32)], 1
        )
        here = (lane >= r * pitch) & (lane < (r + 1) * pitch)
        for c in range(3):
            moved = pltpu.roll(columns, (r * pitch - c) % LANES, 1)
            strips[c] = jnp.where(here, moved, strips[c])
    noisy = jnp.concatenate([strips[1]] + [block_ref[:, r, :] for r in range(high)], 1)
    thin_columns(
        [jnp.concatenate([strips[c], split_strip(beside(noisy, c))[1]], 1) for c in range(3)],
        first_rows,
    )
    first_span, second_span, third_span = (
        (n + 1) * LANES for n in (first_rows, second_rows, third_rows)
    )
    todo = chunks(first_span)
    part = depth * 2 * channels

    def thin_block(b, chunk):
        at, length = chunk
        pre[b * part : (b + 1) * part, at : at + length] = jnp.dot(
            w1_ref[b * part : (b + 1) * part, :],
            thin[:, at : at + length],
            preferred_element_type=f32,
        )

    for chunk in todo:
        thin_block(0, chunk)
    waiting = []
    hidden = jnp.zeros((channels, first_span), f32)
    for z in range(deep):
        at = z * 2 * channels
        hidden = gate(
            pre[at : at + channels, :],
            pre[at + channels : at + 2 * channels, :] + bias1,
            hidden,
        )
        wide_columns(z + 1, clean(hidden))
        if z // depth + 1 < deep // depth:
            for chunk in todo[z % depth :: depth]:
                thin_block(z // depth + 1, chunk)
        if 0 < z <= AHEAD:
            waiting += [(z - 1, chunk) for chunk in todo]
        for _ in range(min(PACE, len(waiting))):
            convolve(w2_ref, *waiting.pop(0))

    later = waiting + [(z, chunk) for z in range(deep - 1, AHEAD - 1, -1) for chunk in todo]
    for _ in range(min(2 * len(todo), len(later))):
        convolve(w2_ref, *later.pop(0))
    hidden = jnp.zeros((channels, second_span), f32)
    for z in range(deep - 1, -1, -1):
        for _ in range(min(len(todo), len(later))):
            convolve(w2_ref, *later.pop(0))
        hidden = gate(
            layer(z, 0, 2 * channels, second_rows),
            layer(z, channels, 2 * channels, second_rows) + bias2,
            hidden,
        )
        scaled = hidden * head
        while scaled.shape[0] > SUBLANES:
            half = scaled.shape[0] // 2
            scaled = scaled[:half] + scaled[half:]
        partial[z * SUBLANES : (z + 1) * SUBLANES, :] = scaled

    shape = (deep, deep * SUBLANES)
    row, column = (lax.broadcasted_iota(jnp.int32, shape, i) for i in range(2))
    own = (column >= row * SUBLANES) & (column < (row + 1) * SUBLANES)
    adder = jnp.where(own, 1.0, 0.0).astype(bf16)
    change = sum(
        jnp.dot(adder, half, preferred_element_type=f32) for half in split(partial[...])
    )
    finished = noisy[:, :second_span] + change
    thin_columns([beside(finished, c) for c in range(3)], third_rows)
    grown = jnp.dot(w3_ref[...], thin[:, :third_span], preferred_element_type=f32)
    for i in range(depth + 2):
        z = place * depth + i - 1
        real = jnp.where((z >= 0) & (z < deep), 1.0, 0.0)
        features = jnp.maximum(grown[i * channels : (i + 1) * channels] + bias3, 0.0)
        wide_columns(i, clean(features * real))

    right = lax.axis_index("gx") == 0
    beyond = lane - jnp.where(right, width - HALO, 0)
    border = (beyond >= 0) & (beyond < HALO)

    def mended(strip, main, r):
        at = r * pitch + HALO - 1
        shift = jnp.where(right, (width - HALO - at) % LANES, (LANES - at) % LANES)
        return jnp.where(border, pltpu.roll(strip, shift, 1), main)

    def at_row(r):
        return jnp.where(turned, height - 1 - r, r)

    mine = finished[:depth]
    for b in range(1, deep // depth):
        mine = jnp.where(place == b, finished[b * depth : (b + 1) * depth], mine)
    mine = jnp.concatenate([mine, jnp.zeros((SUBLANES - depth, second_span), f32)], 0)
    for r in range(height):
        at = pl.multiple_of(at_row(r) * SUBLANES, SUBLANES)
        tiles[pl.ds(at, SUBLANES), :] = mended(
            mine[:, :LANES], mine[:, (r + 1) * LANES : (r + 2) * LANES], r
        )
    for z in range(depth):
        den_ref[z] = tiles[pl.ds(z, height, stride=SUBLANES), :]
    for z in range(depth):
        for chunk in chunks(third_span):
            convolve(w4_ref, z, chunk)
    for z in range(depth):
        total = layer(z, 0, channels, height) + bias4
        for r in range(height):
            at = pl.multiple_of((z * height + at_row(r)) * channels, channels)
            tiles[pl.ds(at, channels), :] = mended(
                total[:, :LANES], total[:, (r + 1) * LANES : (r + 2) * LANES], r
            )
    for z in range(depth):
        for o in range(channels):
            seg_ref[o, z] = tiles[pl.ds(z * height * channels + o, height, stride=channels), :]


def local_body(
    noisy,
    first_weight,
    first_bias,
    second_weight,
    second_bias,
    head_weight,
    seg_weight_in,
    seg_bias_in,
    seg_weight_out,
    seg_bias_out,
):
    depth, height, width = noisy.shape
    count = lax.axis_size("gz")
    place = lax.axis_index("gz")
    deep = count * depth
    channels = first_bias.shape[0]
    high, pitch = height + HALO, 3 * HALO - 2
    narrow = high * LANES

    f32, bf16 = jnp.float32, jnp.bfloat16
    lane = np.arange(27 * deep)
    thin_lane = np.stack(
        [lane // deep % 9, lane % deep, lane // (9 * deep)] + [lane * 0] * 5
    ).astype(np.int32)
    tap = np.arange(27)
    thin_sub = np.stack(
        [tap // 9, tap % 9, (2 - tap // 3 % 3) * 3 + tap % 3], 1
    ).astype(np.int32)
    lane = np.arange(27 * channels)
    b, a, c = lane // channels // 9, lane // channels // 3 % 3, lane // channels % 3
    wide_lane = np.stack(
        [a * 9 + b * 3 + c, a * 9 + (2 - b) * 3 + c] + [lane * 0] * 6
    ).astype(np.int32)
    keep = (np.arange(channels)[:, None] == lane[None] % channels).astype(np.float32)
    lane = np.arange(channels * channels)
    gather = (np.arange(channels)[:, None] == lane[None] // channels).astype(bf16)

    taps = 3 * 9 * channels
    in_vmem = pl.BlockSpec(memory_space=pltpu.VMEM)
    prepared = pl.pallas_call(
        functools.partial(prepare, (deep, depth, channels)),
        out_shape=(
            pltpu.VMEM((deep * 2 * channels, 27 * deep), bf16),
            pltpu.VMEM((3 * 2 * channels, taps), bf16),
            pltpu.VMEM(((depth + 2) * channels, 27 * deep), bf16),
            pltpu.VMEM((3 * channels, taps), bf16),
            pltpu.VMEM((channels, LANES), f32),
        ),
        in_specs=[in_vmem] * 14,
        out_specs=(in_vmem,) * 5,
        scratch_shapes=[pltpu.VMEM((3 * 2 * channels, taps), f32)],
        compiler_params=pltpu.CompilerParams(vmem_limit_bytes=16 * 1024 * 1024),
    )
    weights = (
        jnp.transpose(first_weight, (2, 1, 0)),
        first_bias.reshape(1, -1),
        jnp.transpose(second_weight, (2, 1, 0)).reshape(-1, 2 * channels),
        second_bias.reshape(1, -1),
        head_weight.reshape(1, -1),
        seg_weight_in,
        seg_bias_in.reshape(1, -1),
        seg_weight_out.reshape(-1, 27),
        seg_bias_out.reshape(1, -1),
    )
    tables = tuple(jnp.asarray(v) for v in (thin_lane, thin_sub, wide_lane, keep, gather))

    given = [pltpu.with_memory_space_constraint(v, pltpu.HBM) for v in weights + tables]
    block, strip, laid_out = gathered(noisy, prepared(*given))
    operands = [
        pltpu.with_memory_space_constraint(v, pltpu.VMEM)
        for v in (block, strip, *laid_out)
    ]
    return pl.pallas_call(
        functools.partial(kernel, (deep, depth, channels, pitch, high)),
        out_shape=(
            jax.ShapeDtypeStruct((depth, height, width), f32),
            jax.ShapeDtypeStruct((channels, depth, height, width), f32),
        ),
        in_specs=[in_vmem] * 7,
        out_specs=(in_vmem,) * 2,
        scratch_shapes=[
            pltpu.VMEM((6, deep, (high + 1) * LANES), bf16),
            pltpu.VMEM((27 * deep, narrow), bf16),
            pltpu.VMEM((deep * 2 * channels, narrow), f32),
            pltpu.VMEM((deep * SUBLANES, narrow - LANES), f32),
            pltpu.VMEM(((deep + 2) * 3 * channels, narrow), bf16),
            pltpu.VMEM(((deep + 2) * 3 * channels, narrow), bf16),
            pltpu.VMEM((deep, 3 * 2 * channels, narrow + LANES), f32),
            pltpu.VMEM((depth * height * channels, width), f32),
        ],
        compiler_params=pltpu.CompilerParams(vmem_limit_bytes=36 * 1024 * 1024),
    )(*operands)


def solution(mesh):
    in_specs = (P(("win", "gz"), "gy", "gx"), P(), P(), P(), P(), P(), P(), P(), P(), P())
    out_specs = (P(("win", "gz"), "gy", "gx"), P(None, ("win", "gz"), "gy", "gx"))
    shallow = mesh.shape["gz"] in (1, 2, 4) and mesh.shape["gy"] == 2 and mesh.shape["gx"] == 2
    chosen = local_body if shallow else body
    return jax.shard_map(chosen, mesh=mesh, in_specs=in_specs, out_specs=out_specs, check_vma=False)
```

```python
import functools

import jax
import jax.numpy as jnp
import numpy as np
from jax import lax
from jax.experimental import pallas as pl
from jax.experimental.pallas import tpu as pltpu
from jax.sharding import PartitionSpec as P


def shifted(value, axis, steps):
    count = lax.axis_size(axis)
    first, last = (max(0, -steps), min(count, count - steps))
    return lax.ppermute(value, axis, [(source, source + steps) for source in range(first, last)])


def with_halo(block, sides, width):
    for axis, dim in sides:
        count = lax.axis_size(axis)
        forward = [(i, i + 1) for i in range(count - 1)]
        backward = [(target, source) for source, target in forward]
        low = lax.ppermute(
            lax.slice_in_dim(block, block.shape[dim] - width, None, axis=dim), axis, forward
        )
        high = lax.ppermute(lax.slice_in_dim(block, 0, width, axis=dim), axis, backward)
        block = jnp.concatenate([low, block, high], axis=dim)
    return block


def convolve(padded, weight):
    depth = padded.shape[1] - 2
    height = padded.shape[2] - 2
    width = padded.shape[3] - 2
    total = jnp.zeros((weight.shape[0], depth, height, width), jnp.float32)
    for tap in range(27):
        step_z = tap // 9
        step_y = tap // 3 % 3
        step_x = tap % 3
        piece = padded[
            :, step_z : step_z + depth, step_y : step_y + height, step_x : step_x + width
        ]
        total = total + jnp.einsum(
            "oc,czyx->ozyx", weight[:, :, tap], piece, precision=lax.Precision.HIGHEST
        )
    return total


def affine(earlier, later):
    return (earlier[0] * later[0], later[0] * earlier[1] + later[1])


def recurrent(padded, weight, bias, backward):
    channels = bias.shape[0]
    pre = convolve(padded, weight)
    cand = jnp.tanh(pre[:channels])
    keep = jax.nn.sigmoid(-(pre[channels:] + bias[:, None, None, None]))
    inject = (1.0 - keep) * cand
    if backward:
        keep = jnp.flip(keep, 1)
        inject = jnp.flip(inject, 1)
    cum_keep, cum_inject = lax.associative_scan(affine, (keep, inject), axis=1)
    total_keep = cum_keep[:, -1]
    total_inject = cum_inject[:, -1]
    offset = -1 if backward else 1

    def relay(turn, carry):
        return shifted(total_keep * carry + total_inject, "gz", offset)

    carry = lax.fori_loop(0, lax.axis_size("gz") - 1, relay, jnp.zeros_like(total_inject))
    hidden = cum_keep * carry[:, None] + cum_inject
    if backward:
        hidden = jnp.flip(hidden, 1)
    return hidden


def inside_mask(length, where, count):
    places = jnp.arange(length + 2)
    outside = (places == 0) & (where == 0) | (places == length + 1) & (where == count - 1)
    return jnp.where(outside, 0.0, 1.0).astype(jnp.float32)


def body(
    noisy,
    first_weight,
    first_bias,
    second_weight,
    second_bias,
    head_weight,
    seg_weight_in,
    seg_bias_in,
    seg_weight_out,
    seg_bias_out,
):
    noisy_pad = with_halo(noisy[None], (("gz", 1), ("gy", 2), ("gx", 3)), 1)
    first_hidden = recurrent(noisy_pad, first_weight, first_bias, False)
    hidden_pad = with_halo(first_hidden, (("gz", 1), ("gy", 2), ("gx", 3)), 1)
    second_hidden = recurrent(hidden_pad, second_weight, second_bias, True)
    denoised = noisy + jnp.einsum(
        "c,czyx->zyx", head_weight, second_hidden, precision=lax.Precision.HIGHEST
    )
    deep_pad = with_halo(denoised[None], (("gz", 1), ("gy", 2), ("gx", 3)), 2)
    grown = jnp.maximum(convolve(deep_pad, seg_weight_in) + seg_bias_in[:, None, None, None], 0.0)
    mask_z = inside_mask(denoised.shape[0], lax.axis_index("gz"), lax.axis_size("gz"))
    mask_y = inside_mask(denoised.shape[1], lax.axis_index("gy"), lax.axis_size("gy"))
    mask_x = inside_mask(denoised.shape[2], lax.axis_index("gx"), lax.axis_size("gx"))
    feature_pad = (
        grown * (mask_z[:, None, None] * mask_y[None, :, None] * mask_x[None, None, :])[None]
    )
    segmented = convolve(feature_pad, seg_weight_out) + seg_bias_out[:, None, None, None]
    return (denoised, segmented)


HALO = 4
AHEAD, PACE = 8, 4
LANES, SUBLANES = 128, 8


def split(value):
    high = value.astype(jnp.bfloat16)
    return high, (value - high.astype(jnp.float32)).astype(jnp.bfloat16)


def swapped(value, axis):
    return lax.ppermute(value, axis, [(0, 1), (1, 0)])


def gathered(noisy, laid_out):
    count = lax.axis_size("gz")
    block = noisy
    step = 1
    while step < count:
        pairs = [(i, i ^ step) for i in range(count)]
        other = lax.ppermute(block, "gz", pairs)
        low = lax.axis_index("gz") // step % 2 == 0
        block = jnp.where(
            low, jnp.concatenate([block, other], 0), jnp.concatenate([other, block], 0)
        )
        if step == 1:
            block, laid_out = lax.optimization_barrier((block, laid_out))
        step *= 2
    block = jnp.where(lax.axis_index("gy") == 0, block, jnp.flip(block, 1))
    near = lax.slice_in_dim(block, block.shape[1] - HALO, None, axis=1)
    block = jnp.concatenate([block, swapped(jnp.flip(near, 1), "gy")], 1)
    first = lax.axis_index("gx") == 0
    size = block.shape[2]
    low = lax.slice_in_dim(block, 0, HALO, axis=2)
    high = lax.slice_in_dim(block, size - HALO, size, axis=2)
    other = swapped(jnp.where(first, high, low), "gx")
    strip = jnp.where(
        first,
        jnp.concatenate([block[:, :, -2 * HALO :], other], 2),
        jnp.concatenate([other, block[:, :, : 2 * HALO]], 2),
    )
    return block, strip, laid_out


def prepare(
    geometry,
    w1_ref,
    b1_ref,
    w2_ref,
    b2_ref,
    head_ref,
    w3_ref,
    b3_ref,
    w4_ref,
    b4_ref,
    thin_lane_ref,
    thin_sub_ref,
    wide_lane_ref,
    keep_ref,
    gather_ref,
    w1_out,
    w2_out,
    w3_out,
    w4_out,
    columns_out,
    band,
):
    deep, depth, channels = geometry
    f32, bf16 = jnp.float32, jnp.bfloat16
    place = lax.axis_index("gz") * depth
    turned = lax.axis_index("gy") == 1

    def dot(left, right):
        return jnp.dot(left, right, preferred_element_type=f32)

    tap_lane, z_lane, part_lane = (thin_lane_ref[i : i + 1, :] for i in range(3))
    a_sub, tap_ahead, tap_turned = (thin_sub_ref[:, i : i + 1] for i in range(3))
    same = tap_lane + 9 * (part_lane & 1) == jnp.where(turned, tap_turned, tap_ahead)
    reach = jnp.where(same, z_lane - a_sub + 1, -2 * deep)

    def paired(weight):
        blank = jnp.zeros((weight.shape[0], thin_sub_ref.shape[0] // 2 - weight.shape[1]), f32)
        high, low = (half.astype(f32) for half in split(weight))
        return jnp.concatenate([high, blank, low, blank], 1).astype(bf16)

    def thin_rows(pair, z):
        return dot(pair, jnp.where(reach == z, 1.0, 0.0).astype(bf16)).astype(bf16)

    first = paired(w1_ref[:, 0, :].T)
    out = 2 * channels
    for z in range(deep):
        w1_out[z * out : (z + 1) * out, :] = thin_rows(first, z)
    grow = paired(w3_ref[:, 0, :])
    for i in range(depth + 2):
        z = place + i - 1
        inside = (z >= 0) & (z < deep)
        w3_out[i * channels : (i + 1) * channels, :] = thin_rows(
            grow, jnp.where(inside, z, -deep)
        )

    step = 3 * channels

    def lay(pieces, w_out):
        out = pieces[0][0].shape[0]
        for b in range(3):
            for i, half in enumerate((0, 0, 1)):
                band[b * out : (b + 1) * out, pl.ds(i * 3 * step, 3 * step)] = pieces[b][half]
        w_out[...] = band[: w_out.shape[0], :].astype(bf16)

    tall = w2_ref[...]
    pieces = []
    for b in range(3):
        ahead, back = (
            jnp.concatenate([tall[(a * 3 + k) * step : (a * 3 + k + 1) * step] for a in range(3)], 0)
            for k in (b, 2 - b)
        )
        pieces.append(tuple(h.astype(f32) for h in split(jnp.where(turned, back, ahead).T)))
    lay(pieces, w2_out)

    taps = lax.broadcasted_iota(jnp.int32, (27, wide_lane_ref.shape[1]), 0)
    spread = taps == jnp.where(turned, wide_lane_ref[1:2, :], wide_lane_ref[0:1, :])
    spread = jnp.where(spread, 1.0, 0.0).astype(bf16)
    keep = jnp.concatenate([keep_ref[...]] * channels, 0)
    both = dot(jnp.concatenate(split(w4_ref[...]), 0), spread)
    flats = [
        dot(gather_ref[...], (half * keep).astype(bf16)) for half in jnp.split(both, 2, 0)
    ]
    lay([[f[:, b * 3 * step : (b + 1) * 3 * step] for f in flats] for b in range(3)], w4_out)

    at_row = lax.broadcasted_iota(jnp.int32, (channels, channels), 0)
    at_lane = lax.broadcasted_iota(jnp.int32, (channels, channels), 1)
    for i, ref in enumerate((b1_ref, b2_ref, head_ref, b3_ref, b4_ref)):
        columns_out[:, i : i + 1] = jnp.sum(
            jnp.where(at_row == at_lane, ref[...], 0.0), axis=1, keepdims=True
        )


def kernel(
    geometry,
    block_ref,
    strip_ref,
    w1_ref,
    w2_ref,
    w3_ref,
    w4_ref,
    columns_ref,
    den_ref,
    seg_ref,
    lines,
    thin,
    pre,
    partial,
    wide_hi,
    wide_lo,
    sums,
    tiles,
):
    deep, depth, channels, pitch, high = geometry
    f32, bf16 = jnp.float32, jnp.bfloat16
    height, width = den_ref.shape[1:]
    place = lax.axis_index("gz")
    turned = lax.axis_index("gy") == 1
    bias1, bias2, head, bias3, bias4 = (columns_ref[:, i : i + 1] for i in range(5))
    lane = lax.broadcasted_iota(jnp.int32, (1, LANES), 1)
    first_rows, second_rows, third_rows = high - 1, high - 2, high - 3
    edge = 3 * channels

    def split_strip(field):
        return field[:, :LANES], field[:, LANES:]

    def clean(field):
        strip, main = split_strip(field)
        return jnp.concatenate([jnp.where(lane < first_rows * pitch, strip, 0.0), main], 1)

    def beside(field, c, first=0):
        if c == 1:
            return field
        shift, end = (1, 0) if c == 0 else (LANES - 1, LANES - 1)
        out = []
        for at in range(0, field.shape[1], LANES):
            moved = pltpu.roll(field[:, at : at + LANES], shift, 1)
            out.append(jnp.where(lane == end, 0.0, moved) if first + at > 0 else moved)
        return jnp.concatenate(out, 1)

    def strip_row(strip, b):
        if b == 1:
            return strip
        moved = pltpu.roll(strip, pitch if b == 0 else LANES - pitch, 1)
        return jnp.where(lane < pitch, 0.0, moved) if b == 0 else moved

    def thin_columns(fields, rows):
        for c, field in enumerate(fields):
            strip, main = split_strip(field)
            for i, half in enumerate(split(main)):
                lines[3 * i + c, :, pl.ds(LANES, main.shape[1])] = half
            for b in range(3):
                t = 3 * b + c
                halves = split(strip_row(strip, b))
                for k, i in enumerate((0, 0, 1)):
                    at = slice((k * 9 + t) * deep, (k * 9 + t + 1) * deep)
                    thin[at, :LANES] = halves[i]
                    thin[at, LANES : (rows + 1) * LANES] = lines[
                        3 * i + c, :, b * LANES : (b + rows) * LANES
                    ]

    def wide_columns(z, field, first=0):
        lanes = slice(first, first + field.shape[1])
        for c in range(3):
            at = (z * 3 + c) * channels
            h, l = split(beside(field, c, first))
            wide_hi[at : at + channels, lanes] = h
            wide_lo[at : at + channels, lanes] = l

    def chunks(length):
        return [(i, min(2 * LANES, length - i)) for i in range(0, length, 2 * LANES)]

    def convolve(w_ref, z, chunk):
        at, length = chunk
        taps = slice(z * edge, (z + 3) * edge)
        h = wide_hi[taps, at : at + length]
        l = wide_lo[taps, at : at + length]
        out = jnp.dot(w_ref[...], jnp.concatenate([h, l, h], 0), preferred_element_type=f32)
        n = w_ref.shape[0]
        if at == 0:
            sums[z, :n, :LANES] = out[:, :LANES]
            sums[z, :n, 2 * LANES : LANES + length] = out[:, LANES:]
        else:
            sums[z, :n, LANES + at : LANES + at + length] = out

    def layer(z, at, step, rows):
        strip = main = 0.0
        for b in range(3):
            k = slice(at + b * step, at + b * step + channels)
            strip = strip + strip_row(sums[z, k, :LANES], b)
            main = main + sums[z, k, (b + 1) * LANES : (b + 1 + rows) * LANES]
        return jnp.concatenate([strip, main], 1)

    def gate(cand, up, hidden):
        fresh = 1.0 / (1.0 + jnp.exp(-up))
        return hidden + fresh * (jnp.tanh(cand) - hidden)

    lines[:, :, :LANES] = jnp.zeros((6, deep, LANES), bf16)
    sums[:, :, LANES : 2 * LANES] = jnp.zeros((deep, sums.shape[1], LANES), f32)
    zeros = jnp.zeros((edge, wide_hi.shape[1]), bf16)
    for wide in (wide_hi, wide_lo):
        wide[:edge, :] = zeros
        wide[(deep + 1) * edge :, :] = zeros

    strips = [jnp.zeros((deep, LANES), f32)] * 3
    for r in range(high):
        columns = strip_ref[:, r, :]
        columns = jnp.concatenate(
            [columns, jnp.zeros((deep, LANES - columns.shape[1]), f32)], 1
        )
        here = (lane >= r * pitch) & (lane < (r + 1) * pitch)
        for c in range(3):
            moved = pltpu.roll(columns, (r * pitch - c) % LANES, 1)
            strips[c] = jnp.where(here, moved, strips[c])
    noisy = jnp.concatenate([strips[1]] + [block_ref[:, r, :] for r in range(high)], 1)
    thin_columns(
        [jnp.concatenate([strips[c], split_strip(beside(noisy, c))[1]], 1) for c in range(3)],
        first_rows,
    )
    first_span, second_span, third_span = (
        (n + 1) * LANES for n in (first_rows, second_rows, third_rows)
    )
    todo = chunks(first_span)
    part = depth * 2 * channels

    def thin_block(b, chunk):
        at, length = chunk
        pre[b * part : (b + 1) * part, at : at + length] = jnp.dot(
            w1_ref[b * part : (b + 1) * part, :],
            thin[:, at : at + length],
            preferred_element_type=f32,
        )

    for chunk in todo:
        thin_block(0, chunk)
    waiting = []
    hidden = jnp.zeros((channels, first_span), f32)
    for z in range(deep):
        at = z * 2 * channels
        hidden = gate(
            pre[at : at + channels, :],
            pre[at + channels : at + 2 * channels, :] + bias1,
            hidden,
        )
        wide_columns(z + 1, clean(hidden))
        if z // depth + 1 < deep // depth:
            for chunk in todo[z % depth :: depth]:
                thin_block(z // depth + 1, chunk)
        if 0 < z <= AHEAD:
            waiting += [(z - 1, chunk) for chunk in todo]
        for _ in range(min(PACE, len(waiting))):
            convolve(w2_ref, *waiting.pop(0))

    later = waiting + [(z, chunk) for z in range(deep - 1, AHEAD - 1, -1) for chunk in todo]
    for _ in range(min(2 * len(todo), len(later))):
        convolve(w2_ref, *later.pop(0))
    hidden = jnp.zeros((channels, second_span), f32)
    for z in range(deep - 1, -1, -1):
        for _ in range(min(len(todo), len(later))):
            convolve(w2_ref, *later.pop(0))
        hidden = gate(
            layer(z, 0, 2 * channels, second_rows),
            layer(z, channels, 2 * channels, second_rows) + bias2,
            hidden,
        )
        scaled = hidden * head
        while scaled.shape[0] > SUBLANES:
            half = scaled.shape[0] // 2
            scaled = scaled[:half] + scaled[half:]
        partial[z * SUBLANES : (z + 1) * SUBLANES, :] = scaled

    shape = (deep, deep * SUBLANES)
    row, column = (lax.broadcasted_iota(jnp.int32, shape, i) for i in range(2))
    own = (column >= row * SUBLANES) & (column < (row + 1) * SUBLANES)
    adder = jnp.where(own, 1.0, 0.0).astype(bf16)
    change = sum(
        jnp.dot(adder, half, preferred_element_type=f32) for half in split(partial[...])
    )
    finished = noisy[:, :second_span] + change
    thin_columns([beside(finished, c) for c in range(3)], third_rows)

    def grow(chunk):
        at, length = chunk
        return jnp.dot(w3_ref[...], thin[:, at : at + length], preferred_element_type=f32)

    def spread(chunk, grown):
        for i in range(depth + 2):
            z = place * depth + i - 1
            real = jnp.where((z >= 0) & (z < deep), 1.0, 0.0)
            features = jnp.maximum(grown[i * channels : (i + 1) * channels] + bias3, 0.0)
            features = features * real
            wide_columns(i, features if chunk[0] else clean(features), chunk[0])

    todo = chunks(third_span)
    grown = {}
    for k in range(len(todo) + 2):
        if k < len(todo):
            grown[k] = grow(todo[k])
        if 0 <= k - 1 < len(todo):
            spread(todo[k - 1], grown[k - 1])
        if k >= 2:
            for z in range(depth):
                convolve(w4_ref, z, todo[k - 2])

    right = lax.axis_index("gx") == 0
    beyond = lane - jnp.where(right, width - HALO, 0)
    border = (beyond >= 0) & (beyond < HALO)

    def mended(strip, main, r):
        at = r * pitch + HALO - 1
        shift = jnp.where(right, (width - HALO - at) % LANES, (LANES - at) % LANES)
        return jnp.where(border, pltpu.roll(strip, shift, 1), main)

    def at_row(r):
        return jnp.where(turned, height - 1 - r, r)

    mine = finished[:depth]
    for b in range(1, deep // depth):
        mine = jnp.where(place == b, finished[b * depth : (b + 1) * depth], mine)
    mine = jnp.concatenate([mine, jnp.zeros((SUBLANES - depth, second_span), f32)], 0)
    for r in range(height):
        at = pl.multiple_of(at_row(r) * SUBLANES, SUBLANES)
        tiles[pl.ds(at, SUBLANES), :] = mended(
            mine[:, :LANES], mine[:, (r + 1) * LANES : (r + 2) * LANES], r
        )
    for z in range(depth):
        den_ref[z] = tiles[pl.ds(z, height, stride=SUBLANES), :]
    for z in range(depth):
        total = layer(z, 0, channels, height) + bias4
        for r in range(height):
            at = pl.multiple_of((z * height + at_row(r)) * channels, channels)
            tiles[pl.ds(at, channels), :] = mended(
                total[:, :LANES], total[:, (r + 1) * LANES : (r + 2) * LANES], r
            )
    for z in range(depth):
        for o in range(channels):
            seg_ref[o, z] = tiles[pl.ds(z * height * channels + o, height, stride=channels), :]


def local_body(
    noisy,
    first_weight,
    first_bias,
    second_weight,
    second_bias,
    head_weight,
    seg_weight_in,
    seg_bias_in,
    seg_weight_out,
    seg_bias_out,
):
    depth, height, width = noisy.shape
    count = lax.axis_size("gz")
    place = lax.axis_index("gz")
    deep = count * depth
    channels = first_bias.shape[0]
    high, pitch = height + HALO, 3 * HALO - 2
    narrow = high * LANES

    f32, bf16 = jnp.float32, jnp.bfloat16
    lane = np.arange(27 * deep)
    thin_lane = np.stack(
        [lane // deep % 9, lane % deep, lane // (9 * deep)] + [lane * 0] * 5
    ).astype(np.int32)
    tap = np.arange(27)
    ahead, back = tap % 9, (2 - tap // 3 % 3) * 3 + tap % 3
    never = np.full(5, -1)
    thin_sub = np.stack(
        [
            np.concatenate([low, never, high, never])
            for low, high in ((tap // 9, tap // 9), (ahead, ahead + 9), (back, back + 9))
        ],
        1,
    ).astype(np.int32)
    lane = np.arange(27 * channels)
    b, a, c = lane // channels // 9, lane // channels // 3 % 3, lane // channels % 3
    wide_lane = np.stack(
        [a * 9 + b * 3 + c, a * 9 + (2 - b) * 3 + c] + [lane * 0] * 6
    ).astype(np.int32)
    keep = (np.arange(channels)[:, None] == lane[None] % channels).astype(np.float32)
    lane = np.arange(channels * channels)
    gather = (np.arange(channels)[:, None] == lane[None] // channels).astype(bf16)

    taps = 3 * 9 * channels
    in_vmem = pl.BlockSpec(memory_space=pltpu.VMEM)
    prepared = pl.pallas_call(
        functools.partial(prepare, (deep, depth, channels)),
        out_shape=(
            pltpu.VMEM((deep * 2 * channels, 27 * deep), bf16),
            pltpu.VMEM((3 * 2 * channels, taps), bf16),
            pltpu.VMEM(((depth + 2) * channels, 27 * deep), bf16),
            pltpu.VMEM((3 * channels, taps), bf16),
            pltpu.VMEM((channels, LANES), f32),
        ),
        in_specs=[in_vmem] * 14,
        out_specs=(in_vmem,) * 5,
        scratch_shapes=[pltpu.VMEM((3 * 2 * channels, taps), f32)],
        compiler_params=pltpu.CompilerParams(vmem_limit_bytes=16 * 1024 * 1024),
    )
    weights = (
        jnp.transpose(first_weight, (2, 1, 0)),
        first_bias.reshape(1, -1),
        jnp.transpose(second_weight, (2, 1, 0)).reshape(-1, 2 * channels),
        second_bias.reshape(1, -1),
        head_weight.reshape(1, -1),
        seg_weight_in,
        seg_bias_in.reshape(1, -1),
        seg_weight_out.reshape(-1, 27),
        seg_bias_out.reshape(1, -1),
    )
    tables = tuple(jnp.asarray(v) for v in (thin_lane, thin_sub, wide_lane, keep, gather))

    given = [pltpu.with_memory_space_constraint(v, pltpu.HBM) for v in weights + tables]
    block, strip, laid_out = gathered(noisy, prepared(*given))
    operands = [
        pltpu.with_memory_space_constraint(v, pltpu.VMEM)
        for v in (block, strip, *laid_out)
    ]
    return pl.pallas_call(
        functools.partial(kernel, (deep, depth, channels, pitch, high)),
        out_shape=(
            jax.ShapeDtypeStruct((depth, height, width), f32),
            jax.ShapeDtypeStruct((channels, depth, height, width), f32),
        ),
        in_specs=[in_vmem] * 7,
        out_specs=(in_vmem,) * 2,
        scratch_shapes=[
            pltpu.VMEM((6, deep, (high + 1) * LANES), bf16),
            pltpu.VMEM((27 * deep, narrow), bf16),
            pltpu.VMEM((deep * 2 * channels, narrow), f32),
            pltpu.VMEM((deep * SUBLANES, narrow - LANES), f32),
            pltpu.VMEM(((deep + 2) * 3 * channels, narrow), bf16),
            pltpu.VMEM(((deep + 2) * 3 * channels, narrow), bf16),
            pltpu.VMEM((deep, 3 * 2 * channels, narrow + LANES), f32),
            pltpu.VMEM((depth * height * channels, width), f32),
        ],
        compiler_params=pltpu.CompilerParams(vmem_limit_bytes=36 * 1024 * 1024),
    )(*operands)


def solution(mesh):
    in_specs = (P(("win", "gz"), "gy", "gx"), P(), P(), P(), P(), P(), P(), P(), P(), P())
    out_specs = (P(("win", "gz"), "gy", "gx"), P(None, ("win", "gz"), "gy", "gx"))
    shallow = mesh.shape["gz"] in (1, 2, 4) and mesh.shape["gy"] == 2 and mesh.shape["gx"] == 2
    chosen = local_body if shallow else body
    return jax.shard_map(chosen, mesh=mesh, in_specs=in_specs, out_specs=out_specs, check_vma=False)
```

```python
import functools

import jax
import jax.numpy as jnp
import numpy as np
from jax import lax
from jax.experimental import pallas as pl
from jax.experimental.pallas import tpu as pltpu
from jax.sharding import PartitionSpec as P


def shifted(value, axis, steps):
    count = lax.axis_size(axis)
    first, last = (max(0, -steps), min(count, count - steps))
    return lax.ppermute(value, axis, [(source, source + steps) for source in range(first, last)])


def with_halo(block, sides, width):
    for axis, dim in sides:
        count = lax.axis_size(axis)
        forward = [(i, i + 1) for i in range(count - 1)]
        backward = [(target, source) for source, target in forward]
        low = lax.ppermute(
            lax.slice_in_dim(block, block.shape[dim] - width, None, axis=dim), axis, forward
        )
        high = lax.ppermute(lax.slice_in_dim(block, 0, width, axis=dim), axis, backward)
        block = jnp.concatenate([low, block, high], axis=dim)
    return block


def convolve(padded, weight):
    depth = padded.shape[1] - 2
    height = padded.shape[2] - 2
    width = padded.shape[3] - 2
    total = jnp.zeros((weight.shape[0], depth, height, width), jnp.float32)
    for tap in range(27):
        step_z = tap // 9
        step_y = tap // 3 % 3
        step_x = tap % 3
        piece = padded[
            :, step_z : step_z + depth, step_y : step_y + height, step_x : step_x + width
        ]
        total = total + jnp.einsum(
            "oc,czyx->ozyx", weight[:, :, tap], piece, precision=lax.Precision.HIGHEST
        )
    return total


def affine(earlier, later):
    return (earlier[0] * later[0], later[0] * earlier[1] + later[1])


def recurrent(padded, weight, bias, backward):
    channels = bias.shape[0]
    pre = convolve(padded, weight)
    cand = jnp.tanh(pre[:channels])
    keep = jax.nn.sigmoid(-(pre[channels:] + bias[:, None, None, None]))
    inject = (1.0 - keep) * cand
    if backward:
        keep = jnp.flip(keep, 1)
        inject = jnp.flip(inject, 1)
    cum_keep, cum_inject = lax.associative_scan(affine, (keep, inject), axis=1)
    total_keep = cum_keep[:, -1]
    total_inject = cum_inject[:, -1]
    offset = -1 if backward else 1

    def relay(turn, carry):
        return shifted(total_keep * carry + total_inject, "gz", offset)

    carry = lax.fori_loop(0, lax.axis_size("gz") - 1, relay, jnp.zeros_like(total_inject))
    hidden = cum_keep * carry[:, None] + cum_inject
    if backward:
        hidden = jnp.flip(hidden, 1)
    return hidden


def inside_mask(length, where, count):
    places = jnp.arange(length + 2)
    outside = (places == 0) & (where == 0) | (places == length + 1) & (where == count - 1)
    return jnp.where(outside, 0.0, 1.0).astype(jnp.float32)


def body(
    noisy,
    first_weight,
    first_bias,
    second_weight,
    second_bias,
    head_weight,
    seg_weight_in,
    seg_bias_in,
    seg_weight_out,
    seg_bias_out,
):
    noisy_pad = with_halo(noisy[None], (("gz", 1), ("gy", 2), ("gx", 3)), 1)
    first_hidden = recurrent(noisy_pad, first_weight, first_bias, False)
    hidden_pad = with_halo(first_hidden, (("gz", 1), ("gy", 2), ("gx", 3)), 1)
    second_hidden = recurrent(hidden_pad, second_weight, second_bias, True)
    denoised = noisy + jnp.einsum(
        "c,czyx->zyx", head_weight, second_hidden, precision=lax.Precision.HIGHEST
    )
    deep_pad = with_halo(denoised[None], (("gz", 1), ("gy", 2), ("gx", 3)), 2)
    grown = jnp.maximum(convolve(deep_pad, seg_weight_in) + seg_bias_in[:, None, None, None], 0.0)
    mask_z = inside_mask(denoised.shape[0], lax.axis_index("gz"), lax.axis_size("gz"))
    mask_y = inside_mask(denoised.shape[1], lax.axis_index("gy"), lax.axis_size("gy"))
    mask_x = inside_mask(denoised.shape[2], lax.axis_index("gx"), lax.axis_size("gx"))
    feature_pad = (
        grown * (mask_z[:, None, None] * mask_y[None, :, None] * mask_x[None, None, :])[None]
    )
    segmented = convolve(feature_pad, seg_weight_out) + seg_bias_out[:, None, None, None]
    return (denoised, segmented)


HALO = 4
AHEAD, PACE = 8, 4
LANES, SUBLANES = 128, 8


def split(value):
    high = value.astype(jnp.bfloat16)
    return high, (value - high.astype(jnp.float32)).astype(jnp.bfloat16)


def swapped(value, axis):
    return lax.ppermute(value, axis, [(0, 1), (1, 0)])


def gathered(noisy, laid_out):
    count = lax.axis_size("gz")
    block = noisy
    step = 1
    while step < count:
        pairs = [(i, i ^ step) for i in range(count)]
        other = lax.ppermute(block, "gz", pairs)
        low = lax.axis_index("gz") // step % 2 == 0
        block = jnp.where(
            low, jnp.concatenate([block, other], 0), jnp.concatenate([other, block], 0)
        )
        if step == 1:
            block, laid_out = lax.optimization_barrier((block, laid_out))
        step *= 2
    block = jnp.where(lax.axis_index("gy") == 0, block, jnp.flip(block, 1))
    near = lax.slice_in_dim(block, block.shape[1] - HALO, None, axis=1)
    block = jnp.concatenate([block, swapped(jnp.flip(near, 1), "gy")], 1)
    first = lax.axis_index("gx") == 0
    size = block.shape[2]
    low = lax.slice_in_dim(block, 0, HALO, axis=2)
    high = lax.slice_in_dim(block, size - HALO, size, axis=2)
    other = swapped(jnp.where(first, high, low), "gx")
    strip = jnp.where(
        first,
        jnp.concatenate([block[:, :, -2 * HALO :], other], 2),
        jnp.concatenate([other, block[:, :, : 2 * HALO]], 2),
    )
    return block, strip, laid_out


def prepare(
    geometry,
    w1_ref,
    b1_ref,
    w2_ref,
    b2_ref,
    head_ref,
    w3_ref,
    b3_ref,
    w4_ref,
    b4_ref,
    thin_lane_ref,
    thin_sub_ref,
    wide_lane_ref,
    keep_ref,
    gather_ref,
    w1_out,
    w2_out,
    w3_out,
    w4_out,
    columns_out,
    band,
):
    deep, depth, channels = geometry
    f32, bf16 = jnp.float32, jnp.bfloat16
    place = lax.axis_index("gz") * depth
    turned = lax.axis_index("gy") == 1

    def dot(left, right):
        return jnp.dot(left, right, preferred_element_type=f32)

    tap_lane, z_lane, part_lane = (thin_lane_ref[i : i + 1, :] for i in range(3))
    a_sub, tap_ahead, tap_turned = (thin_sub_ref[:, i : i + 1] for i in range(3))
    same = tap_lane + 9 * (part_lane & 1) == jnp.where(turned, tap_turned, tap_ahead)
    reach = jnp.where(same, z_lane - a_sub + 1, -2 * deep)

    def paired(weight):
        blank = jnp.zeros((weight.shape[0], thin_sub_ref.shape[0] // 2 - weight.shape[1]), f32)
        high, low = (half.astype(f32) for half in split(weight))
        return jnp.concatenate([high, blank, low, blank], 1).astype(bf16)

    def thin_rows(pair, z):
        return dot(pair, jnp.where(reach == z, 1.0, 0.0).astype(bf16)).astype(bf16)

    first = paired(w1_ref[:, 0, :].T)
    out = 2 * channels
    for z in range(deep):
        w1_out[z * out : (z + 1) * out, :] = thin_rows(first, z)
    grow = paired(w3_ref[:, 0, :])
    for i in range(depth + 2):
        z = place + i - 1
        inside = (z >= 0) & (z < deep)
        w3_out[i * channels : (i + 1) * channels, :] = thin_rows(
            grow, jnp.where(inside, z, -deep)
        )

    step = 3 * channels

    def lay(pieces, w_out):
        out = pieces[0][0].shape[0]
        for b in range(3):
            for i, half in enumerate((0, 0, 1)):
                band[b * out : (b + 1) * out, pl.ds(i * 3 * step, 3 * step)] = pieces[b][half]
        w_out[...] = band[: w_out.shape[0], :].astype(bf16)

    tall = w2_ref[...]
    pieces = []
    for b in range(3):
        ahead, back = (
            jnp.concatenate([tall[(a * 3 + k) * step : (a * 3 + k + 1) * step] for a in range(3)], 0)
            for k in (b, 2 - b)
        )
        pieces.append(tuple(h.astype(f32) for h in split(jnp.where(turned, back, ahead).T)))
    lay(pieces, w2_out)

    taps = lax.broadcasted_iota(jnp.int32, (27, wide_lane_ref.shape[1]), 0)
    spread = taps == jnp.where(turned, wide_lane_ref[1:2, :], wide_lane_ref[0:1, :])
    spread = jnp.where(spread, 1.0, 0.0).astype(bf16)
    keep = jnp.concatenate([keep_ref[...]] * channels, 0)
    both = dot(jnp.concatenate(split(w4_ref[...]), 0), spread)
    flats = [
        dot(gather_ref[...], (half * keep).astype(bf16)) for half in jnp.split(both, 2, 0)
    ]
    lay([[f[:, b * 3 * step : (b + 1) * 3 * step] for f in flats] for b in range(3)], w4_out)

    at_row = lax.broadcasted_iota(jnp.int32, (channels, channels), 0)
    at_lane = lax.broadcasted_iota(jnp.int32, (channels, channels), 1)
    for i, ref in enumerate((b1_ref, b2_ref, head_ref, b3_ref, b4_ref)):
        columns_out[:, i : i + 1] = jnp.sum(
            jnp.where(at_row == at_lane, ref[...], 0.0), axis=1, keepdims=True
        )


def kernel(
    geometry,
    block_ref,
    strip_ref,
    w1_ref,
    w2_ref,
    w3_ref,
    w4_ref,
    columns_ref,
    den_ref,
    seg_ref,
    lines,
    thin,
    pre,
    partial,
    wide_hi,
    wide_lo,
    sums,
    tiles,
):
    deep, depth, channels, pitch, high = geometry
    f32, bf16 = jnp.float32, jnp.bfloat16
    height, width = den_ref.shape[1:]
    place = lax.axis_index("gz")
    turned = lax.axis_index("gy") == 1
    bias1, bias2, head, bias3, bias4 = (columns_ref[:, i : i + 1] for i in range(5))
    lane = lax.broadcasted_iota(jnp.int32, (1, LANES), 1)
    first_rows, second_rows, third_rows = high - 1, high - 2, high - 3
    edge = 3 * channels

    def split_strip(field):
        return field[:, :LANES], field[:, LANES:]

    def clean(field):
        strip, main = split_strip(field)
        return jnp.concatenate([jnp.where(lane < first_rows * pitch, strip, 0.0), main], 1)

    def beside(field, c, first=0):
        if c == 1:
            return field
        shift, end = (1, 0) if c == 0 else (LANES - 1, LANES - 1)
        out = []
        for at in range(0, field.shape[1], LANES):
            moved = pltpu.roll(field[:, at : at + LANES], shift, 1)
            out.append(jnp.where(lane == end, 0.0, moved) if first + at > 0 else moved)
        return jnp.concatenate(out, 1)

    def strip_row(strip, b):
        if b == 1:
            return strip
        moved = pltpu.roll(strip, pitch if b == 0 else LANES - pitch, 1)
        return jnp.where(lane < pitch, 0.0, moved) if b == 0 else moved

    def thin_columns(fields, rows):
        for c, field in enumerate(fields):
            strip, main = split_strip(field)
            for i, half in enumerate(split(main)):
                lines[3 * i + c, :, pl.ds(LANES, main.shape[1])] = half
            for b in range(3):
                t = 3 * b + c
                halves = split(strip_row(strip, b))
                for k, i in enumerate((0, 0, 1)):
                    at = slice((k * 9 + t) * deep, (k * 9 + t + 1) * deep)
                    thin[at, :LANES] = halves[i]
                    thin[at, LANES : (rows + 1) * LANES] = lines[
                        3 * i + c, :, b * LANES : (b + rows) * LANES
                    ]

    def wide_columns(z, field, first=0):
        lanes = slice(first, first + field.shape[1])
        for c in range(3):
            at = (z * 3 + c) * channels
            h, l = split(beside(field, c, first))
            wide_hi[at : at + channels, lanes] = h
            wide_lo[at : at + channels, lanes] = l

    def chunks(length):
        return [(i, min(2 * LANES, length - i)) for i in range(0, length, 2 * LANES)]

    def convolve(w_ref, z, chunk):
        at, length = chunk
        taps = slice(z * edge, (z + 3) * edge)
        h = wide_hi[taps, at : at + length]
        l = wide_lo[taps, at : at + length]
        out = jnp.dot(w_ref[...], jnp.concatenate([h, l, h], 0), preferred_element_type=f32)
        n = w_ref.shape[0]
        if at == 0:
            sums[z, :n, :LANES] = out[:, :LANES]
            sums[z, :n, 2 * LANES : LANES + length] = out[:, LANES:]
        else:
            sums[z, :n, LANES + at : LANES + at + length] = out

    def layer(z, at, step, rows):
        strip = main = 0.0
        for b in range(3):
            k = slice(at + b * step, at + b * step + channels)
            strip = strip + strip_row(sums[z, k, :LANES], b)
            main = main + sums[z, k, (b + 1) * LANES : (b + 1 + rows) * LANES]
        return jnp.concatenate([strip, main], 1)

    def gate(cand, up, hidden):
        fresh = 1.0 / (1.0 + jnp.exp(-up))
        return hidden + fresh * (jnp.tanh(cand) - hidden)

    lines[:, :, :LANES] = jnp.zeros((6, deep, LANES), bf16)
    sums[:, :, LANES : 2 * LANES] = jnp.zeros((deep, sums.shape[1], LANES), f32)
    zeros = jnp.zeros((edge, wide_hi.shape[1]), bf16)
    for wide in (wide_hi, wide_lo):
        wide[:edge, :] = zeros
        wide[(deep + 1) * edge :, :] = zeros

    strips = [jnp.zeros((deep, LANES), f32)] * 3
    for r in range(high):
        columns = strip_ref[:, r, :]
        columns = jnp.concatenate(
            [columns, jnp.zeros((deep, LANES - columns.shape[1]), f32)], 1
        )
        here = (lane >= r * pitch) & (lane < (r + 1) * pitch)
        for c in range(3):
            moved = pltpu.roll(columns, (r * pitch - c) % LANES, 1)
            strips[c] = jnp.where(here, moved, strips[c])
    noisy = jnp.concatenate([strips[1]] + [block_ref[:, r, :] for r in range(high)], 1)
    thin_columns(
        [jnp.concatenate([strips[c], split_strip(beside(noisy, c))[1]], 1) for c in range(3)],
        first_rows,
    )
    first_span, second_span, third_span = (
        (n + 1) * LANES for n in (first_rows, second_rows, third_rows)
    )
    todo = chunks(first_span)
    share = min(2 * depth, deep)
    part = share * 2 * channels

    def thin_block(b, chunk):
        at, length = chunk
        pre[b * part : (b + 1) * part, at : at + length] = jnp.dot(
            w1_ref[b * part : (b + 1) * part, :],
            thin[:, at : at + length],
            preferred_element_type=f32,
        )

    for chunk in todo:
        thin_block(0, chunk)
    waiting = []
    hidden = jnp.zeros((channels, first_span), f32)
    for z in range(deep):
        at = z * 2 * channels
        hidden = gate(
            pre[at : at + channels, :],
            pre[at + channels : at + 2 * channels, :] + bias1,
            hidden,
        )
        wide_columns(z + 1, clean(hidden))
        if z // share + 1 < deep // share:
            for chunk in todo[z % share :: share]:
                thin_block(z // share + 1, chunk)
        if 0 < z <= AHEAD:
            waiting += [(z - 1, chunk) for chunk in todo]
        for _ in range(min(PACE, len(waiting))):
            convolve(w2_ref, *waiting.pop(0))

    later = waiting + [(z, chunk) for z in range(deep - 1, AHEAD - 1, -1) for chunk in todo]
    for _ in range(min(2 * len(todo), len(later))):
        convolve(w2_ref, *later.pop(0))
    hidden = jnp.zeros((channels, second_span), f32)
    for z in range(deep - 1, -1, -1):
        for _ in range(min(len(todo), len(later))):
            convolve(w2_ref, *later.pop(0))
        hidden = gate(
            layer(z, 0, 2 * channels, second_rows),
            layer(z, channels, 2 * channels, second_rows) + bias2,
            hidden,
        )
        scaled = hidden * head
        while scaled.shape[0] > SUBLANES:
            half = scaled.shape[0] // 2
            scaled = scaled[:half] + scaled[half:]
        partial[z * SUBLANES : (z + 1) * SUBLANES, :] = scaled

    shape = (deep, deep * SUBLANES)
    row, column = (lax.broadcasted_iota(jnp.int32, shape, i) for i in range(2))
    own = (column >= row * SUBLANES) & (column < (row + 1) * SUBLANES)
    adder = jnp.where(own, 1.0, 0.0).astype(bf16)
    change = sum(
        jnp.dot(adder, half, preferred_element_type=f32) for half in split(partial[...])
    )
    finished = noisy[:, :second_span] + change
    thin_columns([beside(finished, c) for c in range(3)], third_rows)

    def grow(chunk):
        at, length = chunk
        return jnp.dot(w3_ref[...], thin[:, at : at + length], preferred_element_type=f32)

    def spread(chunk, grown):
        for i in range(depth + 2):
            z = place * depth + i - 1
            real = jnp.where((z >= 0) & (z < deep), 1.0, 0.0)
            features = jnp.maximum(grown[i * channels : (i + 1) * channels] + bias3, 0.0)
            features = features * real
            wide_columns(i, features if chunk[0] else clean(features), chunk[0])

    todo = chunks(third_span)
    grown = {}
    for k in range(len(todo) + 2):
        if k < len(todo):
            grown[k] = grow(todo[k])
        if 0 <= k - 1 < len(todo):
            spread(todo[k - 1], grown[k - 1])
        if k >= 2:
            for z in range(depth):
                convolve(w4_ref, z, todo[k - 2])

    right = lax.axis_index("gx") == 0
    beyond = lane - jnp.where(right, width - HALO, 0)
    border = (beyond >= 0) & (beyond < HALO)

    def mended(strip, main, r):
        at = r * pitch + HALO - 1
        shift = jnp.where(right, (width - HALO - at) % LANES, (LANES - at) % LANES)
        return jnp.where(border, pltpu.roll(strip, shift, 1), main)

    def at_row(r):
        return jnp.where(turned, height - 1 - r, r)

    mine = finished[:depth]
    for b in range(1, deep // depth):
        mine = jnp.where(place == b, finished[b * depth : (b + 1) * depth], mine)
    mine = jnp.concatenate([mine, jnp.zeros((SUBLANES - depth, second_span), f32)], 0)
    for r in range(height):
        at = pl.multiple_of(at_row(r) * SUBLANES, SUBLANES)
        tiles[pl.ds(at, SUBLANES), :] = mended(
            mine[:, :LANES], mine[:, (r + 1) * LANES : (r + 2) * LANES], r
        )
    for z in range(depth):
        den_ref[z] = tiles[pl.ds(z, height, stride=SUBLANES), :]
    for z in range(depth):
        total = layer(z, 0, channels, height) + bias4
        for r in range(height):
            at = pl.multiple_of((z * height + at_row(r)) * channels, channels)
            tiles[pl.ds(at, channels), :] = mended(
                total[:, :LANES], total[:, (r + 1) * LANES : (r + 2) * LANES], r
            )
    for z in range(depth):
        for o in range(channels):
            seg_ref[o, z] = tiles[pl.ds(z * height * channels + o, height, stride=channels), :]


def local_body(
    noisy,
    first_weight,
    first_bias,
    second_weight,
    second_bias,
    head_weight,
    seg_weight_in,
    seg_bias_in,
    seg_weight_out,
    seg_bias_out,
):
    depth, height, width = noisy.shape
    count = lax.axis_size("gz")
    place = lax.axis_index("gz")
    deep = count * depth
    channels = first_bias.shape[0]
    high, pitch = height + HALO, 3 * HALO - 2
    narrow = high * LANES

    f32, bf16 = jnp.float32, jnp.bfloat16
    lane = np.arange(27 * deep)
    thin_lane = np.stack(
        [lane // deep % 9, lane % deep, lane // (9 * deep)] + [lane * 0] * 5
    ).astype(np.int32)
    tap = np.arange(27)
    ahead, back = tap % 9, (2 - tap // 3 % 3) * 3 + tap % 3
    never = np.full(5, -1)
    thin_sub = np.stack(
        [
            np.concatenate([low, never, high, never])
            for low, high in ((tap // 9, tap // 9), (ahead, ahead + 9), (back, back + 9))
        ],
        1,
    ).astype(np.int32)
    lane = np.arange(27 * channels)
    b, a, c = lane // channels // 9, lane // channels // 3 % 3, lane // channels % 3
    wide_lane = np.stack(
        [a * 9 + b * 3 + c, a * 9 + (2 - b) * 3 + c] + [lane * 0] * 6
    ).astype(np.int32)
    keep = (np.arange(channels)[:, None] == lane[None] % channels).astype(np.float32)
    lane = np.arange(channels * channels)
    gather = (np.arange(channels)[:, None] == lane[None] // channels).astype(bf16)

    taps = 3 * 9 * channels
    in_vmem = pl.BlockSpec(memory_space=pltpu.VMEM)
    prepared = pl.pallas_call(
        functools.partial(prepare, (deep, depth, channels)),
        out_shape=(
            pltpu.VMEM((deep * 2 * channels, 27 * deep), bf16),
            pltpu.VMEM((3 * 2 * channels, taps), bf16),
            pltpu.VMEM(((depth + 2) * channels, 27 * deep), bf16),
            pltpu.VMEM((3 * channels, taps), bf16),
            pltpu.VMEM((channels, LANES), f32),
        ),
        in_specs=[in_vmem] * 14,
        out_specs=(in_vmem,) * 5,
        scratch_shapes=[pltpu.VMEM((3 * 2 * channels, taps), f32)],
        compiler_params=pltpu.CompilerParams(vmem_limit_bytes=16 * 1024 * 1024),
    )
    weights = (
        jnp.transpose(first_weight, (2, 1, 0)),
        first_bias.reshape(1, -1),
        jnp.transpose(second_weight, (2, 1, 0)).reshape(-1, 2 * channels),
        second_bias.reshape(1, -1),
        head_weight.reshape(1, -1),
        seg_weight_in,
        seg_bias_in.reshape(1, -1),
        seg_weight_out.reshape(-1, 27),
        seg_bias_out.reshape(1, -1),
    )
    tables = tuple(jnp.asarray(v) for v in (thin_lane, thin_sub, wide_lane, keep, gather))

    given = [pltpu.with_memory_space_constraint(v, pltpu.HBM) for v in weights + tables]
    block, strip, laid_out = gathered(noisy, prepared(*given))
    operands = [
        pltpu.with_memory_space_constraint(v, pltpu.VMEM)
        for v in (block, strip, *laid_out)
    ]
    return pl.pallas_call(
        functools.partial(kernel, (deep, depth, channels, pitch, high)),
        out_shape=(
            jax.ShapeDtypeStruct((depth, height, width), f32),
            jax.ShapeDtypeStruct((channels, depth, height, width), f32),
        ),
        in_specs=[in_vmem] * 7,
        out_specs=(in_vmem,) * 2,
        scratch_shapes=[
            pltpu.VMEM((6, deep, (high + 1) * LANES), bf16),
            pltpu.VMEM((27 * deep, narrow), bf16),
            pltpu.VMEM((deep * 2 * channels, narrow), f32),
            pltpu.VMEM((deep * SUBLANES, narrow - LANES), f32),
            pltpu.VMEM(((deep + 2) * 3 * channels, narrow), bf16),
            pltpu.VMEM(((deep + 2) * 3 * channels, narrow), bf16),
            pltpu.VMEM((deep, 3 * 2 * channels, narrow + LANES), f32),
            pltpu.VMEM((depth * height * channels, width), f32),
        ],
        compiler_params=pltpu.CompilerParams(vmem_limit_bytes=36 * 1024 * 1024),
    )(*operands)


def solution(mesh):
    in_specs = (P(("win", "gz"), "gy", "gx"), P(), P(), P(), P(), P(), P(), P(), P(), P())
    out_specs = (P(("win", "gz"), "gy", "gx"), P(None, ("win", "gz"), "gy", "gx"))
    shallow = mesh.shape["gz"] in (1, 2, 4) and mesh.shape["gy"] == 2 and mesh.shape["gx"] == 2
    chosen = local_body if shallow else body
    return jax.shard_map(chosen, mesh=mesh, in_specs=in_specs, out_specs=out_specs, check_vma=False)
```

```python
import functools

import jax
import jax.numpy as jnp
import numpy as np
from jax import lax
from jax.experimental import pallas as pl
from jax.experimental.pallas import tpu as pltpu
from jax.sharding import PartitionSpec as P


def shifted(value, axis, steps):
    count = lax.axis_size(axis)
    first, last = (max(0, -steps), min(count, count - steps))
    return lax.ppermute(value, axis, [(source, source + steps) for source in range(first, last)])


def with_halo(block, sides, width):
    for axis, dim in sides:
        count = lax.axis_size(axis)
        forward = [(i, i + 1) for i in range(count - 1)]
        backward = [(target, source) for source, target in forward]
        low = lax.ppermute(
            lax.slice_in_dim(block, block.shape[dim] - width, None, axis=dim), axis, forward
        )
        high = lax.ppermute(lax.slice_in_dim(block, 0, width, axis=dim), axis, backward)
        block = jnp.concatenate([low, block, high], axis=dim)
    return block


def convolve(padded, weight):
    depth = padded.shape[1] - 2
    height = padded.shape[2] - 2
    width = padded.shape[3] - 2
    total = jnp.zeros((weight.shape[0], depth, height, width), jnp.float32)
    for tap in range(27):
        step_z = tap // 9
        step_y = tap // 3 % 3
        step_x = tap % 3
        piece = padded[
            :, step_z : step_z + depth, step_y : step_y + height, step_x : step_x + width
        ]
        total = total + jnp.einsum(
            "oc,czyx->ozyx", weight[:, :, tap], piece, precision=lax.Precision.HIGHEST
        )
    return total


def affine(earlier, later):
    return (earlier[0] * later[0], later[0] * earlier[1] + later[1])


def recurrent(padded, weight, bias, backward):
    channels = bias.shape[0]
    pre = convolve(padded, weight)
    cand = jnp.tanh(pre[:channels])
    keep = jax.nn.sigmoid(-(pre[channels:] + bias[:, None, None, None]))
    inject = (1.0 - keep) * cand
    if backward:
        keep = jnp.flip(keep, 1)
        inject = jnp.flip(inject, 1)
    cum_keep, cum_inject = lax.associative_scan(affine, (keep, inject), axis=1)
    total_keep = cum_keep[:, -1]
    total_inject = cum_inject[:, -1]
    offset = -1 if backward else 1

    def relay(turn, carry):
        return shifted(total_keep * carry + total_inject, "gz", offset)

    carry = lax.fori_loop(0, lax.axis_size("gz") - 1, relay, jnp.zeros_like(total_inject))
    hidden = cum_keep * carry[:, None] + cum_inject
    if backward:
        hidden = jnp.flip(hidden, 1)
    return hidden


def inside_mask(length, where, count):
    places = jnp.arange(length + 2)
    outside = (places == 0) & (where == 0) | (places == length + 1) & (where == count - 1)
    return jnp.where(outside, 0.0, 1.0).astype(jnp.float32)


def body(
    noisy,
    first_weight,
    first_bias,
    second_weight,
    second_bias,
    head_weight,
    seg_weight_in,
    seg_bias_in,
    seg_weight_out,
    seg_bias_out,
):
    noisy_pad = with_halo(noisy[None], (("gz", 1), ("gy", 2), ("gx", 3)), 1)
    first_hidden = recurrent(noisy_pad, first_weight, first_bias, False)
    hidden_pad = with_halo(first_hidden, (("gz", 1), ("gy", 2), ("gx", 3)), 1)
    second_hidden = recurrent(hidden_pad, second_weight, second_bias, True)
    denoised = noisy + jnp.einsum(
        "c,czyx->zyx", head_weight, second_hidden, precision=lax.Precision.HIGHEST
    )
    deep_pad = with_halo(denoised[None], (("gz", 1), ("gy", 2), ("gx", 3)), 2)
    grown = jnp.maximum(convolve(deep_pad, seg_weight_in) + seg_bias_in[:, None, None, None], 0.0)
    mask_z = inside_mask(denoised.shape[0], lax.axis_index("gz"), lax.axis_size("gz"))
    mask_y = inside_mask(denoised.shape[1], lax.axis_index("gy"), lax.axis_size("gy"))
    mask_x = inside_mask(denoised.shape[2], lax.axis_index("gx"), lax.axis_size("gx"))
    feature_pad = (
        grown * (mask_z[:, None, None] * mask_y[None, :, None] * mask_x[None, None, :])[None]
    )
    segmented = convolve(feature_pad, seg_weight_out) + seg_bias_out[:, None, None, None]
    return (denoised, segmented)


HALO = 4
AHEAD, PACE = 8, 4
LANES, SUBLANES = 128, 8


def split(value):
    high = value.astype(jnp.bfloat16)
    return high, (value - high.astype(jnp.float32)).astype(jnp.bfloat16)


def swapped(value, axis):
    return lax.ppermute(value, axis, [(0, 1), (1, 0)])


def gathered(noisy, laid_out):
    count = lax.axis_size("gz")
    block = noisy
    step = 1
    while step < count:
        pairs = [(i, i ^ step) for i in range(count)]
        other = lax.ppermute(block, "gz", pairs)
        low = lax.axis_index("gz") // step % 2 == 0
        block = jnp.where(
            low, jnp.concatenate([block, other], 0), jnp.concatenate([other, block], 0)
        )
        if step == 1:
            block, laid_out = lax.optimization_barrier((block, laid_out))
        step *= 2
    block = jnp.where(lax.axis_index("gy") == 0, block, jnp.flip(block, 1))
    near = lax.slice_in_dim(block, block.shape[1] - HALO, None, axis=1)
    block = jnp.concatenate([block, swapped(jnp.flip(near, 1), "gy")], 1)
    first = lax.axis_index("gx") == 0
    size = block.shape[2]
    low = lax.slice_in_dim(block, 0, HALO, axis=2)
    high = lax.slice_in_dim(block, size - HALO, size, axis=2)
    other = swapped(jnp.where(first, high, low), "gx")
    strip = jnp.where(
        first,
        jnp.concatenate([block[:, :, -2 * HALO :], other], 2),
        jnp.concatenate([other, block[:, :, : 2 * HALO]], 2),
    )
    return block, strip, laid_out


def prepare(
    geometry,
    w1_ref,
    b1_ref,
    w2_ref,
    b2_ref,
    head_ref,
    w3_ref,
    b3_ref,
    w4_ref,
    b4_ref,
    thin_lane_ref,
    thin_sub_ref,
    wide_lane_ref,
    keep_ref,
    gather_ref,
    w1_out,
    w2_out,
    w3_out,
    w4_out,
    columns_out,
    band,
):
    deep, depth, channels = geometry
    f32, bf16 = jnp.float32, jnp.bfloat16
    place = lax.axis_index("gz") * depth
    turned = lax.axis_index("gy") == 1

    def dot(left, right):
        return jnp.dot(left, right, preferred_element_type=f32)

    tap_lane, z_lane, part_lane = (thin_lane_ref[i : i + 1, :] for i in range(3))
    a_sub, tap_ahead, tap_turned = (thin_sub_ref[:, i : i + 1] for i in range(3))
    same = tap_lane + 9 * (part_lane & 1) == jnp.where(turned, tap_turned, tap_ahead)
    reach = jnp.where(same, z_lane - a_sub + 1, -2 * deep)

    def paired(weight):
        blank = jnp.zeros((weight.shape[0], thin_sub_ref.shape[0] // 2 - weight.shape[1]), f32)
        high, low = (half.astype(f32) for half in split(weight))
        return jnp.concatenate([high, blank, low, blank], 1).astype(bf16)

    def thin_rows(pair, z):
        return dot(pair, jnp.where(reach == z, 1.0, 0.0).astype(bf16)).astype(bf16)

    first = paired(w1_ref[:, 0, :].T)
    out = 2 * channels
    for z in range(deep):
        w1_out[z * out : (z + 1) * out, :] = thin_rows(first, z)
    grow = paired(w3_ref[:, 0, :])
    for i in range(depth + 2):
        z = place + i - 1
        inside = (z >= 0) & (z < deep)
        w3_out[i * channels : (i + 1) * channels, :] = thin_rows(
            grow, jnp.where(inside, z, -deep)
        )

    step = 3 * channels

    def lay(pieces, w_out):
        out = pieces[0][0].shape[0]
        for b in range(3):
            for i, half in enumerate((0, 0, 1)):
                band[b * out : (b + 1) * out, pl.ds(i * 3 * step, 3 * step)] = pieces[b][half]
        w_out[...] = band[: w_out.shape[0], :].astype(bf16)

    tall = w2_ref[...]
    pieces = []
    for b in range(3):
        ahead, back = (
            jnp.concatenate([tall[(a * 3 + k) * step : (a * 3 + k + 1) * step] for a in range(3)], 0)
            for k in (b, 2 - b)
        )
        pieces.append(tuple(h.astype(f32) for h in split(jnp.where(turned, back, ahead).T)))
    lay(pieces, w2_out)

    taps = lax.broadcasted_iota(jnp.int32, (27, wide_lane_ref.shape[1]), 0)
    spread = taps == jnp.where(turned, wide_lane_ref[1:2, :], wide_lane_ref[0:1, :])
    spread = jnp.where(spread, 1.0, 0.0).astype(bf16)
    keep = jnp.concatenate([keep_ref[...]] * channels, 0)
    both = dot(jnp.concatenate(split(w4_ref[...]), 0), spread)
    flats = [
        dot(gather_ref[...], (half * keep).astype(bf16)) for half in jnp.split(both, 2, 0)
    ]
    lay([[f[:, b * 3 * step : (b + 1) * 3 * step] for f in flats] for b in range(3)], w4_out)

    at_row = lax.broadcasted_iota(jnp.int32, (channels, channels), 0)
    at_lane = lax.broadcasted_iota(jnp.int32, (channels, channels), 1)
    for i, ref in enumerate((b1_ref, b2_ref, head_ref, b3_ref, b4_ref)):
        columns_out[:, i : i + 1] = jnp.sum(
            jnp.where(at_row == at_lane, ref[...], 0.0), axis=1, keepdims=True
        )


def kernel(
    geometry,
    block_ref,
    strip_ref,
    w1_ref,
    w2_ref,
    w3_ref,
    w4_ref,
    columns_ref,
    den_ref,
    seg_ref,
    lines,
    thin,
    pre,
    partial,
    wide_hi,
    wide_lo,
    sums,
    tiles,
):
    deep, depth, channels, pitch, high = geometry
    f32, bf16 = jnp.float32, jnp.bfloat16
    height, width = den_ref.shape[1:]
    place = lax.axis_index("gz")
    turned = lax.axis_index("gy") == 1
    bias1, bias2, head, bias3, bias4 = (columns_ref[:, i : i + 1] for i in range(5))
    lane = lax.broadcasted_iota(jnp.int32, (1, LANES), 1)
    first_rows, second_rows, third_rows = high - 1, high - 2, high - 3
    edge = 3 * channels

    def split_strip(field):
        return field[:, :LANES], field[:, LANES:]

    def clean(field):
        strip, main = split_strip(field)
        return jnp.concatenate([jnp.where(lane < first_rows * pitch, strip, 0.0), main], 1)

    def beside(field, c, first=0):
        if c == 1:
            return field
        shift, end = (1, 0) if c == 0 else (LANES - 1, LANES - 1)
        out = []
        for at in range(0, field.shape[1], LANES):
            moved = pltpu.roll(field[:, at : at + LANES], shift, 1)
            out.append(jnp.where(lane == end, 0.0, moved) if first + at > 0 else moved)
        return jnp.concatenate(out, 1)

    def strip_row(strip, b):
        if b == 1:
            return strip
        moved = pltpu.roll(strip, pitch if b == 0 else LANES - pitch, 1)
        return jnp.where(lane < pitch, 0.0, moved) if b == 0 else moved

    def thin_columns(fields, rows):
        for c, field in enumerate(fields):
            strip, main = split_strip(field)
            for i, half in enumerate(split(main)):
                lines[3 * i + c, :, pl.ds(LANES, main.shape[1])] = half
            for b in range(3):
                t = 3 * b + c
                halves = split(strip_row(strip, b))
                for k, i in enumerate((0, 0, 1)):
                    at = slice((k * 9 + t) * deep, (k * 9 + t + 1) * deep)
                    thin[at, :LANES] = halves[i]
                    thin[at, LANES : (rows + 1) * LANES] = lines[
                        3 * i + c, :, b * LANES : (b + rows) * LANES
                    ]

    def wide_columns(z, field, first=0):
        lanes = slice(first, first + field.shape[1])
        for c in range(3):
            at = (z * 3 + c) * channels
            h, l = split(beside(field, c, first))
            wide_hi[at : at + channels, lanes] = h
            wide_lo[at : at + channels, lanes] = l

    def chunks(length):
        return [(i, min(4 * LANES, length - i)) for i in range(0, length, 4 * LANES)]

    def convolve(w_ref, z, chunk):
        at, length = chunk
        taps = slice(z * edge, (z + 3) * edge)
        h = wide_hi[taps, at : at + length]
        l = wide_lo[taps, at : at + length]
        out = jnp.dot(w_ref[...], jnp.concatenate([h, l, h], 0), preferred_element_type=f32)
        n = w_ref.shape[0]
        if at == 0:
            sums[z, :n, :LANES] = out[:, :LANES]
            sums[z, :n, 2 * LANES : LANES + length] = out[:, LANES:]
        else:
            sums[z, :n, LANES + at : LANES + at + length] = out

    def layer(z, at, step, rows):
        strip = main = 0.0
        for b in range(3):
            k = slice(at + b * step, at + b * step + channels)
            strip = strip + strip_row(sums[z, k, :LANES], b)
            main = main + sums[z, k, (b + 1) * LANES : (b + 1 + rows) * LANES]
        return jnp.concatenate([strip, main], 1)

    def gate(cand, up, hidden):
        fresh = 1.0 / (1.0 + jnp.exp(-up))
        return hidden + fresh * (jnp.tanh(cand) - hidden)

    lines[:, :, :LANES] = jnp.zeros((6, deep, LANES), bf16)
    sums[:, :, LANES : 2 * LANES] = jnp.zeros((deep, sums.shape[1], LANES), f32)
    zeros = jnp.zeros((edge, wide_hi.shape[1]), bf16)
    for wide in (wide_hi, wide_lo):
        wide[:edge, :] = zeros
        wide[(deep + 1) * edge :, :] = zeros

    strips = [jnp.zeros((deep, LANES), f32)] * 3
    for r in range(high):
        columns = strip_ref[:, r, :]
        columns = jnp.concatenate(
            [columns, jnp.zeros((deep, LANES - columns.shape[1]), f32)], 1
        )
        here = (lane >= r * pitch) & (lane < (r + 1) * pitch)
        for c in range(3):
            moved = pltpu.roll(columns, (r * pitch - c) % LANES, 1)
            strips[c] = jnp.where(here, moved, strips[c])
    noisy = jnp.concatenate([strips[1]] + [block_ref[:, r, :] for r in range(high)], 1)
    thin_columns(
        [jnp.concatenate([strips[c], split_strip(beside(noisy, c))[1]], 1) for c in range(3)],
        first_rows,
    )
    first_span, second_span, third_span = (
        (n + 1) * LANES for n in (first_rows, second_rows, third_rows)
    )
    todo = chunks(first_span)
    share = min(2 * depth, deep)
    part = share * 2 * channels

    def thin_block(b, chunk):
        at, length = chunk
        pre[b * part : (b + 1) * part, at : at + length] = jnp.dot(
            w1_ref[b * part : (b + 1) * part, :],
            thin[:, at : at + length],
            preferred_element_type=f32,
        )

    for chunk in todo:
        thin_block(0, chunk)
    waiting = []
    hidden = jnp.zeros((channels, first_span), f32)
    for z in range(deep):
        at = z * 2 * channels
        hidden = gate(
            pre[at : at + channels, :],
            pre[at + channels : at + 2 * channels, :] + bias1,
            hidden,
        )
        wide_columns(z + 1, clean(hidden))
        if z // share + 1 < deep // share:
            for chunk in todo[z % share :: share]:
                thin_block(z // share + 1, chunk)
        if 0 < z <= AHEAD:
            waiting += [(z - 1, chunk) for chunk in todo]
        for _ in range(min(PACE, len(waiting))):
            convolve(w2_ref, *waiting.pop(0))

    later = waiting + [(z, chunk) for z in range(deep - 1, AHEAD - 1, -1) for chunk in todo]
    for _ in range(min(2 * len(todo), len(later))):
        convolve(w2_ref, *later.pop(0))
    hidden = jnp.zeros((channels, second_span), f32)
    for z in range(deep - 1, -1, -1):
        for _ in range(min(len(todo), len(later))):
            convolve(w2_ref, *later.pop(0))
        hidden = gate(
            layer(z, 0, 2 * channels, second_rows),
            layer(z, channels, 2 * channels, second_rows) + bias2,
            hidden,
        )
        scaled = hidden * head
        while scaled.shape[0] > SUBLANES:
            half = scaled.shape[0] // 2
            scaled = scaled[:half] + scaled[half:]
        partial[z * SUBLANES : (z + 1) * SUBLANES, :] = scaled

    shape = (deep, deep * SUBLANES)
    row, column = (lax.broadcasted_iota(jnp.int32, shape, i) for i in range(2))
    own = (column >= row * SUBLANES) & (column < (row + 1) * SUBLANES)
    adder = jnp.where(own, 1.0, 0.0).astype(bf16)
    change = sum(
        jnp.dot(adder, half, preferred_element_type=f32) for half in split(partial[...])
    )
    finished = noisy[:, :second_span] + change
    thin_columns([beside(finished, c) for c in range(3)], third_rows)

    def grow(chunk):
        at, length = chunk
        return jnp.dot(w3_ref[...], thin[:, at : at + length], preferred_element_type=f32)

    def spread(chunk, grown):
        for i in range(depth + 2):
            z = place * depth + i - 1
            real = jnp.where((z >= 0) & (z < deep), 1.0, 0.0)
            features = jnp.maximum(grown[i * channels : (i + 1) * channels] + bias3, 0.0)
            features = features * real
            wide_columns(i, features if chunk[0] else clean(features), chunk[0])

    todo = chunks(third_span)
    grown = {}
    for k in range(len(todo) + 2):
        if k < len(todo):
            grown[k] = grow(todo[k])
        if 0 <= k - 1 < len(todo):
            spread(todo[k - 1], grown[k - 1])
        if k >= 2:
            for z in range(depth):
                convolve(w4_ref, z, todo[k - 2])

    right = lax.axis_index("gx") == 0
    beyond = lane - jnp.where(right, width - HALO, 0)
    border = (beyond >= 0) & (beyond < HALO)

    def mended(strip, main, r):
        at = r * pitch + HALO - 1
        shift = jnp.where(right, (width - HALO - at) % LANES, (LANES - at) % LANES)
        return jnp.where(border, pltpu.roll(strip, shift, 1), main)

    def at_row(r):
        return jnp.where(turned, height - 1 - r, r)

    mine = finished[:depth]
    for b in range(1, deep // depth):
        mine = jnp.where(place == b, finished[b * depth : (b + 1) * depth], mine)
    mine = jnp.concatenate([mine, jnp.zeros((SUBLANES - depth, second_span), f32)], 0)
    for r in range(height):
        at = pl.multiple_of(at_row(r) * SUBLANES, SUBLANES)
        tiles[pl.ds(at, SUBLANES), :] = mended(
            mine[:, :LANES], mine[:, (r + 1) * LANES : (r + 2) * LANES], r
        )
    for z in range(depth):
        den_ref[z] = tiles[pl.ds(z, height, stride=SUBLANES), :]
    for z in range(depth):
        total = layer(z, 0, channels, height) + bias4
        for r in range(height):
            at = pl.multiple_of((z * height + at_row(r)) * channels, channels)
            tiles[pl.ds(at, channels), :] = mended(
                total[:, :LANES], total[:, (r + 1) * LANES : (r + 2) * LANES], r
            )
    for z in range(depth):
        for o in range(channels):
            seg_ref[o, z] = tiles[pl.ds(z * height * channels + o, height, stride=channels), :]


def local_body(
    noisy,
    first_weight,
    first_bias,
    second_weight,
    second_bias,
    head_weight,
    seg_weight_in,
    seg_bias_in,
    seg_weight_out,
    seg_bias_out,
):
    depth, height, width = noisy.shape
    count = lax.axis_size("gz")
    place = lax.axis_index("gz")
    deep = count * depth
    channels = first_bias.shape[0]
    high, pitch = height + HALO, 3 * HALO - 2
    narrow = high * LANES

    f32, bf16 = jnp.float32, jnp.bfloat16
    lane = np.arange(27 * deep)
    thin_lane = np.stack(
        [lane // deep % 9, lane % deep, lane // (9 * deep)] + [lane * 0] * 5
    ).astype(np.int32)
    tap = np.arange(27)
    ahead, back = tap % 9, (2 - tap // 3 % 3) * 3 + tap % 3
    never = np.full(5, -1)
    thin_sub = np.stack(
        [
            np.concatenate([low, never, high, never])
            for low, high in ((tap // 9, tap // 9), (ahead, ahead + 9), (back, back + 9))
        ],
        1,
    ).astype(np.int32)
    lane = np.arange(27 * channels)
    b, a, c = lane // channels // 9, lane // channels // 3 % 3, lane // channels % 3
    wide_lane = np.stack(
        [a * 9 + b * 3 + c, a * 9 + (2 - b) * 3 + c] + [lane * 0] * 6
    ).astype(np.int32)
    keep = (np.arange(channels)[:, None] == lane[None] % channels).astype(np.float32)
    lane = np.arange(channels * channels)
    gather = (np.arange(channels)[:, None] == lane[None] // channels).astype(bf16)

    taps = 3 * 9 * channels
    in_vmem = pl.BlockSpec(memory_space=pltpu.VMEM)
    prepared = pl.pallas_call(
        functools.partial(prepare, (deep, depth, channels)),
        out_shape=(
            pltpu.VMEM((deep * 2 * channels, 27 * deep), bf16),
            pltpu.VMEM((3 * 2 * channels, taps), bf16),
            pltpu.VMEM(((depth + 2) * channels, 27 * deep), bf16),
            pltpu.VMEM((3 * channels, taps), bf16),
            pltpu.VMEM((channels, LANES), f32),
        ),
        in_specs=[in_vmem] * 14,
        out_specs=(in_vmem,) * 5,
        scratch_shapes=[pltpu.VMEM((3 * 2 * channels, taps), f32)],
        compiler_params=pltpu.CompilerParams(vmem_limit_bytes=16 * 1024 * 1024),
    )
    weights = (
        jnp.transpose(first_weight, (2, 1, 0)),
        first_bias.reshape(1, -1),
        jnp.transpose(second_weight, (2, 1, 0)).reshape(-1, 2 * channels),
        second_bias.reshape(1, -1),
        head_weight.reshape(1, -1),
        seg_weight_in,
        seg_bias_in.reshape(1, -1),
        seg_weight_out.reshape(-1, 27),
        seg_bias_out.reshape(1, -1),
    )
    tables = tuple(jnp.asarray(v) for v in (thin_lane, thin_sub, wide_lane, keep, gather))

    given = [pltpu.with_memory_space_constraint(v, pltpu.HBM) for v in weights + tables]
    block, strip, laid_out = gathered(noisy, prepared(*given))
    operands = [
        pltpu.with_memory_space_constraint(v, pltpu.VMEM)
        for v in (block, strip, *laid_out)
    ]
    return pl.pallas_call(
        functools.partial(kernel, (deep, depth, channels, pitch, high)),
        out_shape=(
            jax.ShapeDtypeStruct((depth, height, width), f32),
            jax.ShapeDtypeStruct((channels, depth, height, width), f32),
        ),
        in_specs=[in_vmem] * 7,
        out_specs=(in_vmem,) * 2,
        scratch_shapes=[
            pltpu.VMEM((6, deep, (high + 1) * LANES), bf16),
            pltpu.VMEM((27 * deep, narrow), bf16),
            pltpu.VMEM((deep * 2 * channels, narrow), f32),
            pltpu.VMEM((deep * SUBLANES, narrow - LANES), f32),
            pltpu.VMEM(((deep + 2) * 3 * channels, narrow), bf16),
            pltpu.VMEM(((deep + 2) * 3 * channels, narrow), bf16),
            pltpu.VMEM((deep, 3 * 2 * channels, narrow + LANES), f32),
            pltpu.VMEM((depth * height * channels, width), f32),
        ],
        compiler_params=pltpu.CompilerParams(vmem_limit_bytes=36 * 1024 * 1024),
    )(*operands)


def solution(mesh):
    in_specs = (P(("win", "gz"), "gy", "gx"), P(), P(), P(), P(), P(), P(), P(), P(), P())
    out_specs = (P(("win", "gz"), "gy", "gx"), P(None, ("win", "gz"), "gy", "gx"))
    shallow = mesh.shape["gz"] in (1, 2, 4) and mesh.shape["gy"] == 2 and mesh.shape["gx"] == 2
    chosen = local_body if shallow else body
    return jax.shard_map(chosen, mesh=mesh, in_specs=in_specs, out_specs=out_specs, check_vma=False)
```
